32 devices in a mesh: dp: 8 (over z, x), tensor: 4 (over y, core).
Axes of the slice: x: 2, y: 2, z: 4, core: 2. Of those that a mesh axis runs over, the one named last changes fastest.
Arguments:
- tokens: bfloat16 [8192, 2048], P(('dp', 'tensor')), may hold values from -6 to 6
- gain_attn: float32 [2048], replicated, may hold values from 0.5 to 1.5
- gain_mlp: float32 [2048], replicated, may hold values from 0.5 to 1.5
- w_query: bfloat16 [2048, 256], P(None, 'tensor'), may hold values from -0.125 to 0.125
- w_key: bfloat16 [2048, 256], P(None, 'tensor'), may hold values from -0.125 to 0.125
- w_value: bfloat16 [2048, 2048], P(None, 'tensor'), may hold values from -0.125 to 0.125
- w_out: bfloat16 [2048, 2048], P('tensor'), may hold values from -1.5 to 1.5
- w_gate: bfloat16 [2048, 5504], P(None, 'tensor'), may hold values from -0.125 to 0.125
- w_up: bfloat16 [2048, 5504], P(None, 'tensor'), may hold values from -0.125 to 0.125
- w_down: bfloat16 [5504, 2048], P('tensor'), may hold values from -0.078125 to 0.078125
- cotangent: bfloat16 [8192, 2048], P(('dp', 'tensor')), may hold values from -6 to 6
- lengths: int32 [8], replicated, may hold values from 256 to 1024, as said below
Outputs:
- output: bfloat16 [8192, 2048], P(('dp', 'tensor'))
- input_grad: float32 [8192, 2048], P(('dp', 'tensor'))
- gain_attn_grad: float32 [2048], replicated
- gain_mlp_grad: float32 [2048], replicated
- query_grad: float32 [2048, 256], P('dp', 'tensor')
- key_grad: float32 [2048, 256], P('dp', 'tensor')
- value_grad: float32 [2048, 2048], P('dp', 'tensor')
- out_grad: float32 [2048, 2048], P('tensor', 'dp')
- gate_grad: float32 [2048, 5504], P('dp', 'tensor')
- up_grad: float32 [2048, 5504], P('dp', 'tensor')
- down_grad: float32 [5504, 2048], P('tensor', 'dp')
- den_mean: float32 [], replicated
The draws below stay inside these ranges and needn't reach their ends.
Inputs may be any that keep to these rules, and one draw needn't show every extreme that they name: `lengths`: some sequence has length exactly 1024 and some other exactly 256.
All inputs are finite; a program needn't handle non-finite values.
Results may differ from the reference program's by a relative error of at most 0.018.
Values may be sent and summed in bfloat16 or wider, within the bound.
A program may use at most 192 MiB of HBM per device.

```python
import math
import jax
import jax.numpy as jnp
from jax import lax

D = 2048
HEADS = 16
FEAT = 16
HV = 128
FF = 5504
BUCKET = 1024
TOKENS = 8192
N_DP = 8


def draw_lengths(key, part):
    key = jax.random.fold_in(key, 7)
    key_base, key_order = jax.random.split(key)
    base_lengths = jax.random.randint(key_base, (N_DP,), BUCKET // 4, BUCKET + 1)
    order_idx = jax.random.permutation(key_order, N_DP)
    base_lengths = base_lengths.at[order_idx[0]].set(BUCKET)
    base_lengths = base_lengths.at[order_idx[1]].set(BUCKET // 4)
    return base_lengths.astype(jnp.int32)


def steps_of(own_key, dims, cuts, smallest, largest):
    loudness = 1.0
    for dim, parts in cuts:
        heights = jax.random.uniform(jax.random.fold_in(jax.random.fold_in(own_key, 6), dim), (parts,), jnp.float32, smallest / len(cuts), largest / len(cuts))
        loudness = loudness * jnp.repeat(jnp.exp(heights), dims[dim] // parts).reshape((-1,) + (1,) * (len(dims) - 1 - dim))
    return loudness


def noise(own_key, extent, spread, limit, shards=(), held_as=jnp.bfloat16):
    values = spread * jax.random.normal(own_key, extent, jnp.float32)
    if shards:
        values = values * steps_of(own_key, extent, shards, -0.22, 0.18)
    return jnp.clip(values, -limit, limit).astype(held_as)


def setup_inputs(seed: int = 0) -> dict:
    seeds = jax.random.split(jax.random.key(seed), 13)
    tokens = noise(seeds[0], (TOKENS, D), 1.0, 6.0, ((0, 32),))
    gain_attn = jnp.clip(1.0 + 0.1 * jax.random.normal(seeds[1], (D,), jnp.float32), 0.5, 1.5)
    gain_mlp = jnp.clip(1.0 + 0.1 * jax.random.normal(seeds[2], (D,), jnp.float32), 0.5, 1.5)
    w_query = noise(seeds[3], (D, HEADS * FEAT), D ** -0.5, 0.125, ((1, 4),))
    w_key = noise(seeds[4], (D, HEADS * FEAT), D ** -0.5, 0.125, ((1, 4),))
    w_value = noise(seeds[5], (D, HEADS * HV), D ** -0.5, 0.125, ((1, 4),))
    w_out = noise(seeds[6], (HEADS * HV, D), (HEADS * HV * 8 // BUCKET) ** -0.5, 1.5, ((0, 4),))
    w_gate = noise(seeds[7], (D, FF), D ** -0.5, 0.125, ((1, 4),))
    w_up = noise(seeds[8], (D, FF), D ** -0.5, 0.125, ((1, 4),))
    w_down = noise(seeds[9], (FF, D), FF ** -0.5, 0.078125, ((0, 4),))
    cotangent = noise(seeds[10], (TOKENS, D), 1.0, 6.0, ((0, 32),))
    lengths = draw_lengths(jax.random.fold_in(seeds[12], 71), 0)
    return dict(tokens=tokens, gain_attn=gain_attn, gain_mlp=gain_mlp, w_query=w_query, w_key=w_key, w_value=w_value, w_out=w_out, w_gate=w_gate, w_up=w_up, w_down=w_down, cotangent=cotangent, lengths=lengths)


@jax.custom_vjp
def low(v):
    return lax.optimization_barrier(v.astype(jnp.bfloat16)).astype(jnp.float32)

@jax.custom_vjp
def low_back(v):
    return v

def low_keep(v):
    return (low(v), None)

def low_pass(kept, grad):
    return (grad,)

def back_keep(v):
    return (v, None)

def back_low(kept, grad):
    return (low(grad),)
low.defvjp(low_keep, low_pass)
low_back.defvjp(back_keep, back_low)

def matmul(left_side, right_side):
    return jnp.dot(left_side, right_side, precision=lax.Precision.HIGHEST, preferred_element_type=jnp.float32)

def normalize(source, gain_vec):
    return source * lax.rsqrt(lax.optimization_barrier(jnp.mean(source * source, axis=-1, keepdims=True)) + 1e-06) * gain_vec

def block_forward(params, seq_tokens, length):
    gain_attn, gain_mlp, w_query, w_key, w_value, w_out, w_gate, w_up, w_down = params
    position = jnp.arange(BUCKET, dtype=jnp.int32)
    valid_rows = (position < length).astype(jnp.float32)
    causal = ((position[None, :] <= position[:, None]) & (position[None, :] < length)).astype(jnp.float32)
    qk_scale = 1.0 / math.sqrt(FEAT)
    normed = low(normalize(seq_tokens, gain_attn))
    query_rows = low_back(low(matmul(normed, w_query))).reshape(BUCKET, HEADS, FEAT).transpose(1, 0, 2)
    key_head_rows = low_back(low(matmul(normed, w_key))).reshape(BUCKET, HEADS, FEAT).transpose(1, 0, 2)
    value_heads = low_back(low(matmul(normed, w_value))).reshape(BUCKET, HEADS, HV).transpose(1, 0, 2)

    def single_head(operands):
        head_query, head_key, head_value = operands
        scores = low_back(matmul(head_query, head_key.T) * qk_scale)
        taylor = (1.0 + scores + 0.5 * scores * scores) * causal
        numerator = low_back(matmul(low(taylor), head_value))
        denominator = lax.optimization_barrier(jnp.sum(taylor, axis=-1))
        return (numerator / denominator[:, None], denominator)
    mixed_heads, denominator = lax.map(jax.checkpoint(single_head), (query_rows, key_head_rows, value_heads))
    attended = low_back(low(mixed_heads.transpose(1, 0, 2).reshape(BUCKET, HEADS * HV)))
    mid_state = seq_tokens + low_back(matmul(attended, w_out))
    normed_mlp = low(normalize(mid_state, gain_mlp))
    gate_value = low_back(matmul(normed_mlp, w_gate))
    up_value = low_back(matmul(normed_mlp, w_up))
    hidden = low(jax.nn.silu(gate_value) * up_value)
    result = valid_rows[:, None] * (mid_state + low_back(matmul(hidden, w_down)))
    den_part = jnp.sum(denominator * (valid_rows / (position + 1.0))[None, :])
    return (result, den_part)

def reference(tokens, gain_attn, gain_mlp, w_query, w_key, w_value, w_out, w_gate, w_up, w_down, cotangent, lengths):
    params = tuple((item.astype(jnp.float32) for item in (gain_attn, gain_mlp, w_query, w_key, w_value, w_out, w_gate, w_up, w_down)))
    token_blocks = tokens.astype(jnp.float32).reshape(N_DP, BUCKET, D)
    cot_blocks = cotangent.astype(jnp.float32).reshape(N_DP, BUCKET, D)

    def add_pair(first_item, second_item):
        return first_item + second_item

    def scan_step(carried, inputs):
        grad_sums, den_total = carried
        block_tokens, block_cot, length = inputs

        def forward_here(param_set, token_set):
            return block_forward(param_set, token_set, length)
        result, pullback, den_part = jax.vjp(forward_here, params, block_tokens, has_aux=True)
        grad_params, grad_tokens = pullback(block_cot)
        grad_sums = jax.tree.map(add_pair, grad_sums, grad_params)
        return ((grad_sums, den_total + den_part), (result, grad_tokens))
    zero_grads = jax.tree.map(jnp.zeros_like, params)
    (grad_sums, den_total), (results, grad_tokens) = lax.scan(scan_step, (zero_grads, jnp.zeros((), jnp.float32)), (token_blocks, cot_blocks, lengths))
    den_mean = den_total / (HEADS * jnp.sum(lengths).astype(jnp.float32))
    output = results.reshape(TOKENS, D).astype(jnp.bfloat16)
    return (output, grad_tokens.reshape(TOKENS, D), grad_sums[0], grad_sums[1], grad_sums[2], grad_sums[3], grad_sums[4], grad_sums[5], grad_sums[6], grad_sums[7], grad_sums[8], den_mean)
```

```python
import functools
import math

import jax
import jax.numpy as jnp
from jax import lax
from jax.experimental import pallas as pl
from jax.experimental.pallas import tpu as pltpu
from jax.sharding import PartitionSpec as P

FEAT = 16
MESH = pl.DeviceIdType.MESH
f32 = jnp.float32
bf16 = jnp.bfloat16


def weight_kernel(dp_size, count, x_of, *refs):
    n_x = max(x_of) + 1
    lefts, refs = refs[:n_x], refs[n_x:]
    rights, refs = refs[:count], refs[count:]
    outs, refs = refs[:count], refs[count:]
    xsend, xrecv, zsend, zrecv = (refs[i * count : (i + 1) * count] for i in range(4))
    xs_sem, xr_sem, zs_sem, zr_sem = refs[4 * count :]
    nz = dp_size // 2
    rows = outs[0].shape[0]
    dp = lax.axis_index("dp")
    tensor = lax.axis_index("tensor")
    z, x = dp // 2, lax.rem(dp, 2)
    partner = (z * 2 + 1 - x, tensor)

    def target(k):
        return lax.rem(z + 1 + k, nz)

    barrier = pltpu.get_barrier_semaphore()
    pl.semaphore_signal(barrier, inc=1, device_id=partner, device_id_type=MESH)
    for k in range(nz - 1):
        pl.semaphore_signal(barrier, inc=1, device_id=(target(k) * 2 + x, tensor), device_id_type=MESH)
    pl.semaphore_wait(barrier, nz)

    def block(i, zt, xt):
        start = pl.multiple_of((zt * 2 + xt) * rows, rows)
        if rows % 128:
            left, dims = lefts[x_of[i]][pl.ds(start, rows), :], ((1,), (0,))
        else:
            left, dims = lefts[x_of[i]][:, pl.ds(start, rows)], ((0,), (0,))
        return lax.dot_general(left, rights[i][...], (dims, ((), ())), preferred_element_type=f32)

    def xcopy(i, k):
        return pltpu.make_async_remote_copy(
            xsend[i].at[k], xrecv[i].at[k], xs_sem.at[i, k], xr_sem.at[i, k], device_id=partner, device_id_type=MESH
        )

    def zcopy(i, k):
        return pltpu.make_async_remote_copy(
            zsend[i].at[k], zrecv[i].at[k], zs_sem.at[i, k], zr_sem.at[i, k],
            device_id=(target(k) * 2 + x, tensor), device_id_type=MESH,
        )

    def cross(i):
        def body(k, carry):
            xsend[i][k] = block(i, target(k), 1 - x).astype(bf16)
            if i == 0:
                @pl.when(k < 2)
                def _():
                    xcopy(i, k).start()
            return carry
        lax.fori_loop(0, nz, body, 0)

    def more(i, k):
        if i + 1 < count:
            later = k + 2
            @pl.when(later < nz)
            def _():
                xcopy(i, later).start()
            @pl.when(later >= nz)
            def _():
                xcopy(i + 1, later - nz).start()
        else:
            @pl.when(k + 2 < nz)
            def _():
                xcopy(i, k + 2).start()

    def keep(i):
        def body(k, carry):
            own = block(i, target(k), x)
            xcopy(i, k).wait_recv()
            more(i, k)
            zsend[i][k] = (own + xrecv[i][k].astype(f32)).astype(bf16)
            zcopy(i, k).start()
            return carry
        lax.fori_loop(0, nz - 1, body, 0)
        own = block(i, z, x)
        xcopy(i, nz - 1).wait_recv()
        more(i, nz - 1)
        outs[i][...] = own + xrecv[i][nz - 1].astype(f32)

    cross(0)
    for i in range(count):
        if i + 1 < count:
            cross(i + 1)
        keep(i)
    for i in range(count):
        def add(k, carry):
            zcopy(i, k).wait_recv()
            outs[i][...] += zrecv[i][k].astype(f32)
            return carry
        lax.fori_loop(0, nz - 1, add, 0)
    for i in range(count):
        def done(k, carry):
            zcopy(i, k).wait_send()
            return carry
        lax.fori_loop(0, nz - 1, done, 0)
        def donex(k, carry):
            xcopy(i, k).wait_send()
            return carry
        lax.fori_loop(0, nz, donex, 0)


def weight_sums(lefts, rights, x_of, collective_id):
    dp_size = lax.axis_size("dp")
    nz = dp_size // 2
    count = len(rights)
    rows = lefts[0].shape[1] // dp_size
    if rows % 128:
        lefts = [left.T for left in lefts]
    buf = lambda n: [pltpu.VMEM((n, rows, r.shape[1]), bf16) for r in rights]
    vm = pl.BlockSpec(memory_space=pltpu.VMEM)
    sem = lambda n: pltpu.SemaphoreType.DMA((count, n))
    return pl.pallas_call(
        functools.partial(weight_kernel, dp_size, count, x_of),
        out_shape=[jax.ShapeDtypeStruct((rows, r.shape[1]), f32) for r in rights],
        in_specs=[vm] * (len(lefts) + count),
        out_specs=[vm] * count,
        scratch_shapes=buf(nz) + buf(nz) + buf(nz - 1) + buf(nz - 1) + [sem(nz), sem(nz), sem(nz - 1), sem(nz - 1)],
        compiler_params=pltpu.CompilerParams(
            collective_id=collective_id, has_side_effects=True, vmem_limit_bytes=60 << 20
        ),
        name="weight_sums",
    )(*lefts, *rights)


def norm_forward(source, gain_vec):
    inv_scale = lax.rsqrt(jnp.mean(source * source, axis=-1, keepdims=True) + 1e-06)
    normal = source * inv_scale
    return (normal, inv_scale, (normal * gain_vec).astype(jnp.bfloat16))


def norm_back(grad_norm, normal, inv_scale, gain_vec):
    weighted = grad_norm * gain_vec
    return inv_scale * (weighted - normal * jnp.mean(weighted * normal, axis=-1, keepdims=True))


def per_device(
    tokens,
    gain_attn,
    gain_mlp,
    w_query,
    w_key,
    w_value,
    w_out,
    w_gate,
    w_up,
    w_down,
    cotangent,
    lengths,
):
    tok_rows = tokens.shape[0]
    groups = lax.axis_size("tensor")
    bucket = tok_rows * groups
    length = lengths[lax.axis_index("dp")]
    position = jnp.arange(bucket, dtype=jnp.int32)
    valid_rows = (position < length).astype(jnp.float32)
    own_rows = lax.axis_index("tensor") * tok_rows + jnp.arange(tok_rows, dtype=jnp.int32)
    own_valid = (own_rows < length).astype(jnp.float32)[:, None]
    head_count = w_query.shape[1] // FEAT
    head_width = w_value.shape[1] // head_count
    qk_scale = 1.0 / math.sqrt(FEAT)
    block_rows = min(512, bucket)
    float_single = jnp.float32
    bf16 = jnp.bfloat16
    x_full = tokens.astype(float_single)
    normal_attn, scale_attn, normed = norm_forward(x_full, gain_attn)
    normed_all = lax.all_gather(normed, "tensor", axis=0, tiled=True)
    query_rows = (
        jnp.dot(normed_all, w_query, preferred_element_type=float_single)
        .astype(bf16)
        .reshape(bucket, head_count, FEAT)
    )
    key_head_rows = (
        jnp.dot(normed_all, w_key, preferred_element_type=float_single)
        .astype(bf16)
        .reshape(bucket, head_count, FEAT)
    )
    value_heads = (
        jnp.dot(normed_all, w_value, preferred_element_type=float_single)
        .astype(bf16)
        .reshape(bucket, head_count, head_width)
    )

    def block_scores(first_row_index, last_row_index):
        scores = (
            jnp.einsum(
                "wra,tra->rwt",
                query_rows[first_row_index:last_row_index],
                key_head_rows[:last_row_index],
                preferred_element_type=float_single,
            )
            * qk_scale
        )
        key_mask = (
            (position[None, :last_row_index] <= position[first_row_index:last_row_index, None])
            & (position[None, :last_row_index] < length)
        ).astype(float_single)
        taylor = (1.0 + scores + 0.5 * scores * scores) * key_mask
        return (scores, key_mask, taylor)

    numer_parts = []
    denom_parts = []
    for first_row_index in range(0, bucket, block_rows):
        last_row_index = first_row_index + block_rows
        scores, key_mask, taylor = block_scores(first_row_index, last_row_index)
        numer_parts.append(
            jnp.einsum(
                "hqk,khv->qhv",
                taylor.astype(bf16),
                value_heads[:last_row_index],
                preferred_element_type=float_single,
            )
        )
        denom_parts.append(jnp.sum(taylor, axis=-1).T)
    numerator = jnp.concatenate(numer_parts, axis=0)
    denominator = jnp.concatenate(denom_parts, axis=0)
    attended = (
        (numerator / denominator[:, :, None]).reshape(bucket, head_count * head_width).astype(bf16)
    )
    den_part = jnp.sum(denominator * (valid_rows / (position + 1.0))[:, None])
    den_total = lax.psum(den_part, ("dp", "tensor"))
    attn_local = lax.psum_scatter(
        jnp.dot(attended, w_out, preferred_element_type=float_single),
        "tensor",
        scatter_dimension=0,
        tiled=True,
    )
    mid_state = x_full + attn_local
    normal_mlp, scale_mlp, normed_mlp = norm_forward(mid_state, gain_mlp)
    mlp_all = lax.all_gather(normed_mlp, "tensor", axis=0, tiled=True)
    gate_value = jnp.dot(mlp_all, w_gate, preferred_element_type=float_single)
    up_value = jnp.dot(mlp_all, w_up, preferred_element_type=float_single)
    sigmoid_gate = jax.nn.sigmoid(gate_value)
    active = gate_value * sigmoid_gate
    hidden = (active * up_value).astype(bf16)
    mlp_local = lax.psum_scatter(
        jnp.dot(hidden, w_down, preferred_element_type=float_single).astype(jnp.bfloat16),
        "tensor",
        scatter_dimension=0,
        tiled=True,
    ).astype(jnp.float32)
    output = (own_valid * (mid_state + mlp_local)).astype(bf16)
    grad_out = cotangent.astype(float_single) * own_valid
    grad_mlp_all = lax.all_gather(grad_out.astype(bf16), "tensor", axis=0, tiled=True)
    grad_hidden = jnp.einsum("td,fd->tf", grad_mlp_all, w_down, preferred_element_type=float_single)
    grad_gate = (
        grad_hidden * up_value * sigmoid_gate * (1.0 + gate_value * (1.0 - sigmoid_gate))
    ).astype(bf16)
    grad_up = (grad_hidden * active).astype(bf16)
    part_gate = jnp.einsum("tf,df->td", grad_gate, w_gate, preferred_element_type=float_single)
    part_up = jnp.einsum("tf,df->td", grad_up, w_up, preferred_element_type=float_single)
    grad_normed_mlp = lax.psum_scatter(
        part_gate + part_up, "tensor", scatter_dimension=0, tiled=True
    )
    gain_mlp_part = jnp.sum(grad_normed_mlp * normal_mlp, axis=0)
    grad_state = grad_out + norm_back(grad_normed_mlp, normal_mlp, scale_mlp, gain_mlp)
    grad_attn_all = lax.all_gather(grad_state.astype(bf16), "tensor", axis=0, tiled=True)
    grad_attended = jnp.einsum(
        "td,vd->tv", grad_attn_all, w_out, preferred_element_type=float_single
    ).astype(bf16)
    grad_attended = grad_attended.reshape(bucket, head_count, head_width).astype(float_single)
    grad_numerator = (grad_attended / denominator[:, :, None]).astype(bf16)
    grad_denominator = -jnp.sum(grad_attended * numerator, axis=-1) / (denominator * denominator)
    grad_value_acc = jnp.zeros((bucket, head_count, head_width), float_single)
    grad_key_acc = jnp.zeros((bucket, head_count, FEAT), float_single)
    query_parts = []
    for first_row_index in range(0, bucket, block_rows):
        last_row_index = first_row_index + block_rows
        scores, key_mask, taylor = block_scores(first_row_index, last_row_index)
        numer_block = grad_numerator[first_row_index:last_row_index]
        grad_value_acc = grad_value_acc.at[:last_row_index].add(
            jnp.einsum(
                "hqk,qhv->khv",
                taylor.astype(bf16),
                numer_block,
                preferred_element_type=float_single,
            )
        )
        taylor_feature_gradient = jnp.einsum(
            "qhv,khv->hqk",
            numer_block,
            value_heads[:last_row_index],
            preferred_element_type=float_single,
        )
        taylor_feature_gradient = (
            taylor_feature_gradient + grad_denominator[first_row_index:last_row_index].T[:, :, None]
        )
        score_gradients = (taylor_feature_gradient * key_mask * (1.0 + scores)).astype(bf16)
        query_parts.append(
            jnp.einsum(
                "dwr,rdj->wdj",
                score_gradients,
                key_head_rows[:last_row_index],
                preferred_element_type=float_single,
            )
            * qk_scale
        )
        grad_key_acc = grad_key_acc.at[:last_row_index].add(
            jnp.einsum(
                "nor,onz->rnz",
                score_gradients,
                query_rows[first_row_index:last_row_index],
                preferred_element_type=float_single,
            )
            * qk_scale
        )
    grad_queries = (
        jnp.concatenate(query_parts, axis=0).reshape(bucket, head_count * FEAT).astype(bf16)
    )
    grad_keys = grad_key_acc.reshape(bucket, head_count * FEAT).astype(bf16)
    grad_values = grad_value_acc.reshape(bucket, head_count * head_width).astype(bf16)
    part_query = jnp.einsum("tf,df->td", grad_queries, w_query, preferred_element_type=float_single)
    part_key = jnp.einsum("tf,df->td", grad_keys, w_key, preferred_element_type=float_single)
    part_value = jnp.einsum("tf,df->td", grad_values, w_value, preferred_element_type=float_single)
    grad_normed = lax.psum_scatter(
        (part_query + part_key + part_value).astype(jnp.bfloat16),
        "tensor",
        scatter_dimension=0,
        tiled=True,
    ).astype(jnp.float32)
    gain_attn_part = jnp.sum(grad_normed * normal_attn, axis=0)
    input_grad = grad_state + norm_back(grad_normed, normal_attn, scale_attn, gain_attn)
    down_total, gate_total, up_total = weight_sums(
        (grad_mlp_all, mlp_all), (hidden, grad_gate, grad_up), (0, 1, 1), 1
    )
    qk_width = head_count * FEAT
    out_total, qkv_total = weight_sums(
        (grad_attn_all, normed_all),
        (attended, jnp.concatenate([grad_values, grad_queries, grad_keys], axis=1)),
        (0, 1),
        2,
    )
    value_width = head_count * head_width
    value_total = qkv_total[:, :value_width]
    query_total = qkv_total[:, value_width : value_width + qk_width]
    key_total = qkv_total[:, value_width + qk_width :]
    gain_attn_total, gain_mlp_total = lax.psum((gain_attn_part, gain_mlp_part), ("dp", "tensor"))
    den_mean = den_total / (head_count * groups * jnp.sum(lengths).astype(float_single))
    return (
        output,
        input_grad,
        gain_attn_total,
        gain_mlp_total,
        query_total,
        key_total,
        value_total,
        out_total.T,
        gate_total,
        up_total,
        down_total.T,
        den_mean,
    )


def solution(mesh):
    return jax.shard_map(
        per_device,
        mesh=mesh,
        in_specs=(
            P(("dp", "tensor"), None),
            P(),
            P(),
            P(None, "tensor"),
            P(None, "tensor"),
            P(None, "tensor"),
            P("tensor", None),
            P(None, "tensor"),
            P(None, "tensor"),
            P("tensor", None),
            P(("dp", "tensor"), None),
            P(),
        ),
        out_specs=(
            P(("dp", "tensor"), None),
            P(("dp", "tensor"), None),
            P(),
            P(),
            P("dp", "tensor"),
            P("dp", "tensor"),
            P("dp", "tensor"),
            P("tensor", "dp"),
            P("dp", "tensor"),
            P("dp", "tensor"),
            P("tensor", "dp"),
            P(),
        ),
        check_vma=False,
    )
```

```python
import functools
import math

import jax
import jax.numpy as jnp
from jax import lax
from jax.experimental import pallas as pl
from jax.experimental.pallas import tpu as pltpu
from jax.sharding import PartitionSpec as P

FEAT = 16
MESH = pl.DeviceIdType.MESH
f32 = jnp.float32
bf16 = jnp.bfloat16
NT = (((1,), (1,)), ((), ()))
TN = (((0,), (0,)), ((), ()))
AHEAD = 4
LAG = 2
SETTLE = 3
STRIP = 16


def dot(a, b, dims=(((1,), (0,)), ((), ()))):
    return lax.dot_general(a, b, dims, preferred_element_type=f32)


def loop(count, body):
    def step(i, carry):
        body(i)
        return carry

    lax.fori_loop(0, count, step, 0)


def pieces(width, size):
    return [(start, min(size, width - start)) for start in range(0, width, size)]


class Group:
    def __init__(self):
        self.dp = lax.axis_index("dp")
        self.t = lax.axis_index("tensor")
        self.y, self.c = self.t // 2, lax.rem(self.t, 2)
        self.sibling = (self.dp, self.y * 2 + 1 - self.c)
        self.across = (self.dp, (1 - self.y) * 2 + self.c)


def remote(src, dst, send, recv, device):
    return pltpu.make_async_remote_copy(src, dst, send, recv, device_id=device, device_id_type=MESH)


class RowSums:
    def __init__(self, g, own_rows, phase, chunk, part, bufs, sems):
        self.g, self.own, self.p, self.chunk, self.part = g, own_rows, phase, chunk, part
        self.sibsend, self.sibrecv, self.ysend, self.yrecv, self.total = bufs
        self.sib_s, self.sib_r, self.y_s, self.y_r = sems
        self.count = own_rows // chunk

    def at(self, j):
        return pl.ds(pl.multiple_of(j * self.chunk, self.chunk), self.chunk)

    def rows(self, y, c, j):
        return pl.ds(pl.multiple_of((y * 2 + c) * self.own + j * self.chunk, self.chunk), self.chunk)

    def sib(self, far, j):
        return remote(
            self.sibsend.at[far, self.at(j)], self.sibrecv.at[far, self.at(j)],
            self.sib_s.at[self.p, far, j], self.sib_r.at[self.p, far, j], self.g.sibling,
        )

    def ycopy(self, j):
        return remote(
            self.ysend.at[self.at(j)], self.yrecv.at[self.at(j)],
            self.y_s.at[self.p, j], self.y_r.at[self.p, j], self.g.across,
        )

    def give(self, far, j):
        y = 1 - self.g.y if far else self.g.y
        for n, w in pieces(self.total.shape[1], 512):
            self.sibsend[far, self.at(j), n : n + w] = self.part(self.rows(y, 1 - self.g.c, j), n, w).astype(bf16)
        self.sib(far, j).start()

    def send(self, j):
        g = self.g
        for n, w in pieces(self.total.shape[1], 512):
            self.total[self.at(j), n : n + w] = self.part(self.rows(1 - g.y, g.c, j), n, w)
        self.sib(1, j).wait_recv()
        self.ysend[self.at(j)] = (self.total[self.at(j)] + self.sibrecv[1, self.at(j)].astype(f32)).astype(bf16)
        self.ycopy(j).start()

    def hold(self, j):
        for n, w in pieces(self.total.shape[1], 512):
            self.total[self.at(j), n : n + w] = self.part(self.rows(self.g.y, self.g.c, j), n, w)

    def finish(self, j, use):
        self.sib(0, j).wait_recv()
        self.ycopy(j).wait_recv()

        def strip(i):
            r = pl.ds(pl.multiple_of(j * self.chunk + i * STRIP, STRIP), STRIP)
            use(r, self.total[r] + self.sibrecv[0, r].astype(f32) + self.yrecv[r].astype(f32))

        loop(self.chunk // STRIP, strip)

    def drain(self):
        def body(j):
            self.sib(0, j).wait_send()
            self.sib(1, j).wait_send()
            self.ycopy(j).wait_send()

        loop(self.count, body)


class Spread:
    def __init__(self, g, own_rows, chunk, src, full, sems, phase):
        self.g, self.own, self.chunk, self.src, self.full, self.p = g, own_rows, chunk, src, full, phase
        self.s, self.r = sems
        self.count = own_rows // chunk

    def rows(self, y, c, j):
        return pl.ds(pl.multiple_of((y * 2 + c) * self.own + j * self.chunk, self.chunk), self.chunk)

    def copy(self, kind, j):
        g = self.g
        rows = self.rows(g.y, g.c, j)
        if kind == 2:
            rows = self.rows(1 - g.y, g.c, j)
            src = self.full.at[rows]
        elif self.src is None:
            src = self.full.at[rows]
        else:
            src = self.src.at[pl.ds(pl.multiple_of(j * self.chunk, self.chunk), self.chunk)]
        return remote(
            src, self.full.at[rows], self.s.at[self.p, kind, j], self.r.at[self.p, kind, j],
            g.across if kind == 1 else g.sibling,
        )

    def start(self, j):
        self.copy(1, j).start()
        self.copy(0, j).start()

    def relay(self, j):
        self.copy(1, j).wait_recv()
        self.copy(2, j).start()

    def sib_in(self, j):
        self.copy(0, j).wait_recv()

    def far_in(self, j):
        self.copy(2, j).wait_recv()

    def drain(self):
        def body(j):
            for kind in range(3):
                self.copy(kind, j).wait_send()

        loop(self.count, body)


class WeightSums:
    def __init__(self, g, dp_size, rows, jobs, block, lefts_of, refs, sems, out):
        self.g, self.dp_size, self.rows, self.block = g, dp_size, rows, block
        self.nz = dp_size // 2
        self.z, self.x = g.dp // 2, lax.rem(g.dp, 2)
        self.halves = max(1, rows // 128)
        self.rn = rows // self.halves
        self.ring = self.zs_slots(self.nz)
        self.jobs = jobs * self.halves - 1
        self.steps = self.jobs * self.nz
        (self.xs, self.zs, self.zf, self.zfx, self.acc, self.facc, self.xtmp, self.ztmp,
         self.xrecv, self.zrecv, self.frecv, self.fxrecv) = refs
        (self.xs_s, self.xr_s, self.zs_s, self.zr_s, self.zf_s, self.zf_r, self.fx_s, self.fx_r, self.loc) = sems
        self.out = out
        self.partner = (self.z * 2 + 1 - self.x, g.t)

    @staticmethod
    def zs_slots(nz):
        return 2 * nz if nz <= 4 else nz

    def job(self, s):
        lin = s // self.nz + 1
        return lin // self.halves, lax.rem(lin, self.halves)

    def order(self, k):
        last = self.nz - 1
        upper = self.z >= self.nz // 2
        z = jnp.where(upper, last - self.z, self.z)
        zt = jnp.where(k < last - z, last - k, jnp.where(k < last, last - 1 - k, z))
        return jnp.where(upper, last - zt, zt)

    def coming(self, zt):
        return jnp.where(zt > self.z, self.z > 0, self.z < self.nz - 1)

    def towards(self, zt):
        return (jnp.where(zt > self.z, self.z + 1, self.z - 1) * 2 + self.x, self.g.t)

    def slot(self, zt):
        return jnp.where(zt == self.z - 1, self.nz, zt)

    def xcopy(self, s):
        slot = lax.rem(s, AHEAD)
        return remote(self.xs.at[slot], self.xrecv.at[s], self.xs_s.at[slot], self.xr_s.at[s], self.partner)

    def zcopy(self, s, zt):
        ring = lax.rem(s, self.ring)
        j = s // self.nz * (self.nz + 1) + self.slot(zt)
        return remote(self.zs.at[ring], self.zrecv.at[j], self.zs_s.at[ring], self.zr_s.at[j], self.towards(zt))

    def zwait(self, j):
        remote(self.zs.at[0], self.zrecv.at[j], self.zs_s.at[0], self.zr_s.at[j], self.partner).wait_recv()

    def fetch(self, src, dst, k):
        copy = pltpu.make_async_copy(src, dst, self.loc.at[k])
        copy.start()
        return copy

    def xsend(self, s):
        @pl.when(s >= AHEAD)
        def _():
            self.xcopy(s - AHEAD).wait_send()

        i, h = self.job(s)
        self.xs[lax.rem(s, AHEAD)] = self.block(i, self.order(lax.rem(s, self.nz)), 1 - self.x, h).astype(bf16)
        self.xcopy(s).start()

    def xstep(self, s):
        k = lax.rem(s, self.nz)
        zt = self.order(k)
        i, h = self.job(s)
        self.xcopy(s).wait_recv()
        copy = self.fetch(self.xrecv.at[s], self.xtmp, 0)
        own = self.block(i, zt, self.x, h)
        slot = lax.rem(s // self.nz, 2)
        ring = lax.rem(s, self.ring)

        @pl.when((s >= self.ring) & (k < self.nz - 1))
        def _():
            self.zcopy(s - self.ring, zt).wait_send()

        self.acc[slot] = own
        copy.wait()
        total = self.acc[slot] + self.xtmp[...].astype(f32)

        @pl.when(k == self.nz - 1)
        def _():
            self.acc[slot] = total

        @pl.when(k < self.nz - 1)
        def _():
            self.zs[ring] = total.astype(bf16)

            @pl.when(jnp.logical_not(self.coming(zt)))
            def _():
                self.zcopy(s, zt).start()

    def zstep(self, s):
        k = lax.rem(s, self.nz)
        zt = self.order(k)
        ring = lax.rem(s, self.ring)

        @pl.when((k < self.nz - 1) & self.coming(zt))
        def _():
            j = s // self.nz * (self.nz + 1) + zt
            self.zwait(j)
            self.fetch(self.zrecv.at[j], self.ztmp.at[pl.ds(0, self.rn)], 1).wait()
            self.zs[ring] = (self.zs[ring].astype(f32) + self.ztmp[: self.rn].astype(f32)).astype(bf16)
            self.zcopy(s, zt).start()

    def final(self, jx):
        slot = lax.rem(jx, 2)

        def take(j):
            self.zwait(j)
            self.fetch(self.zrecv.at[j], self.ztmp.at[pl.ds(0, self.rn)], 1).wait()
            self.acc[slot] += self.ztmp[: self.rn].astype(f32)

        @pl.when(self.z > 0)
        def _():
            take(jx * (self.nz + 1) + self.z)

        @pl.when(self.z < self.nz - 1)
        def _():
            take(jx * (self.nz + 1) + self.nz)

        i, h = self.job(jx * self.nz)
        at = pl.ds(pl.multiple_of(h * self.rn, self.rn), self.rn)
        self.fetch(self.acc.at[slot], self.out.at[i, at], 2).wait()

    def fcopy(self, q, zt):
        slot = self.slot(zt)
        return remote(self.zf.at[q], self.frecv.at[slot], self.zf_s.at[q], self.zf_r.at[slot], self.towards(zt))

    def fwait(self, slot):
        remote(self.zf.at[0], self.frecv.at[slot], self.zf_s.at[0], self.zf_r.at[slot], self.partner).wait_recv()

    def fstart(self, q):
        zt = self.order(q)
        for xt in range(2):
            self.zf[q, xt * self.rn : (xt + 1) * self.rn] = self.block(0, zt, xt, 0).astype(bf16)

        @pl.when(jnp.logical_not(self.coming(zt)))
        def _():
            self.fcopy(q, zt).start()

    def fstep(self, q):
        zt = self.order(q)

        @pl.when(self.coming(zt))
        def _():
            self.fwait(zt)
            self.fetch(self.frecv.at[zt], self.ztmp, 1).wait()
            self.zf[q] = (self.zf[q].astype(f32) + self.ztmp[...].astype(f32)).astype(bf16)
            self.fcopy(q, zt).start()

    def fxcopy(self):
        return remote(self.zfx, self.fxrecv, self.fx_s.at[0], self.fx_r.at[0], self.partner)

    def fend(self):
        for xt in range(2):
            self.facc[xt * self.rn : (xt + 1) * self.rn] = self.block(0, self.z, xt, 0)

        def take(slot):
            self.fwait(slot)
            self.fetch(self.frecv.at[slot], self.ztmp, 1).wait()
            self.facc[...] += self.ztmp[...].astype(f32)

        @pl.when(self.z > 0)
        def _():
            take(self.z)

        @pl.when(self.z < self.nz - 1)
        def _():
            take(self.nz)

        away = pl.ds(pl.multiple_of((1 - self.x) * self.rn, self.rn), self.rn)
        self.zfx[...] = self.facc[away].astype(bf16)
        self.fxcopy().start()

    def ffinal(self):
        self.fxcopy().wait_recv()
        self.fetch(self.fxrecv, self.xtmp, 1).wait()
        own = pl.ds(pl.multiple_of(self.x * self.rn, self.rn), self.rn)
        self.facc[own] += self.xtmp[...].astype(f32)
        self.fetch(self.facc.at[own], self.out.at[0, pl.ds(0, self.rn)], 2).wait()

    def begin(self):
        loop(AHEAD, self.xsend)
        loop(self.nz - 1, self.fstart)

    def services(self):
        return max(self.steps + SETTLE + 1, 2 * self.nz + 5)

    def service(self, s):
        @pl.when(s < self.steps)
        def _():
            self.xstep(s)

        @pl.when(s + AHEAD < self.steps)
        def _():
            self.xsend(s + AHEAD)

        @pl.when((s >= LAG) & (s - LAG < self.steps))
        def _():
            self.zstep(s - LAG)

        @pl.when((lax.rem(s, 2) == 1) & (s // 2 < self.nz - 1))
        def _():
            self.fstep(s // 2)

        @pl.when(s == 2 * self.nz - 1)
        def _():
            self.fend()

        @pl.when(s == 2 * self.nz + 4)
        def _():
            self.ffinal()

        @pl.when((s >= self.nz + SETTLE) & (lax.rem(s - SETTLE, self.nz) == 0) & (s - SETTLE <= self.steps))
        def _():
            self.final((s - SETTLE) // self.nz - 1)

    def drain(self):
        loop(AHEAD, lambda a: self.xcopy(self.steps - AHEAD + a).wait_send())

        def zdone(a):
            s = self.steps - self.ring + a
            k = lax.rem(s, self.nz)

            @pl.when(k < self.nz - 1)
            def _():
                self.zcopy(s, self.order(k)).wait_send()

        loop(self.ring, zdone)
        loop(self.nz - 1, lambda q: self.fcopy(q, self.order(q)).wait_send())
        self.fxcopy().wait_send()


def meet(g, nz):
    z, x = g.dp // 2, lax.rem(g.dp, 2)
    barrier = pltpu.get_barrier_semaphore()

    def hello(device):
        pl.semaphore_signal(barrier, inc=1, device_id=device, device_id_type=MESH)

    hello(g.sibling)
    hello(g.across)
    hello((z * 2 + 1 - x, g.t))

    @pl.when(z > 0)
    def _():
        hello(((z - 1) * 2 + x, g.t))

    @pl.when(z < nz - 1)
    def _():
        hello(((z + 1) * 2 + x, g.t))

    peers = 5 - jnp.where(z == 0, 1, 0) - jnp.where(z == nz - 1, 1, 0)
    pl.semaphore_wait(barrier, peers)


def block_of(lefts, rights, left_of, rows, halves):
    rn = rows // halves

    def block(i, zt, xt, h):
        li, right = left_of(i), rights.at[i]
        if rows % 128:
            cols = pl.ds(pl.multiple_of(zt * (2 * rows), 2 * rows), 2 * rows)
            both = dot(lefts[li, :, cols], right[...], TN)
            return jnp.where(xt == 0, both[:rows], both[rows:])
        cols = pl.ds(pl.multiple_of((zt * 2 + xt) * rows + h * rn, rn), rn)
        return dot(lefts[li, :, cols], right[...], TN)

    return block


def norm_parts(state):
    scale = lax.rsqrt(jnp.mean(state * state, axis=-1, keepdims=True) + 1e-06)
    return state * scale, scale


def mlp_kernel(
    dp_size,
    attended, w_out, gain, valid, tokens_h, w_gate_h, w_up_h, w_down_h, cot_h,
    output, state_grad_h, gain_grad, state_all_h, totals_h, xrecv, zrecv, frecv, fxrecv,
    w_gate, w_up, w_down, lefts, rights, mid, sibsend, sibrecv, ysend, yrecv, total, spread_buf,
    xs, zs, zf, zfx, acc, facc, xtmp, ztmp,
    load_sem, sib_s, sib_r, y_s, y_r, ag_s, ag_r,
    xs_s, xr_s, zs_s, zr_s, zf_s, zf_r, fx_s, fx_r, loc,
):
    g = Group()
    own_rows, width = tokens_h.shape
    tokens = spread_buf
    hidden_units = rights.shape[2]
    rows = width // dp_size
    loads = [
        pltpu.make_async_copy(src, dst, load_sem.at[n])
        for n, (src, dst) in enumerate(
            [(w_gate_h, w_gate), (w_up_h, w_up), (w_down_h, w_down), (cot_h, lefts.at[0]), (tokens_h, tokens)]
        )
    ]
    for copy in loads:
        copy.start()
    meet(g, dp_size // 2)
    bufs = (sibsend, sibrecv, ysend, yrecv, total)
    sems = (sib_s, sib_r, y_s, y_r)

    def attn_part(r, n, w):
        return dot(attended[r], w_out[:, n : n + w])

    sums = RowSums(g, own_rows, 0, 64, attn_part, bufs, sems)
    normed = Spread(g, own_rows, 64, None, lefts.at[1], (ag_s, ag_r), 0)
    own_first = pl.multiple_of(g.t * own_rows, own_rows)

    def first_state(r, summed):
        state = tokens[r].astype(f32) + summed
        mid[r] = state
        normal, _ = norm_parts(state)
        start = pl.multiple_of(own_first + r.start, STRIP)
        lefts[1, pl.ds(start, STRIP)] = (normal * gain[...]).astype(bf16)

    sums.give(1, 0)

    def far(j):
        @pl.when(j + 1 < sums.count)
        def _():
            sums.give(1, j + 1)

        sums.send(j)

    loop(sums.count, far)

    def near(j):
        sums.give(0, j)
        sums.hold(j)

    loop(sums.count, near)

    def feed(y, c, half):
        r = pl.ds(pl.multiple_of((y * 2 + c) * own_rows + half * 128, 128), 128)
        for n, w in pieces(hidden_units, 512):
            gate = dot(lefts[1, r], w_gate[:, n : n + w])
            up = dot(lefts[1, r], w_up[:, n : n + w])
            back = dot(lefts[0, r], w_down[n : n + w], NT)
            sig = jax.nn.sigmoid(gate)
            active = gate * sig
            rights[0, r, n : n + w] = (active * up).astype(bf16)
            rights[1, r, n : n + w] = (back * up * sig * (1.0 + gate * (1.0 - sig))).astype(bf16)
            rights[2, r, n : n + w] = (back * active).astype(bf16)

    def close(j):
        sums.finish(j, first_state)
        normed.start(j)

    loads[4].wait()

    def half_near(half):
        loop(2, lambda a: close(half * 2 + a))

        @pl.when(half == 0)
        def _():
            for copy in loads[:4]:
                copy.wait()

        feed(g.y, g.c, half)
        loop(2, lambda a: normed.sib_in(half * 2 + a))
        feed(g.y, 1 - g.c, half)

    loop(2, half_near)

    def half_far(half):
        loop(2, lambda a: normed.relay(half * 2 + a))
        feed(1 - g.y, g.c, half)
        loop(2, lambda a: normed.far_in(half * 2 + a))
        feed(1 - g.y, 1 - g.c, half)

    loop(2, half_far)
    sums.drain()

    halves = max(1, rows // 128)
    engine = WeightSums(
        g, dp_size, rows, 3, block_of(lefts, rights, lambda i: jnp.minimum(i, 1), rows, halves), None,
        (xs, zs, zf, zfx, acc, facc, xtmp, ztmp, xrecv, zrecv, frecv, fxrecv),
        (xs_s, xr_s, zs_s, zr_s, zf_s, zf_r, fx_s, fx_r, loc), totals_h,
    )
    engine.begin()

    def back_part(r, n, w):
        return dot(rights[1, r], w_gate[n : n + w], NT) + dot(rights[2, r], w_up[n : n + w], NT)

    sums = RowSums(g, own_rows, 1, 128, back_part, bufs, sems)
    states = Spread(g, own_rows, 128, spread_buf, state_all_h, (ag_s, ag_r), 1)
    gain_grad[...] = jnp.zeros_like(gain_grad)

    def state_back(r, grad):
        normal, scale = norm_parts(mid[r])
        weighted = grad * gain[...]
        start = pl.multiple_of(own_first + r.start, STRIP)
        change = scale * (weighted - normal * jnp.mean(weighted * normal, axis=-1, keepdims=True))
        state = lefts[0, pl.ds(start, STRIP)].astype(f32) + change
        gain_grad[...] += jnp.sum(grad * normal, axis=0, keepdims=True)
        total[r] = state
        spread_buf[r] = state.astype(bf16)

    def far_back(j):
        sums.give(1, j)
        sums.send(j)

    loop(sums.count, far_back)

    def near_back(j):
        sums.give(0, j)
        engine.service(2 * j)
        sums.hold(j)
        engine.service(2 * j + 1)

    loop(sums.count, near_back)
    used = 2 * sums.count

    def own_copy(j):
        r = pl.ds(pl.multiple_of(j * 128, 128), 128)
        to = pl.ds(pl.multiple_of(own_first + j * 128, 128), 128)
        return (
            pltpu.make_async_copy(total.at[r], state_grad_h.at[r], load_sem.at[0]),
            pltpu.make_async_copy(spread_buf.at[r], state_all_h.at[to], load_sem.at[1]),
        )

    def close_back(j):
        sums.finish(j, state_back)
        states.start(j)
        copies = own_copy(j)
        for copy in copies:
            copy.start()
        engine.service(used + j)
        for copy in copies:
            copy.wait()

    loop(sums.count, close_back)
    used = used + sums.count

    def pass_back(j):
        states.relay(j)
        engine.service(used + j)

    loop(sums.count, pass_back)
    used = used + sums.count

    def arrive(j):
        states.sib_in(j)
        states.far_in(j)

    loop(sums.count, arrive)
    sums.drain()

    def down_part(r, n, w):
        return dot(rights[0, r], w_down[:, n : n + w])

    sums = RowSums(g, own_rows, 2, 128, down_part, bufs, sems)

    def far_down(j):
        sums.give(1, j)
        engine.service(used + 2 * j)
        sums.send(j)
        engine.service(used + 2 * j + 1)

    loop(sums.count, far_down)
    used = used + 2 * sums.count

    def near_down(j):
        sums.give(0, j)
        sums.hold(j)
        engine.service(used + j)

    loop(sums.count, near_down)
    used = used + sums.count

    def last_state(r, summed):
        output[r] = (valid[r] * (mid[r] + summed)).astype(bf16)

    loop(sums.count, lambda j: sums.finish(j, last_state))
    loop(engine.services() - used, lambda n: engine.service(used + n))
    sums.drain()
    normed.drain()
    states.drain()
    engine.drain()


def mlp_call(attended, w_out, tokens, gain, valid, w_gate, w_up, w_down, cot_all, collective_id):
    dp_size = lax.axis_size("dp")
    nz = dp_size // 2
    own_rows, width = tokens.shape
    bucket = cot_all.shape[0]
    units = w_gate.shape[1]
    rows = width // dp_size
    halves = max(1, rows // 128)
    rn = rows // halves
    jobs = 3 * halves - 1
    steps = jobs * nz
    vm, hbm = pl.BlockSpec(memory_space=pltpu.VMEM), pl.BlockSpec(memory_space=pl.ANY)
    dma = lambda *shape: pltpu.SemaphoreType.DMA(shape)
    vmem = lambda shape, kind=bf16: pltpu.VMEM(shape, kind)
    sds = jax.ShapeDtypeStruct
    outs = pl.pallas_call(
        functools.partial(mlp_kernel, dp_size),
        out_shape=[
            sds((own_rows, width), bf16),
            sds((own_rows, width), f32),
            sds((1, width), f32),
            sds((bucket, width), bf16),
            sds((3, rows, units), f32),
            sds((steps, rn, units), bf16),
            sds((jobs * (nz + 1), rn, units), bf16),
            sds((nz + 1, 2 * rn, units), bf16),
            sds((rn, units), bf16),
        ],
        in_specs=[vm] * 4 + [hbm] * 5,
        out_specs=[vm, hbm, vm] + [hbm] * 6,
        scratch_shapes=[
            vmem((width, units)), vmem((width, units)), vmem((units, width)),
            vmem((2, bucket, width)), vmem((3, bucket, units)), vmem((own_rows, width), f32),
            vmem((2, own_rows, width)), vmem((2, own_rows, width)), vmem((own_rows, width)), vmem((own_rows, width)),
            vmem((own_rows, width), f32), vmem((own_rows, width)),
            vmem((AHEAD, rn, units)), vmem((WeightSums.zs_slots(nz), rn, units)), vmem((nz - 1, 2 * rn, units)), vmem((rn, units)),
            vmem((2, rn, units), f32), vmem((2 * rn, units), f32), vmem((rn, units)), vmem((2 * rn, units)),
            dma(5), dma(3, 2, 4), dma(3, 2, 4), dma(3, 4), dma(3, 4), dma(2, 3, 4), dma(2, 3, 4),
            dma(AHEAD), dma(steps), dma(WeightSums.zs_slots(nz)), dma(jobs * (nz + 1)), dma(nz), dma(nz + 1), dma(1), dma(1), dma(3),
        ],
        compiler_params=pltpu.CompilerParams(
            collective_id=collective_id, has_side_effects=True, vmem_limit_bytes=62 << 20
        ),
        name="mlp",
    )(attended, w_out, gain, valid, tokens, w_gate, w_up, w_down, cot_all)
    return outs[:5]


def weight_kernel(dp_size, count, x_of, *refs):
    n_x = max(x_of) + 1
    lefts, refs = refs[:n_x], refs[n_x:]
    rights, refs = refs[:count], refs[count:]
    outs, refs = refs[:count], refs[count:]
    xsend, xrecv, zsend, zrecv = (refs[i * count : (i + 1) * count] for i in range(4))
    xs_sem, xr_sem, zs_sem, zr_sem = refs[4 * count :]
    nz = dp_size // 2
    rows = outs[0].shape[0]
    dp = lax.axis_index("dp")
    tensor = lax.axis_index("tensor")
    z, x = dp // 2, lax.rem(dp, 2)
    partner = (z * 2 + 1 - x, tensor)

    def target(k):
        return lax.rem(z + 1 + k, nz)

    barrier = pltpu.get_barrier_semaphore()
    pl.semaphore_signal(barrier, inc=1, device_id=partner, device_id_type=MESH)
    for k in range(nz - 1):
        pl.semaphore_signal(barrier, inc=1, device_id=(target(k) * 2 + x, tensor), device_id_type=MESH)
    pl.semaphore_wait(barrier, nz)

    def block(i, zt, xt):
        start = pl.multiple_of((zt * 2 + xt) * rows, rows)
        if rows % 128:
            left, dims = lefts[x_of[i]][pl.ds(start, rows), :], ((1,), (0,))
        else:
            left, dims = lefts[x_of[i]][:, pl.ds(start, rows)], ((0,), (0,))
        return lax.dot_general(left, rights[i][...], (dims, ((), ())), preferred_element_type=f32)

    def xcopy(i, k):
        return pltpu.make_async_remote_copy(
            xsend[i].at[k], xrecv[i].at[k], xs_sem.at[i, k], xr_sem.at[i, k], device_id=partner, device_id_type=MESH
        )

    def zcopy(i, k):
        return pltpu.make_async_remote_copy(
            zsend[i].at[k], zrecv[i].at[k], zs_sem.at[i, k], zr_sem.at[i, k],
            device_id=(target(k) * 2 + x, tensor), device_id_type=MESH,
        )

    def cross(i):
        def body(k, carry):
            xsend[i][k] = block(i, target(k), 1 - x).astype(bf16)
            if i == 0:
                @pl.when(k < 2)
                def _():
                    xcopy(i, k).start()
            return carry
        lax.fori_loop(0, nz, body, 0)

    def more(i, k):
        if i + 1 < count:
            later = k + 2
            @pl.when(later < nz)
            def _():
                xcopy(i, later).start()
            @pl.when(later >= nz)
            def _():
                xcopy(i + 1, later - nz).start()
        else:
            @pl.when(k + 2 < nz)
            def _():
                xcopy(i, k + 2).start()

    def keep(i):
        def body(k, carry):
            own = block(i, target(k), x)
            xcopy(i, k).wait_recv()
            more(i, k)
            zsend[i][k] = (own + xrecv[i][k].astype(f32)).astype(bf16)
            zcopy(i, k).start()
            return carry
        lax.fori_loop(0, nz - 1, body, 0)
        own = block(i, z, x)
        xcopy(i, nz - 1).wait_recv()
        more(i, nz - 1)
        outs[i][...] = own + xrecv[i][nz - 1].astype(f32)

    cross(0)
    for i in range(count):
        if i + 1 < count:
            cross(i + 1)
        keep(i)
    for i in range(count):
        def add(k, carry):
            zcopy(i, k).wait_recv()
            outs[i][...] += zrecv[i][k].astype(f32)
            return carry
        lax.fori_loop(0, nz - 1, add, 0)
    for i in range(count):
        def done(k, carry):
            zcopy(i, k).wait_send()
            return carry
        lax.fori_loop(0, nz - 1, done, 0)
        def donex(k, carry):
            xcopy(i, k).wait_send()
            return carry
        lax.fori_loop(0, nz, donex, 0)


def weight_sums(lefts, rights, x_of, collective_id):
    dp_size = lax.axis_size("dp")
    nz = dp_size // 2
    count = len(rights)
    rows = lefts[0].shape[1] // dp_size
    if rows % 128:
        lefts = [left.T for left in lefts]
    buf = lambda n: [pltpu.VMEM((n, rows, r.shape[1]), bf16) for r in rights]
    vm = pl.BlockSpec(memory_space=pltpu.VMEM)
    sem = lambda n: pltpu.SemaphoreType.DMA((count, n))
    return pl.pallas_call(
        functools.partial(weight_kernel, dp_size, count, x_of),
        out_shape=[jax.ShapeDtypeStruct((rows, r.shape[1]), f32) for r in rights],
        in_specs=[vm] * (len(lefts) + count),
        out_specs=[vm] * count,
        scratch_shapes=buf(nz) + buf(nz) + buf(nz - 1) + buf(nz - 1) + [sem(nz), sem(nz), sem(nz - 1), sem(nz - 1)],
        compiler_params=pltpu.CompilerParams(
            collective_id=collective_id, has_side_effects=True, vmem_limit_bytes=60 << 20
        ),
        name="weight_sums",
    )(*lefts, *rights)


def norm_forward(source, gain_vec):
    inv_scale = lax.rsqrt(jnp.mean(source * source, axis=-1, keepdims=True) + 1e-06)
    normal = source * inv_scale
    return (normal, inv_scale, (normal * gain_vec).astype(jnp.bfloat16))


def norm_back(grad_norm, normal, inv_scale, gain_vec):
    weighted = grad_norm * gain_vec
    return inv_scale * (weighted - normal * jnp.mean(weighted * normal, axis=-1, keepdims=True))


def per_device(
    tokens,
    gain_attn,
    gain_mlp,
    w_query,
    w_key,
    w_value,
    w_out,
    w_gate,
    w_up,
    w_down,
    cotangent,
    lengths,
):
    tok_rows = tokens.shape[0]
    groups = lax.axis_size("tensor")
    bucket = tok_rows * groups
    length = lengths[lax.axis_index("dp")]
    position = jnp.arange(bucket, dtype=jnp.int32)
    valid_rows = (position < length).astype(jnp.float32)
    own_rows = lax.axis_index("tensor") * tok_rows + jnp.arange(tok_rows, dtype=jnp.int32)
    own_valid = (own_rows < length).astype(jnp.float32)[:, None]
    head_count = w_query.shape[1] // FEAT
    head_width = w_value.shape[1] // head_count
    qk_scale = 1.0 / math.sqrt(FEAT)
    block_rows = min(512, bucket)
    float_single = jnp.float32
    bf16 = jnp.bfloat16
    x_full = tokens.astype(float_single)
    normal_attn, scale_attn, normed = norm_forward(x_full, gain_attn)
    normed_all = lax.all_gather(normed, "tensor", axis=0, tiled=True)
    query_rows = (
        jnp.dot(normed_all, w_query, preferred_element_type=float_single)
        .astype(bf16)
        .reshape(bucket, head_count, FEAT)
    )
    key_head_rows = (
        jnp.dot(normed_all, w_key, preferred_element_type=float_single)
        .astype(bf16)
        .reshape(bucket, head_count, FEAT)
    )
    value_heads = (
        jnp.dot(normed_all, w_value, preferred_element_type=float_single)
        .astype(bf16)
        .reshape(bucket, head_count, head_width)
    )

    def block_scores(first_row_index, last_row_index):
        scores = (
            jnp.einsum(
                "wra,tra->rwt",
                query_rows[first_row_index:last_row_index],
                key_head_rows[:last_row_index],
                preferred_element_type=float_single,
            )
            * qk_scale
        )
        key_mask = (
            (position[None, :last_row_index] <= position[first_row_index:last_row_index, None])
            & (position[None, :last_row_index] < length)
        ).astype(float_single)
        taylor = (1.0 + scores + 0.5 * scores * scores) * key_mask
        return (scores, key_mask, taylor)

    numer_parts = []
    denom_parts = []
    for first_row_index in range(0, bucket, block_rows):
        last_row_index = first_row_index + block_rows
        scores, key_mask, taylor = block_scores(first_row_index, last_row_index)
        numer_parts.append(
            jnp.einsum(
                "hqk,khv->qhv",
                taylor.astype(bf16),
                value_heads[:last_row_index],
                preferred_element_type=float_single,
            )
        )
        denom_parts.append(jnp.sum(taylor, axis=-1).T)
    numerator = jnp.concatenate(numer_parts, axis=0)
    denominator = jnp.concatenate(denom_parts, axis=0)
    attended = (
        (numerator / denominator[:, :, None]).reshape(bucket, head_count * head_width).astype(bf16)
    )
    den_part = jnp.sum(denominator * (valid_rows / (position + 1.0))[:, None])
    den_total = lax.psum(den_part, ("dp", "tensor"))
    grad_out = cotangent.astype(float_single) * own_valid
    grad_mlp_all = lax.all_gather(grad_out.astype(bf16), "tensor", axis=0, tiled=True)
    output, grad_state, gain_mlp_part, grad_attn_all, mlp_totals = mlp_call(
        attended, w_out, tokens, gain_mlp[None], own_valid, w_gate, w_up, w_down, grad_mlp_all, 1
    )
    gain_mlp_part = gain_mlp_part[0]
    down_total, gate_total, up_total = mlp_totals[0], mlp_totals[1], mlp_totals[2]
    grad_attended = jnp.einsum(
        "td,vd->tv", grad_attn_all, w_out, preferred_element_type=float_single
    ).astype(bf16)
    grad_attended = grad_attended.reshape(bucket, head_count, head_width).astype(float_single)
    grad_numerator = (grad_attended / denominator[:, :, None]).astype(bf16)
    grad_denominator = -jnp.sum(grad_attended * numerator, axis=-1) / (denominator * denominator)
    grad_value_acc = jnp.zeros((bucket, head_count, head_width), float_single)
    grad_key_acc = jnp.zeros((bucket, head_count, FEAT), float_single)
    query_parts = []
    for first_row_index in range(0, bucket, block_rows):
        last_row_index = first_row_index + block_rows
        scores, key_mask, taylor = block_scores(first_row_index, last_row_index)
        numer_block = grad_numerator[first_row_index:last_row_index]
        grad_value_acc = grad_value_acc.at[:last_row_index].add(
            jnp.einsum(
                "hqk,qhv->khv",
                taylor.astype(bf16),
                numer_block,
                preferred_element_type=float_single,
            )
        )
        taylor_feature_gradient = jnp.einsum(
            "qhv,khv->hqk",
            numer_block,
            value_heads[:last_row_index],
            preferred_element_type=float_single,
        )
        taylor_feature_gradient = (
            taylor_feature_gradient + grad_denominator[first_row_index:last_row_index].T[:, :, None]
        )
        score_gradients = (taylor_feature_gradient * key_mask * (1.0 + scores)).astype(bf16)
        query_parts.append(
            jnp.einsum(
                "dwr,rdj->wdj",
                score_gradients,
                key_head_rows[:last_row_index],
                preferred_element_type=float_single,
            )
            * qk_scale
        )
        grad_key_acc = grad_key_acc.at[:last_row_index].add(
            jnp.einsum(
                "nor,onz->rnz",
                score_gradients,
                query_rows[first_row_index:last_row_index],
                preferred_element_type=float_single,
            )
            * qk_scale
        )
    grad_queries = (
        jnp.concatenate(query_parts, axis=0).reshape(bucket, head_count * FEAT).astype(bf16)
    )
    grad_keys = grad_key_acc.reshape(bucket, head_count * FEAT).astype(bf16)
    grad_values = grad_value_acc.reshape(bucket, head_count * head_width).astype(bf16)
    part_query = jnp.einsum("tf,df->td", grad_queries, w_query, preferred_element_type=float_single)
    part_key = jnp.einsum("tf,df->td", grad_keys, w_key, preferred_element_type=float_single)
    part_value = jnp.einsum("tf,df->td", grad_values, w_value, preferred_element_type=float_single)
    grad_normed = lax.psum_scatter(
        (part_query + part_key + part_value).astype(jnp.bfloat16),
        "tensor",
        scatter_dimension=0,
        tiled=True,
    ).astype(jnp.float32)
    gain_attn_part = jnp.sum(grad_normed * normal_attn, axis=0)
    input_grad = grad_state + norm_back(grad_normed, normal_attn, scale_attn, gain_attn)
    qk_width = head_count * FEAT
    out_total, qkv_total = weight_sums(
        (grad_attn_all, normed_all),
        (attended, jnp.concatenate([grad_values, grad_queries, grad_keys], axis=1)),
        (0, 1),
        2,
    )
    value_width = head_count * head_width
    value_total = qkv_total[:, :value_width]
    query_total = qkv_total[:, value_width : value_width + qk_width]
    key_total = qkv_total[:, value_width + qk_width :]
    gain_attn_total, gain_mlp_total = lax.psum((gain_attn_part, gain_mlp_part), ("dp", "tensor"))
    den_mean = den_total / (head_count * groups * jnp.sum(lengths).astype(float_single))
    return (
        output,
        input_grad,
        gain_attn_total,
        gain_mlp_total,
        query_total,
        key_total,
        value_total,
        out_total.T,
        gate_total,
        up_total,
        down_total.T,
        den_mean,
    )


def solution(mesh):
    return jax.shard_map(
        per_device,
        mesh=mesh,
        in_specs=(
            P(("dp", "tensor"), None),
            P(),
            P(),
            P(None, "tensor"),
            P(None, "tensor"),
            P(None, "tensor"),
            P("tensor", None),
            P(None, "tensor"),
            P(None, "tensor"),
            P("tensor", None),
            P(("dp", "tensor"), None),
            P(),
        ),
        out_specs=(
            P(("dp", "tensor"), None),
            P(("dp", "tensor"), None),
            P(),
            P(),
            P("dp", "tensor"),
            P("dp", "tensor"),
            P("dp", "tensor"),
            P("tensor", "dp"),
            P("dp", "tensor"),
            P("dp", "tensor"),
            P("tensor", "dp"),
            P(),
        ),
        check_vma=False,
    )
```

```python
import functools
import math

import jax
import jax.numpy as jnp
from jax import lax
from jax.experimental import pallas as pl
from jax.experimental.pallas import tpu as pltpu
from jax.sharding import PartitionSpec as P

FEAT = 16
MESH = pl.DeviceIdType.MESH
f32 = jnp.float32
bf16 = jnp.bfloat16
NT = (((1,), (1,)), ((), ()))
TN = (((0,), (0,)), ((), ()))
AHEAD = 4
LAG = 2
SETTLE = 3
STRIP = 16


def dot(a, b, dims=(((1,), (0,)), ((), ()))):
    return lax.dot_general(a, b, dims, preferred_element_type=f32)


def loop(count, body):
    def step(i, carry):
        body(i)
        return carry

    lax.fori_loop(0, count, step, 0)


def pieces(width, size):
    return [(start, min(size, width - start)) for start in range(0, width, size)]


class Group:
    def __init__(self):
        self.dp = lax.axis_index("dp")
        self.t = lax.axis_index("tensor")
        self.y, self.c = self.t // 2, lax.rem(self.t, 2)
        self.sibling = (self.dp, self.y * 2 + 1 - self.c)
        self.across = (self.dp, (1 - self.y) * 2 + self.c)


def remote(src, dst, send, recv, device):
    return pltpu.make_async_remote_copy(src, dst, send, recv, device_id=device, device_id_type=MESH)


class RowSums:
    def __init__(self, g, own_rows, phase, chunk, part, bufs, sems):
        self.g, self.own, self.p, self.chunk, self.part = g, own_rows, phase, chunk, part
        self.sibsend, self.sibrecv, self.ysend, self.yrecv, self.total = bufs
        self.sib_s, self.sib_r, self.y_s, self.y_r = sems
        self.count = own_rows // chunk

    def at(self, j):
        return pl.ds(pl.multiple_of(j * self.chunk, self.chunk), self.chunk)

    def rows(self, y, c, j):
        return pl.ds(pl.multiple_of((y * 2 + c) * self.own + j * self.chunk, self.chunk), self.chunk)

    def sib(self, far, j):
        return remote(
            self.sibsend.at[far, self.at(j)], self.sibrecv.at[far, self.at(j)],
            self.sib_s.at[self.p, far, j], self.sib_r.at[self.p, far, j], self.g.sibling,
        )

    def ycopy(self, j):
        return remote(
            self.ysend.at[self.at(j)], self.yrecv.at[self.at(j)],
            self.y_s.at[self.p, j], self.y_r.at[self.p, j], self.g.across,
        )

    def give(self, far, j):
        y = 1 - self.g.y if far else self.g.y
        for n, w in pieces(self.total.shape[1], 512):
            self.sibsend[far, self.at(j), n : n + w] = self.part(self.rows(y, 1 - self.g.c, j), n, w).astype(bf16)
        self.sib(far, j).start()

    def send(self, j):
        g = self.g
        for n, w in pieces(self.total.shape[1], 512):
            self.total[self.at(j), n : n + w] = self.part(self.rows(1 - g.y, g.c, j), n, w)
        self.sib(1, j).wait_recv()
        self.ysend[self.at(j)] = (self.total[self.at(j)] + self.sibrecv[1, self.at(j)].astype(f32)).astype(bf16)
        self.ycopy(j).start()

    def hold(self, j):
        for n, w in pieces(self.total.shape[1], 512):
            self.total[self.at(j), n : n + w] = self.part(self.rows(self.g.y, self.g.c, j), n, w)

    def finish(self, j, use):
        self.sib(0, j).wait_recv()
        self.ycopy(j).wait_recv()

        def strip(i):
            r = pl.ds(pl.multiple_of(j * self.chunk + i * STRIP, STRIP), STRIP)
            use(r, self.total[r] + self.sibrecv[0, r].astype(f32) + self.yrecv[r].astype(f32))

        loop(self.chunk // STRIP, strip)

    def drain(self):
        def body(j):
            self.sib(0, j).wait_send()
            self.sib(1, j).wait_send()
            self.ycopy(j).wait_send()

        loop(self.count, body)


class Spread:
    def __init__(self, g, own_rows, chunk, src, full, sems, phase):
        self.g, self.own, self.chunk, self.src, self.full, self.p = g, own_rows, chunk, src, full, phase
        self.s, self.r = sems
        self.count = own_rows // chunk

    def rows(self, y, c, j):
        return pl.ds(pl.multiple_of((y * 2 + c) * self.own + j * self.chunk, self.chunk), self.chunk)

    def copy(self, kind, j):
        g = self.g
        rows = self.rows(g.y, g.c, j)
        if kind == 2:
            rows = self.rows(1 - g.y, g.c, j)
            src = self.full.at[rows]
        elif self.src is None:
            src = self.full.at[rows]
        else:
            src = self.src.at[pl.ds(pl.multiple_of(j * self.chunk, self.chunk), self.chunk)]
        return remote(
            src, self.full.at[rows], self.s.at[self.p, kind, j], self.r.at[self.p, kind, j],
            g.across if kind == 1 else g.sibling,
        )

    def start(self, j):
        self.copy(1, j).start()
        self.copy(0, j).start()

    def relay(self, j):
        self.copy(1, j).wait_recv()
        self.copy(2, j).start()

    def sib_in(self, j):
        self.copy(0, j).wait_recv()

    def far_in(self, j):
        self.copy(2, j).wait_recv()

    def drain(self):
        def body(j):
            for kind in range(3):
                self.copy(kind, j).wait_send()

        loop(self.count, body)


class WeightSums:
    def __init__(self, g, dp_size, rows, jobs, z_first, block, refs, sems, emit):
        self.g, self.rows, self.block, self.z_first, self.emit = g, rows, block, z_first, emit
        self.nz = dp_size // 2
        self.z, self.x = g.dp // 2, lax.rem(g.dp, 2)
        self.halves = max(1, rows // 128)
        self.rn = rows // self.halves
        self.ring = self.zs_slots(self.nz)
        self.jobs = jobs * self.halves - z_first
        self.steps = self.jobs * self.nz
        self.xs, self.zs, self.acc, self.xtmp, self.ztmp, self.xrecv, self.zrecv = refs[:7]
        self.xs_s, self.xr_s, self.zs_s, self.zr_s, self.loc = sems[:5]
        if z_first:
            self.zf, self.zfx, self.facc, self.frecv, self.fxrecv = refs[7:]
            self.zf_s, self.zf_r, self.fx_s, self.fx_r = sems[5:]
        self.ahead = self.xs.shape[0]
        self.partner = (self.z * 2 + 1 - self.x, g.t)

    @staticmethod
    def zs_slots(nz):
        return 2 * nz if nz <= 4 else nz

    def job(self, s):
        lin = s // self.nz + self.z_first
        return lin // self.halves, lax.rem(lin, self.halves)

    def order(self, k):
        last = self.nz - 1
        upper = self.z >= self.nz // 2
        z = jnp.where(upper, last - self.z, self.z)
        zt = jnp.where(k < last - z, last - k, jnp.where(k < last, last - 1 - k, z))
        return jnp.where(upper, last - zt, zt)

    def coming(self, zt):
        return jnp.where(zt > self.z, self.z > 0, self.z < self.nz - 1)

    def towards(self, zt):
        return (jnp.where(zt > self.z, self.z + 1, self.z - 1) * 2 + self.x, self.g.t)

    def slot(self, zt):
        return jnp.where(zt == self.z - 1, self.nz, zt)

    def xcopy(self, s):
        slot = lax.rem(s, self.ahead)
        return remote(self.xs.at[slot], self.xrecv.at[s], self.xs_s.at[slot], self.xr_s.at[s], self.partner)

    def zcopy(self, s, zt):
        ring = lax.rem(s, self.ring)
        j = s // self.nz * (self.nz + 1) + self.slot(zt)
        return remote(self.zs.at[ring], self.zrecv.at[j], self.zs_s.at[ring], self.zr_s.at[j], self.towards(zt))

    def zwait(self, j):
        remote(self.zs.at[0], self.zrecv.at[j], self.zs_s.at[0], self.zr_s.at[j], self.partner).wait_recv()

    def fetch(self, src, dst, k):
        copy = pltpu.make_async_copy(src, dst, self.loc.at[k])
        copy.start()
        return copy

    def xsend(self, s):
        @pl.when(s >= self.ahead)
        def _():
            self.xcopy(s - self.ahead).wait_send()

        i, h = self.job(s)
        self.xs[lax.rem(s, self.ahead)] = self.block(i, self.order(lax.rem(s, self.nz)), 1 - self.x, h).astype(bf16)
        self.xcopy(s).start()

    def xstep(self, s):
        k = lax.rem(s, self.nz)
        zt = self.order(k)
        i, h = self.job(s)
        self.xcopy(s).wait_recv()
        copy = self.fetch(self.xrecv.at[s], self.xtmp, 0)
        own = self.block(i, zt, self.x, h)
        slot = lax.rem(s // self.nz, 2)
        ring = lax.rem(s, self.ring)

        @pl.when((s >= self.ring) & (k < self.nz - 1))
        def _():
            self.zcopy(s - self.ring, zt).wait_send()

        self.acc[slot] = own
        copy.wait()
        total = self.acc[slot] + self.xtmp[...].astype(f32)

        @pl.when(k == self.nz - 1)
        def _():
            self.acc[slot] = total

        @pl.when(k < self.nz - 1)
        def _():
            self.zs[ring] = total.astype(bf16)

            @pl.when(jnp.logical_not(self.coming(zt)))
            def _():
                self.zcopy(s, zt).start()

    def zstep(self, s):
        k = lax.rem(s, self.nz)
        zt = self.order(k)
        ring = lax.rem(s, self.ring)

        @pl.when((k < self.nz - 1) & self.coming(zt))
        def _():
            j = s // self.nz * (self.nz + 1) + zt
            self.zwait(j)
            self.fetch(self.zrecv.at[j], self.ztmp.at[pl.ds(0, self.rn)], 1).wait()
            self.zs[ring] = (self.zs[ring].astype(f32) + self.ztmp[: self.rn].astype(f32)).astype(bf16)
            self.zcopy(s, zt).start()

    def final(self, jx):
        slot = lax.rem(jx, 2)

        def take(j):
            self.zwait(j)
            self.fetch(self.zrecv.at[j], self.ztmp.at[pl.ds(0, self.rn)], 1).wait()
            self.acc[slot] += self.ztmp[: self.rn].astype(f32)

        @pl.when(self.z > 0)
        def _():
            take(jx * (self.nz + 1) + self.z)

        @pl.when(self.z < self.nz - 1)
        def _():
            take(jx * (self.nz + 1) + self.nz)

        i, h = self.job(jx * self.nz)
        self.emit(i, h, lambda n, w: self.acc[slot, :, n : n + w])

    def fcopy(self, q, zt):
        slot = self.slot(zt)
        return remote(self.zf.at[q], self.frecv.at[slot], self.zf_s.at[q], self.zf_r.at[slot], self.towards(zt))

    def fwait(self, slot):
        remote(self.zf.at[0], self.frecv.at[slot], self.zf_s.at[0], self.zf_r.at[slot], self.partner).wait_recv()

    def fstart(self, q):
        zt = self.order(q)
        for xt in range(2):
            self.zf[q, xt * self.rn : (xt + 1) * self.rn] = self.block(0, zt, xt, 0).astype(bf16)

        @pl.when(jnp.logical_not(self.coming(zt)))
        def _():
            self.fcopy(q, zt).start()

    def fstep(self, q):
        zt = self.order(q)

        @pl.when(self.coming(zt))
        def _():
            self.fwait(zt)
            self.fetch(self.frecv.at[zt], self.ztmp, 1).wait()
            self.zf[q] = (self.zf[q].astype(f32) + self.ztmp[...].astype(f32)).astype(bf16)
            self.fcopy(q, zt).start()

    def fxcopy(self):
        return remote(self.zfx, self.fxrecv, self.fx_s.at[0], self.fx_r.at[0], self.partner)

    def fend(self):
        for xt in range(2):
            self.facc[xt * self.rn : (xt + 1) * self.rn] = self.block(0, self.z, xt, 0)

        def take(slot):
            self.fwait(slot)
            self.fetch(self.frecv.at[slot], self.ztmp, 1).wait()
            self.facc[...] += self.ztmp[...].astype(f32)

        @pl.when(self.z > 0)
        def _():
            take(self.z)

        @pl.when(self.z < self.nz - 1)
        def _():
            take(self.nz)

        away = pl.ds(pl.multiple_of((1 - self.x) * self.rn, self.rn), self.rn)
        self.zfx[...] = self.facc[away].astype(bf16)
        self.fxcopy().start()

    def ffinal(self):
        self.fxcopy().wait_recv()
        self.fetch(self.fxrecv, self.xtmp, 1).wait()
        own = pl.ds(pl.multiple_of(self.x * self.rn, self.rn), self.rn)
        self.facc[own] += self.xtmp[...].astype(f32)
        self.emit(0, 0, lambda n, w: self.facc[own, n : n + w])

    def begin(self):
        loop(self.ahead, self.xsend)
        if self.z_first:
            loop(self.nz - 1, self.fstart)

    def services(self):
        return max(self.steps + SETTLE + 1, self.z_first * (2 * self.nz + 5))

    def service(self, s):
        @pl.when(s < self.steps)
        def _():
            self.xstep(s)

        @pl.when(s + self.ahead < self.steps)
        def _():
            self.xsend(s + self.ahead)

        @pl.when((s >= LAG) & (s - LAG < self.steps))
        def _():
            self.zstep(s - LAG)

        if self.z_first:

            @pl.when((lax.rem(s, 2) == 1) & (s // 2 < self.nz - 1))
            def _():
                self.fstep(s // 2)

            @pl.when(s == 2 * self.nz - 1)
            def _():
                self.fend()

            @pl.when(s == 2 * self.nz + 4)
            def _():
                self.ffinal()

        @pl.when((s >= self.nz + SETTLE) & (lax.rem(s - SETTLE, self.nz) == 0) & (s - SETTLE <= self.steps))
        def _():
            self.final((s - SETTLE) // self.nz - 1)

    def drain(self):
        loop(self.ahead, lambda a: self.xcopy(self.steps - self.ahead + a).wait_send())

        def zdone(a):
            s = self.steps - self.ring + a
            k = lax.rem(s, self.nz)

            @pl.when(k < self.nz - 1)
            def _():
                self.zcopy(s, self.order(k)).wait_send()

        loop(self.ring, zdone)
        if self.z_first:
            loop(self.nz - 1, lambda q: self.fcopy(q, self.order(q)).wait_send())
            self.fxcopy().wait_send()


def meet(g, nz, every=False):
    z, x = g.dp // 2, lax.rem(g.dp, 2)
    barrier = pltpu.get_barrier_semaphore()

    def hello(device):
        pl.semaphore_signal(barrier, inc=1, device_id=device, device_id_type=MESH)

    hello(g.sibling)
    hello(g.across)
    hello((z * 2 + 1 - x, g.t))
    if every:
        loop(nz - 1, lambda k: hello((lax.rem(z + 1 + k, nz) * 2 + x, g.t)))
        pl.semaphore_wait(barrier, nz + 2)
        return

    @pl.when(z > 0)
    def _():
        hello(((z - 1) * 2 + x, g.t))

    @pl.when(z < nz - 1)
    def _():
        hello(((z + 1) * 2 + x, g.t))

    peers = 5 - jnp.where(z == 0, 1, 0) - jnp.where(z == nz - 1, 1, 0)
    pl.semaphore_wait(barrier, peers)


def turned(out, turn, sem, halves, rn):
    def emit(i, h, value):
        for n, w in pieces(out.shape[1], 512):
            turn[:w] = value(n, w).T
            to = out.at[i, pl.ds(n, w)]
            if halves > 1:
                to = out.at[i, pl.ds(n, w), pl.ds(pl.multiple_of(h * rn, rn), rn)]
            copy = pltpu.make_async_copy(turn.at[pl.ds(0, w)], to, sem)
            copy.start()
            copy.wait()

    return emit


def block_of(lefts, rights, left_of, rows, halves):
    rn = rows // halves

    def block(i, zt, xt, h):
        li, right = left_of(i), rights.at[i]
        if rows % 128:
            cols = pl.ds(pl.multiple_of(zt * (2 * rows), 2 * rows), 2 * rows)
            both = dot(lefts[li, :, cols], right[...], TN)
            return jnp.where(xt == 0, both[:rows], both[rows:])
        cols = pl.ds(pl.multiple_of((zt * 2 + xt) * rows + h * rn, rn), rn)
        return dot(lefts[li, :, cols], right[...], TN)

    return block


def norm_parts(state):
    scale = lax.rsqrt(jnp.mean(state * state, axis=-1, keepdims=True) + 1e-06)
    return state * scale, scale


def mlp_kernel(
    dp_size,
    attended, w_out, gain, valid, tokens_h, w_gate_h, w_up_h, w_down_h, cot_h,
    output, state_grad_h, gain_grad, state_all_h, totals_h, xrecv, zrecv, frecv, fxrecv,
    w_gate, w_up, w_down, lefts, rights, mid, sibsend, sibrecv, ysend, yrecv, total, spread_buf,
    xs, zs, zf, zfx, acc, facc, xtmp, ztmp, turn,
    load_sem, sib_s, sib_r, y_s, y_r, ag_s, ag_r,
    xs_s, xr_s, zs_s, zr_s, zf_s, zf_r, fx_s, fx_r, loc,
):
    g = Group()
    own_rows, width = tokens_h.shape
    tokens = spread_buf
    hidden_units = rights.shape[2]
    rows = width // dp_size
    loads = [
        pltpu.make_async_copy(src, dst, load_sem.at[n])
        for n, (src, dst) in enumerate(
            [(w_gate_h, w_gate), (w_up_h, w_up), (w_down_h, w_down), (cot_h, lefts.at[0]), (tokens_h, tokens)]
        )
    ]
    for copy in loads:
        copy.start()
    meet(g, dp_size // 2)
    bufs = (sibsend, sibrecv, ysend, yrecv, total)
    sems = (sib_s, sib_r, y_s, y_r)

    def attn_part(r, n, w):
        return dot(attended[r], w_out[:, n : n + w])

    sums = RowSums(g, own_rows, 0, 64, attn_part, bufs, sems)
    normed = Spread(g, own_rows, 64, None, lefts.at[1], (ag_s, ag_r), 0)
    own_first = pl.multiple_of(g.t * own_rows, own_rows)

    def first_state(r, summed):
        state = tokens[r].astype(f32) + summed
        mid[r] = state
        normal, _ = norm_parts(state)
        start = pl.multiple_of(own_first + r.start, STRIP)
        lefts[1, pl.ds(start, STRIP)] = (normal * gain[...]).astype(bf16)

    sums.give(1, 0)

    def far(j):
        @pl.when(j + 1 < sums.count)
        def _():
            sums.give(1, j + 1)

        sums.send(j)

    loop(sums.count, far)

    def near(j):
        sums.give(0, j)
        sums.hold(j)

    loop(sums.count, near)

    def feed(y, c, half):
        r = pl.ds(pl.multiple_of((y * 2 + c) * own_rows + half * 128, 128), 128)
        for n, w in pieces(hidden_units, 512):
            gate = dot(lefts[1, r], w_gate[n : n + w], NT)
            up = dot(lefts[1, r], w_up[n : n + w], NT)
            back = dot(lefts[0, r], w_down[n : n + w], NT)
            sig = jax.nn.sigmoid(gate)
            active = gate * sig
            rights[0, r, n : n + w] = (active * up).astype(bf16)
            rights[1, r, n : n + w] = (back * up * sig * (1.0 + gate * (1.0 - sig))).astype(bf16)
            rights[2, r, n : n + w] = (back * active).astype(bf16)

    def close(j):
        sums.finish(j, first_state)
        normed.start(j)

    loads[4].wait()

    def half_near(half):
        loop(2, lambda a: close(half * 2 + a))

        @pl.when(half == 0)
        def _():
            for copy in loads[:4]:
                copy.wait()

        feed(g.y, g.c, half)
        loop(2, lambda a: normed.sib_in(half * 2 + a))
        feed(g.y, 1 - g.c, half)

    loop(2, half_near)

    def half_far(half):
        loop(2, lambda a: normed.relay(half * 2 + a))
        feed(1 - g.y, g.c, half)
        loop(2, lambda a: normed.far_in(half * 2 + a))
        feed(1 - g.y, 1 - g.c, half)

    loop(2, half_far)
    sums.drain()

    halves = max(1, rows // 128)
    rn = rows // halves
    engine = WeightSums(
        g, dp_size, rows, 3, 1, block_of(lefts, rights, lambda i: jnp.minimum(i, 1), rows, halves),
        (xs, zs, acc, xtmp, ztmp, xrecv, zrecv, zf, zfx, facc, frecv, fxrecv),
        (xs_s, xr_s, zs_s, zr_s, loc, zf_s, zf_r, fx_s, fx_r), turned(totals_h, turn, loc.at[2], halves, rn),
    )
    engine.begin()

    def back_part(r, n, w):
        return dot(rights[1, r], w_gate[:, n : n + w]) + dot(rights[2, r], w_up[:, n : n + w])

    sums = RowSums(g, own_rows, 1, 128, back_part, bufs, sems)
    states = Spread(g, own_rows, 128, spread_buf, state_all_h, (ag_s, ag_r), 1)
    gain_grad[...] = jnp.zeros_like(gain_grad)

    def state_back(r, grad):
        normal, scale = norm_parts(mid[r])
        weighted = grad * gain[...]
        start = pl.multiple_of(own_first + r.start, STRIP)
        change = scale * (weighted - normal * jnp.mean(weighted * normal, axis=-1, keepdims=True))
        state = lefts[0, pl.ds(start, STRIP)].astype(f32) + change
        gain_grad[...] += jnp.sum(grad * normal, axis=0, keepdims=True)
        total[r] = state
        spread_buf[r] = state.astype(bf16)

    def far_back(j):
        sums.give(1, j)
        sums.send(j)

    loop(sums.count, far_back)

    def near_back(j):
        sums.give(0, j)
        engine.service(2 * j)
        sums.hold(j)
        engine.service(2 * j + 1)

    loop(sums.count, near_back)
    used = 2 * sums.count

    def own_copy(j):
        r = pl.ds(pl.multiple_of(j * 128, 128), 128)
        to = pl.ds(pl.multiple_of(own_first + j * 128, 128), 128)
        return (
            pltpu.make_async_copy(total.at[r], state_grad_h.at[r], load_sem.at[0]),
            pltpu.make_async_copy(spread_buf.at[r], state_all_h.at[to], load_sem.at[1]),
        )

    def close_back(j):
        sums.finish(j, state_back)
        states.start(j)
        copies = own_copy(j)
        for copy in copies:
            copy.start()
        engine.service(used + j)
        for copy in copies:
            copy.wait()

    loop(sums.count, close_back)
    used = used + sums.count

    def pass_back(j):
        states.relay(j)
        engine.service(used + j)

    loop(sums.count, pass_back)
    used = used + sums.count

    def arrive(j):
        states.sib_in(j)
        states.far_in(j)

    loop(sums.count, arrive)
    sums.drain()

    def down_part(r, n, w):
        return dot(rights[0, r], w_down[:, n : n + w])

    sums = RowSums(g, own_rows, 2, 128, down_part, bufs, sems)

    def far_down(j):
        sums.give(1, j)
        engine.service(used + 2 * j)
        sums.send(j)
        engine.service(used + 2 * j + 1)

    loop(sums.count, far_down)
    used = used + 2 * sums.count

    def near_down(j):
        sums.give(0, j)
        sums.hold(j)
        engine.service(used + j)

    loop(sums.count, near_down)
    used = used + sums.count

    def last_state(r, summed):
        output[r] = (valid[r] * (mid[r] + summed)).astype(bf16)

    loop(sums.count, lambda j: sums.finish(j, last_state))
    loop(engine.services() - used, lambda n: engine.service(used + n))
    sums.drain()
    normed.drain()
    states.drain()
    engine.drain()


def mlp_call(attended, w_out, tokens, gain, valid, w_gate, w_up, w_down, cot_all, collective_id):
    dp_size = lax.axis_size("dp")
    nz = dp_size // 2
    own_rows, width = tokens.shape
    bucket = cot_all.shape[0]
    units = w_down.shape[0]
    rows = width // dp_size
    halves = max(1, rows // 128)
    rn = rows // halves
    jobs = 3 * halves - 1
    steps = jobs * nz
    vm, hbm = pl.BlockSpec(memory_space=pltpu.VMEM), pl.BlockSpec(memory_space=pl.ANY)
    dma = lambda *shape: pltpu.SemaphoreType.DMA(shape)
    vmem = lambda shape, kind=bf16: pltpu.VMEM(shape, kind)
    sds = jax.ShapeDtypeStruct
    outs = pl.pallas_call(
        functools.partial(mlp_kernel, dp_size),
        out_shape=[
            sds((own_rows, width), bf16),
            sds((own_rows, width), f32),
            sds((1, width), f32),
            sds((bucket, width), bf16),
            sds((3, units, rows), f32),
            sds((steps, rn, units), bf16),
            sds((jobs * (nz + 1), rn, units), bf16),
            sds((nz + 1, 2 * rn, units), bf16),
            sds((rn, units), bf16),
        ],
        in_specs=[vm] * 4 + [hbm] * 5,
        out_specs=[vm, hbm, vm] + [hbm] * 6,
        scratch_shapes=[
            vmem((units, width)), vmem((units, width)), vmem((units, width)),
            vmem((2, bucket, width)), vmem((3, bucket, units)), vmem((own_rows, width), f32),
            vmem((2, own_rows, width)), vmem((2, own_rows, width)), vmem((own_rows, width)), vmem((own_rows, width)),
            vmem((own_rows, width), f32), vmem((own_rows, width)),
            vmem((AHEAD, rn, units)), vmem((WeightSums.zs_slots(nz), rn, units)), vmem((nz - 1, 2 * rn, units)), vmem((rn, units)),
            vmem((2, rn, units), f32), vmem((2 * rn, units), f32), vmem((rn, units)), vmem((2 * rn, units)),
            vmem((512, rn), f32),
            dma(5), dma(3, 2, 4), dma(3, 2, 4), dma(3, 4), dma(3, 4), dma(2, 3, 4), dma(2, 3, 4),
            dma(AHEAD), dma(steps), dma(WeightSums.zs_slots(nz)), dma(jobs * (nz + 1)), dma(nz), dma(nz + 1), dma(1), dma(1), dma(3),
        ],
        compiler_params=pltpu.CompilerParams(
            collective_id=collective_id, has_side_effects=True, vmem_limit_bytes=62 << 20
        ),
        name="mlp",
    )(attended, w_out, gain, valid, tokens, w_gate, w_up, w_down, cot_all)
    return outs[:5]


def head_lanes(h, feat, width):
    return (lax.broadcasted_iota(jnp.int32, (1, width), 1) // feat == h).astype(f32).astype(bf16)


def back_kernel(
    dp_size,
    state_all, attended, w_out, numer, denom, key_valid, query, key, value, gain, small_in,
    normed_h, w_query_h, w_key_h, w_value_h, tokens_h, grad_state_h,
    small_out, input_grad_h, out_h, value_h, qk_h, xrecv_o, zrecv_o, xrecv_a, zrecv_a,
    normed, w_query, w_key, w_value, tokens, grad_state, grad_numer, grad_den, key_t, rights,
    gv_acc, gk_acc, gq_acc, sibsend, sibrecv, ysend, yrecv, total,
    xs_o, zs_o, acc_o, xtmp_o, ztmp_o, xs_a, zs_a, acc_a, xtmp_a, ztmp_a, turn, gain_acc, smalls, small_got, small_z,
    load_sem, sib_s, sib_r, y_s, y_r,
    xs_so, xr_so, zs_so, zr_so, loc_o, xs_sa, xr_sa, zs_sa, zr_sa, loc_a, sm_s, sm_r, smz_s, smz_r,
):
    g = Group()
    nz = dp_size // 2
    own_rows, width = tokens_h.shape
    bucket = state_all.shape[1]
    head_width = 128
    feat_width = query.shape[1]
    heads = attended.shape[2] // head_width
    feat = feat_width // heads
    rows = width // dp_size
    halves = max(1, rows // 128)
    rn = rows // halves
    scale = 1.0 / math.sqrt(feat)
    loads = [
        pltpu.make_async_copy(src, dst, load_sem.at[n])
        for n, (src, dst) in enumerate(
            [
                (normed_h, normed.at[0]), (w_query_h, w_query), (w_key_h, w_key), (w_value_h, w_value),
                (tokens_h, tokens), (grad_state_h, grad_state),
            ]
        )
    ]
    for copy in loads:
        copy.start()
    meet(g, nz, every=True)

    first = WeightSums(
        g, dp_size, rows, 1, 0, block_of(state_all, attended, lambda i: i, rows, halves),
        (xs_o, zs_o, acc_o, xtmp_o, ztmp_o, xrecv_o, zrecv_o),
        (xs_so, xr_so, zs_so, zr_so, loc_o), turned(out_h, turn, loc_o.at[2], halves, rn),
    )
    turn_qk = turned(qk_h, turn, loc_a.at[2], halves, rn)

    def emit_attn(i, h, take):
        values = heads * head_width
        copy = pltpu.make_async_copy(
            total.at[pl.ds(0, rn), pl.ds(0, values)], value_h.at[pl.ds(pl.multiple_of(h * rn, rn), rn)], loc_a.at[2]
        )
        total[:rn, :values] = take(0, values)
        copy.start()
        copy.wait()
        turn_qk(i, h, lambda n, w: take(values + n, w))

    second = WeightSums(
        g, dp_size, rows, 1, 0, block_of(normed, rights, lambda i: i, rows, halves),
        (xs_a, zs_a, acc_a, xtmp_a, ztmp_a, xrecv_a, zrecv_a),
        (xs_sa, xr_sa, zs_sa, zr_sa, loc_a), emit_attn,
    )
    first.begin()
    key_t[...] = key[...].astype(f32).T.astype(bf16)

    def spread_grad(b):
        r = pl.ds(pl.multiple_of(b * 128, 128), 128)
        grad = dot(state_all[0, r], w_out[...], NT).astype(bf16).astype(f32)
        lane = lax.broadcasted_iota(jnp.int32, (128, 128), 1)
        dens = jnp.zeros((128, 128), f32)
        for h in range(heads):
            cols = slice(h * head_width, (h + 1) * head_width)
            den = denom[r, h : h + 1]
            part = grad[:, cols]
            grad_numer[r, cols] = (part / den).astype(bf16)
            back = -jnp.sum(part * numer[r, cols], axis=1, keepdims=True) / (den * den)
            dens = jnp.where(lane == h, back, dens)
        grad_den[:, r] = dens.T[: grad_den.shape[0]]

    loop(bucket // 128, spread_grad)
    gk_acc[...] = jnp.zeros_like(gk_acc)
    gq_acc[...] = jnp.zeros_like(gq_acc)
    gv_acc[...] = jnp.zeros_like(gv_acc)
    tile = 256

    def head(h):
        lanes = head_lanes(h, feat, feat_width)
        cols = pl.ds(pl.multiple_of(h * head_width, head_width), head_width)
        sub = lax.broadcasted_iota(jnp.int32, (feat_width, 1), 0) // feat == h
        for qb in range(bucket // tile):
            q0, nk = qb * tile, (qb + 1) * tile
            q_own = query[q0:nk] * lanes
            kept = key_t[:, :nk] * sub.astype(f32).astype(bf16)
            scores = dot(key[:nk], q_own, NT) * scale
            below = lax.broadcasted_iota(jnp.int32, (nk, tile), 0) <= q0 + lax.broadcasted_iota(
                jnp.int32, (nk, tile), 1
            )
            mask = below.astype(f32) * key_valid[:nk]
            taylor = (1.0 + scores + 0.5 * scores * scores) * mask
            grads = grad_numer[q0:nk, cols]
            gv_acc[:nk, cols] += dot(taylor.astype(bf16), grads)
            back = dot(value[:nk, cols], grads, NT) + grad_den[pl.ds(h, 1), q0:nk]
            low = (back * mask * (1.0 + scores)).astype(bf16)
            gk_acc[:nk] += dot(low, q_own)
            gq_acc[:, q0:nk] += dot(kept, low)
        first.service(2 * h)
        first.service(2 * h + 1)

    loop(heads, head)
    used = 2 * heads
    values = heads * head_width
    rights[0, :, :values] = gv_acc[...].astype(bf16)
    rights[0, :, values:] = jnp.concatenate([gq_acc[...].T * scale, gk_acc[...] * scale], axis=1).astype(bf16)
    for copy in loads:
        copy.wait()
    second.begin()

    def part(r, n, w):
        out = dot(rights[0, r, :values], w_value[n : n + w], NT)
        out = out + dot(rights[0, r, values : values + feat_width], w_query[:, n : n + w])
        return out + dot(rights[0, r, values + feat_width :], w_key[:, n : n + w])

    sums = RowSums(g, own_rows, 0, 128, part, (sibsend, sibrecv, ysend, yrecv, total), (sib_s, sib_r, y_s, y_r))

    def far(j):
        sums.give(1, j)
        first.service(used + 2 * j)
        sums.send(j)
        first.service(used + 2 * j + 1)

    loop(sums.count, far)
    used = used + 2 * sums.count

    def near(j):
        sums.give(0, j)
        second.service(2 * j)
        sums.hold(j)
        second.service(2 * j + 1)

    loop(sums.count, near)
    gain_acc[...] = jnp.zeros_like(gain_acc)

    def last(r, grad):
        normal, inv = norm_parts(tokens[r].astype(f32))
        weighted = grad * gain[...]
        change = inv * (weighted - normal * jnp.mean(weighted * normal, axis=-1, keepdims=True))
        gain_acc[...] += jnp.sum(grad * normal, axis=0, keepdims=True)
        grad_state[r] += change

    def close(j):
        sums.finish(j, last)
        r = pl.ds(pl.multiple_of(j * sums.chunk, sums.chunk), sums.chunk)
        pltpu.make_async_copy(grad_state.at[r], input_grad_h.at[r], load_sem.at[0]).start()
        second.service(2 * sums.count + j)
        pltpu.make_async_copy(grad_state.at[r], input_grad_h.at[r], load_sem.at[0]).wait()

    loop(sums.count, close)
    done = 3 * sums.count

    smalls[0] = small_in[...]
    smalls[0, 0:1] = gain_acc[...]
    z, x = second.z, second.x
    peers = (g.sibling, g.across, second.partner)
    for n, device in enumerate(peers):
        copy = remote(smalls.at[n], small_got.at[n], sm_s.at[n], sm_r.at[n], device)
        copy.start()
        second.service(done + n)
        copy.wait()
        smalls[n + 1] = smalls[n] + small_got[n]
    done = done + len(peers)

    def zsmall(k):
        return remote(
            smalls.at[3], small_z.at[z], smz_s.at[k], smz_r.at[k], (lax.rem(z + 1 + k, nz) * 2 + x, g.t)
        )

    loop(nz - 1, lambda k: zsmall(k).start())
    loop(max(0, second.services() - done), lambda n: second.service(done + n))
    loop(max(0, first.services() - used), lambda n: first.service(used + n))
    small_z[z] = smalls[3]

    def zgot(k):
        remote(
            smalls.at[3], small_z.at[lax.rem(z - 1 - k + nz, nz)], smz_s.at[k], smz_r.at[k], g.sibling
        ).wait_recv()

    loop(nz - 1, zgot)
    small_out[...] = jnp.zeros_like(small_out)

    def zadd(k):
        small_out[...] += small_z[k]

    loop(nz, zadd)
    loop(nz - 1, lambda k: zsmall(k).wait_send())
    sums.drain()
    first.drain()
    second.drain()


def back_call(
    state_all, attended, w_out, numer, denom, key_valid, query, key, value, gain, small, normed,
    w_query, w_key, w_value, tokens, grad_state, collective_id,
):
    dp_size = lax.axis_size("dp")
    nz = dp_size // 2
    own_rows, width = tokens.shape
    bucket, values = attended.shape
    feat_width = query.shape[1]
    all_width = values + 2 * feat_width
    rows = width // dp_size
    halves = max(1, rows // 128)
    rn = rows // halves
    steps = halves * nz
    zslots = halves * (nz + 1)
    ahead = min(8, steps)
    ring = WeightSums.zs_slots(nz)
    vm, hbm = pl.BlockSpec(memory_space=pltpu.VMEM), pl.BlockSpec(memory_space=pl.ANY)
    dma = lambda *shape: pltpu.SemaphoreType.DMA(shape)
    vmem = lambda shape, kind=bf16: pltpu.VMEM(shape, kind)
    sds = jax.ShapeDtypeStruct

    def buffers(w):
        return [
            vmem((ahead, rn, w)), vmem((ring, rn, w)), vmem((2, rn, w), f32), vmem((rn, w)), vmem((rn, w)),
        ]

    def engine_sems():
        return [dma(ahead), dma(steps), dma(ring), dma(zslots), dma(3)]

    outs = pl.pallas_call(
        functools.partial(back_kernel, dp_size),
        out_shape=[
            sds((8, width), f32),
            sds((own_rows, width), f32),
            sds((1, values, rows), f32),
            sds((rows, values), f32),
            sds((1, 2 * feat_width, rows), f32),
            sds((steps, rn, values), bf16),
            sds((zslots, rn, values), bf16),
            sds((steps, rn, all_width), bf16),
            sds((zslots, rn, all_width), bf16),
        ],
        in_specs=[vm] * 11 + [hbm] * 6,
        out_specs=[vm] + [hbm] * 8,
        scratch_shapes=[
            vmem((1, bucket, width)), vmem((feat_width, width)), vmem((feat_width, width)), vmem((width, values)),
            vmem((own_rows, width)), vmem((own_rows, width), f32), vmem((bucket, values)), vmem((8, bucket), f32),
            vmem((feat_width, bucket)), vmem((1, bucket, all_width)),
            vmem((bucket, values), f32), vmem((bucket, feat_width), f32), vmem((feat_width, bucket), f32),
            vmem((2, own_rows, width)), vmem((2, own_rows, width)), vmem((own_rows, width)), vmem((own_rows, width)),
            vmem((own_rows, width), f32),
            *buffers(values), *buffers(all_width), vmem((512, rn), f32), vmem((1, width), f32),
            vmem((4, 8, width), f32), vmem((3, 8, width), f32), vmem((nz, 8, width), f32),
            dma(6), dma(1, 2, 4), dma(1, 2, 4), dma(1, 4), dma(1, 4),
            *engine_sems(), *engine_sems(), dma(3), dma(3), dma(nz), dma(nz),
        ],
        compiler_params=pltpu.CompilerParams(
            collective_id=collective_id, has_side_effects=True, vmem_limit_bytes=60 << 20
        ),
        name="attention_back",
    )(
        state_all[None], attended[None], w_out, numer, denom, key_valid, query, key, value, gain, small,
        normed, w_query, w_key, w_value, tokens, grad_state,
    )
    return outs[:5]


def per_device(
    tokens,
    gain_attn,
    gain_mlp,
    w_query,
    w_key,
    w_value,
    w_out,
    w_gate,
    w_up,
    w_down,
    cotangent,
    lengths,
):
    tok_rows = tokens.shape[0]
    groups = lax.axis_size("tensor")
    bucket = tok_rows * groups
    length = lengths[lax.axis_index("dp")]
    position = jnp.arange(bucket, dtype=jnp.int32)
    valid_rows = (position < length).astype(jnp.float32)
    own_rows = lax.axis_index("tensor") * tok_rows + jnp.arange(tok_rows, dtype=jnp.int32)
    own_valid = (own_rows < length).astype(jnp.float32)[:, None]
    head_count = w_query.shape[1] // FEAT
    head_width = w_value.shape[1] // head_count
    qk_scale = 1.0 / math.sqrt(FEAT)
    block_rows = min(512, bucket)
    float_single = jnp.float32
    bf16 = jnp.bfloat16
    x_full = tokens.astype(float_single)
    normed = (norm_parts(x_full)[0] * gain_attn).astype(bf16)
    normed_all = lax.all_gather(normed, "tensor", axis=0, tiled=True)
    query_rows = (
        jnp.dot(normed_all, w_query, preferred_element_type=float_single)
        .astype(bf16)
        .reshape(bucket, head_count, FEAT)
    )
    key_head_rows = (
        jnp.dot(normed_all, w_key, preferred_element_type=float_single)
        .astype(bf16)
        .reshape(bucket, head_count, FEAT)
    )
    value_heads = (
        jnp.dot(normed_all, w_value, preferred_element_type=float_single)
        .astype(bf16)
        .reshape(bucket, head_count, head_width)
    )

    def block_scores(first_row_index, last_row_index):
        scores = (
            jnp.einsum(
                "wra,tra->rwt",
                query_rows[first_row_index:last_row_index],
                key_head_rows[:last_row_index],
                preferred_element_type=float_single,
            )
            * qk_scale
        )
        key_mask = (
            (position[None, :last_row_index] <= position[first_row_index:last_row_index, None])
            & (position[None, :last_row_index] < length)
        ).astype(float_single)
        taylor = (1.0 + scores + 0.5 * scores * scores) * key_mask
        return (scores, key_mask, taylor)

    numer_parts = []
    denom_parts = []
    for first_row_index in range(0, bucket, block_rows):
        last_row_index = first_row_index + block_rows
        scores, key_mask, taylor = block_scores(first_row_index, last_row_index)
        numer_parts.append(
            jnp.einsum(
                "hqk,khv->qhv",
                taylor.astype(bf16),
                value_heads[:last_row_index],
                preferred_element_type=float_single,
            )
        )
        denom_parts.append(jnp.sum(taylor, axis=-1).T)
    numerator = jnp.concatenate(numer_parts, axis=0)
    denominator = jnp.concatenate(denom_parts, axis=0)
    attended = (
        (numerator / denominator[:, :, None]).reshape(bucket, head_count * head_width).astype(bf16)
    )
    den_part = jnp.sum(denominator * (valid_rows / (position + 1.0))[:, None])
    grad_out = cotangent.astype(float_single) * own_valid
    grad_mlp_all = lax.all_gather(grad_out.astype(bf16), "tensor", axis=0, tiled=True)
    output, grad_state, gain_mlp_part, grad_attn_all, mlp_totals = mlp_call(
        attended, w_out, tokens, gain_mlp[None], own_valid, w_gate.T, w_up.T, w_down, grad_mlp_all, 1
    )
    small = jnp.concatenate(
        [
            jnp.zeros_like(gain_mlp_part),
            gain_mlp_part,
            jnp.broadcast_to(den_part, (6, gain_mlp_part.shape[1])),
        ],
        axis=0,
    )
    key_valid = valid_rows[:, None]
    small_total, input_grad, out_total, value_total, qk_total = back_call(
        grad_attn_all,
        attended,
        w_out,
        numerator.reshape(bucket, head_count * head_width),
        denominator,
        key_valid,
        query_rows.reshape(bucket, head_count * FEAT),
        key_head_rows.reshape(bucket, head_count * FEAT),
        value_heads.reshape(bucket, head_count * head_width),
        gain_attn[None],
        small,
        normed_all,
        w_query.T,
        w_key.T,
        w_value,
        tokens,
        grad_state,
        2,
    )
    gain_attn_total, gain_mlp_total, den_total = small_total[0], small_total[1], small_total[2, 0]
    query_total = qk_total[0, : head_count * FEAT].T
    key_total = qk_total[0, head_count * FEAT :].T
    out_total = out_total[0]
    down_total, gate_total, up_total = mlp_totals[0], mlp_totals[1].T, mlp_totals[2].T
    den_mean = den_total / (head_count * groups * jnp.sum(lengths).astype(float_single))
    return (
        output,
        input_grad,
        gain_attn_total,
        gain_mlp_total,
        query_total,
        key_total,
        value_total,
        out_total,
        gate_total,
        up_total,
        down_total,
        den_mean,
    )


def solution(mesh):
    return jax.shard_map(
        per_device,
        mesh=mesh,
        in_specs=(
            P(("dp", "tensor"), None),
            P(),
            P(),
            P(None, "tensor"),
            P(None, "tensor"),
            P(None, "tensor"),
            P("tensor", None),
            P(None, "tensor"),
            P(None, "tensor"),
            P("tensor", None),
            P(("dp", "tensor"), None),
            P(),
        ),
        out_specs=(
            P(("dp", "tensor"), None),
            P(("dp", "tensor"), None),
            P(),
            P(),
            P("dp", "tensor"),
            P("dp", "tensor"),
            P("dp", "tensor"),
            P("tensor", "dp"),
            P("dp", "tensor"),
            P("dp", "tensor"),
            P("tensor", "dp"),
            P(),
        ),
        check_vma=False,
    )
```

```python
import functools
import math

import jax
import jax.numpy as jnp
from jax import lax
from jax.experimental import pallas as pl
from jax.experimental.pallas import tpu as pltpu
from jax.sharding import PartitionSpec as P

FEAT = 16
MESH = pl.DeviceIdType.MESH
f32 = jnp.float32
bf16 = jnp.bfloat16
NT = (((1,), (1,)), ((), ()))
TN = (((0,), (0,)), ((), ()))
AHEAD = 4
LAG = 2
SETTLE = 3
STRIP = 16


def dot(a, b, dims=(((1,), (0,)), ((), ()))):
    return lax.dot_general(a, b, dims, preferred_element_type=f32)


def loop(count, body):
    def step(i, carry):
        body(i)
        return carry

    lax.fori_loop(0, count, step, 0)


def pieces(width, size):
    return [(start, min(size, width - start)) for start in range(0, width, size)]


class Group:
    def __init__(self):
        self.dp = lax.axis_index("dp")
        self.t = lax.axis_index("tensor")
        self.y, self.c = self.t // 2, lax.rem(self.t, 2)
        self.sibling = (self.dp, self.y * 2 + 1 - self.c)
        self.across = (self.dp, (1 - self.y) * 2 + self.c)


def remote(src, dst, send, recv, device):
    return pltpu.make_async_remote_copy(src, dst, send, recv, device_id=device, device_id_type=MESH)


class RowSums:
    def __init__(self, g, own_rows, phase, chunk, part, bufs, sems):
        self.g, self.own, self.p, self.chunk, self.part = g, own_rows, phase, chunk, part
        self.sibsend, self.sibrecv, self.ysend, self.yrecv, self.total = bufs
        self.sib_s, self.sib_r, self.y_s, self.y_r = sems
        self.count = own_rows // chunk

    def at(self, j):
        return pl.ds(pl.multiple_of(j * self.chunk, self.chunk), self.chunk)

    def rows(self, y, c, j):
        return pl.ds(pl.multiple_of((y * 2 + c) * self.own + j * self.chunk, self.chunk), self.chunk)

    def sib(self, far, j):
        return remote(
            self.sibsend.at[far, self.at(j)], self.sibrecv.at[far, self.at(j)],
            self.sib_s.at[self.p, far, j], self.sib_r.at[self.p, far, j], self.g.sibling,
        )

    def ycopy(self, j):
        return remote(
            self.ysend.at[self.at(j)], self.yrecv.at[self.at(j)],
            self.y_s.at[self.p, j], self.y_r.at[self.p, j], self.g.across,
        )

    def give(self, far, j):
        y = 1 - self.g.y if far else self.g.y
        for n, w in pieces(self.total.shape[1], 512):
            self.sibsend[far, self.at(j), n : n + w] = self.part(self.rows(y, 1 - self.g.c, j), n, w).astype(bf16)
        self.sib(far, j).start()

    def send(self, j):
        g = self.g
        for n, w in pieces(self.total.shape[1], 512):
            self.total[self.at(j), n : n + w] = self.part(self.rows(1 - g.y, g.c, j), n, w)
        self.sib(1, j).wait_recv()
        self.ysend[self.at(j)] = (self.total[self.at(j)] + self.sibrecv[1, self.at(j)].astype(f32)).astype(bf16)
        self.ycopy(j).start()

    def hold(self, j):
        for n, w in pieces(self.total.shape[1], 512):
            self.total[self.at(j), n : n + w] = self.part(self.rows(self.g.y, self.g.c, j), n, w)

    def finish(self, j, use):
        self.sib(0, j).wait_recv()
        self.ycopy(j).wait_recv()

        def strip(i):
            r = pl.ds(pl.multiple_of(j * self.chunk + i * STRIP, STRIP), STRIP)
            use(r, self.total[r] + self.sibrecv[0, r].astype(f32) + self.yrecv[r].astype(f32))

        loop(self.chunk // STRIP, strip)

    def drain(self):
        def body(j):
            self.sib(0, j).wait_send()
            self.sib(1, j).wait_send()
            self.ycopy(j).wait_send()

        loop(self.count, body)


class Spread:
    def __init__(self, g, own_rows, chunk, src, full, sems, phase):
        self.g, self.own, self.chunk, self.src, self.full, self.p = g, own_rows, chunk, src, full, phase
        self.s, self.r = sems
        self.count = own_rows // chunk

    def rows(self, y, c, j):
        return pl.ds(pl.multiple_of((y * 2 + c) * self.own + j * self.chunk, self.chunk), self.chunk)

    def copy(self, kind, j):
        g = self.g
        rows = self.rows(g.y, g.c, j)
        if kind == 2:
            rows = self.rows(1 - g.y, g.c, j)
            src = self.full.at[rows]
        elif self.src is None:
            src = self.full.at[rows]
        else:
            src = self.src.at[pl.ds(pl.multiple_of(j * self.chunk, self.chunk), self.chunk)]
        return remote(
            src, self.full.at[rows], self.s.at[self.p, kind, j], self.r.at[self.p, kind, j],
            g.across if kind == 1 else g.sibling,
        )

    def start(self, j):
        self.copy(1, j).start()
        self.copy(0, j).start()

    def relay(self, j):
        self.copy(1, j).wait_recv()
        self.copy(2, j).start()

    def sib_in(self, j):
        self.copy(0, j).wait_recv()

    def far_in(self, j):
        self.copy(2, j).wait_recv()

    def drain(self):
        def body(j):
            for kind in range(3):
                self.copy(kind, j).wait_send()

        loop(self.count, body)


class WeightSums:
    def __init__(self, g, dp_size, rows, jobs, z_first, block, refs, sems, emit):
        self.g, self.rows, self.block, self.z_first, self.emit = g, rows, block, z_first, emit
        self.nz = dp_size // 2
        self.z, self.x = g.dp // 2, lax.rem(g.dp, 2)
        self.halves = max(1, rows // 128)
        self.rn = rows // self.halves
        self.ring = self.zs_slots(self.nz)
        self.jobs = jobs * self.halves - z_first
        self.steps = self.jobs * self.nz
        self.xs, self.zs, self.acc, self.xtmp, self.ztmp, self.xrecv, self.zrecv = refs[:7]
        self.xs_s, self.xr_s, self.zs_s, self.zr_s, self.loc = sems[:5]
        if z_first:
            self.zf, self.zfx, self.facc, self.frecv, self.fxrecv = refs[7:]
            self.zf_s, self.zf_r, self.fx_s, self.fx_r = sems[5:]
        self.ahead = self.xs.shape[0]
        self.partner = (self.z * 2 + 1 - self.x, g.t)

    @staticmethod
    def zs_slots(nz):
        return 2 * nz if nz <= 4 else nz

    def job(self, s):
        lin = s // self.nz + self.z_first
        return lin // self.halves, lax.rem(lin, self.halves)

    def order(self, k):
        last = self.nz - 1
        upper = self.z >= self.nz // 2
        z = jnp.where(upper, last - self.z, self.z)
        zt = jnp.where(k < last - z, last - k, jnp.where(k < last, last - 1 - k, z))
        return jnp.where(upper, last - zt, zt)

    def coming(self, zt):
        return jnp.where(zt > self.z, self.z > 0, self.z < self.nz - 1)

    def towards(self, zt):
        return (jnp.where(zt > self.z, self.z + 1, self.z - 1) * 2 + self.x, self.g.t)

    def slot(self, zt):
        return jnp.where(zt == self.z - 1, self.nz, zt)

    def xcopy(self, s):
        slot = lax.rem(s, self.ahead)
        return remote(self.xs.at[slot], self.xrecv.at[s], self.xs_s.at[slot], self.xr_s.at[s], self.partner)

    def zcopy(self, s, zt):
        ring = lax.rem(s, self.ring)
        j = s // self.nz * (self.nz + 1) + self.slot(zt)
        return remote(self.zs.at[ring], self.zrecv.at[j], self.zs_s.at[ring], self.zr_s.at[j], self.towards(zt))

    def zwait(self, j):
        remote(self.zs.at[0], self.zrecv.at[j], self.zs_s.at[0], self.zr_s.at[j], self.partner).wait_recv()

    def fetch(self, src, dst, k):
        copy = pltpu.make_async_copy(src, dst, self.loc.at[k])
        copy.start()
        return copy

    def xsend(self, s):
        @pl.when(s >= self.ahead)
        def _():
            self.xcopy(s - self.ahead).wait_send()

        i, h = self.job(s)
        self.xs[lax.rem(s, self.ahead)] = self.block(i, self.order(lax.rem(s, self.nz)), 1 - self.x, h).astype(bf16)
        self.xcopy(s).start()

    def xstep(self, s):
        k = lax.rem(s, self.nz)
        zt = self.order(k)
        i, h = self.job(s)
        self.xcopy(s).wait_recv()
        copy = self.fetch(self.xrecv.at[s], self.xtmp, 0)
        own = self.block(i, zt, self.x, h)
        slot = lax.rem(s // self.nz, 2)
        ring = lax.rem(s, self.ring)

        @pl.when((s >= self.ring) & (k < self.nz - 1))
        def _():
            self.zcopy(s - self.ring, zt).wait_send()

        self.acc[slot] = own
        copy.wait()
        total = self.acc[slot] + self.xtmp[...].astype(f32)

        @pl.when(k == self.nz - 1)
        def _():
            self.acc[slot] = total

        @pl.when(k < self.nz - 1)
        def _():
            self.zs[ring] = total.astype(bf16)

            @pl.when(jnp.logical_not(self.coming(zt)))
            def _():
                self.zcopy(s, zt).start()

    def zstep(self, s):
        k = lax.rem(s, self.nz)
        zt = self.order(k)
        ring = lax.rem(s, self.ring)

        @pl.when((k < self.nz - 1) & self.coming(zt))
        def _():
            j = s // self.nz * (self.nz + 1) + zt
            self.zwait(j)
            self.fetch(self.zrecv.at[j], self.ztmp.at[pl.ds(0, self.rn)], 1).wait()
            self.zs[ring] = (self.zs[ring].astype(f32) + self.ztmp[: self.rn].astype(f32)).astype(bf16)
            self.zcopy(s, zt).start()

    def final(self, jx):
        slot = lax.rem(jx, 2)

        def take(j):
            self.zwait(j)
            self.fetch(self.zrecv.at[j], self.ztmp.at[pl.ds(0, self.rn)], 1).wait()
            self.acc[slot] += self.ztmp[: self.rn].astype(f32)

        @pl.when(self.z > 0)
        def _():
            take(jx * (self.nz + 1) + self.z)

        @pl.when(self.z < self.nz - 1)
        def _():
            take(jx * (self.nz + 1) + self.nz)

        i, h = self.job(jx * self.nz)
        self.emit(i, h, lambda n, w: self.acc[slot, :, n : n + w])

    def fcopy(self, q, zt):
        slot = self.slot(zt)
        return remote(self.zf.at[q], self.frecv.at[slot], self.zf_s.at[q], self.zf_r.at[slot], self.towards(zt))

    def fwait(self, slot):
        remote(self.zf.at[0], self.frecv.at[slot], self.zf_s.at[0], self.zf_r.at[slot], self.partner).wait_recv()

    def fstart(self, q):
        zt = self.order(q)
        for xt in range(2):
            self.zf[q, xt * self.rn : (xt + 1) * self.rn] = self.block(0, zt, xt, 0).astype(bf16)

        @pl.when(jnp.logical_not(self.coming(zt)))
        def _():
            self.fcopy(q, zt).start()

    def fstep(self, q):
        zt = self.order(q)

        @pl.when(self.coming(zt))
        def _():
            self.fwait(zt)
            self.fetch(self.frecv.at[zt], self.ztmp, 1).wait()
            self.zf[q] = (self.zf[q].astype(f32) + self.ztmp[...].astype(f32)).astype(bf16)
            self.fcopy(q, zt).start()

    def fxcopy(self):
        return remote(self.zfx, self.fxrecv, self.fx_s.at[0], self.fx_r.at[0], self.partner)

    def fend(self):
        for xt in range(2):
            self.facc[xt * self.rn : (xt + 1) * self.rn] = self.block(0, self.z, xt, 0)

        def take(slot):
            self.fwait(slot)
            self.fetch(self.frecv.at[slot], self.ztmp, 1).wait()
            self.facc[...] += self.ztmp[...].astype(f32)

        @pl.when(self.z > 0)
        def _():
            take(self.z)

        @pl.when(self.z < self.nz - 1)
        def _():
            take(self.nz)

        away = pl.ds(pl.multiple_of((1 - self.x) * self.rn, self.rn), self.rn)
        self.zfx[...] = self.facc[away].astype(bf16)
        self.fxcopy().start()

    def ffinal(self):
        self.fxcopy().wait_recv()
        self.fetch(self.fxrecv, self.xtmp, 1).wait()
        own = pl.ds(pl.multiple_of(self.x * self.rn, self.rn), self.rn)
        self.facc[own] += self.xtmp[...].astype(f32)
        self.emit(0, 0, lambda n, w: self.facc[own, n : n + w])

    def begin(self):
        loop(self.ahead, self.xsend)
        if self.z_first:
            loop(self.nz - 1, self.fstart)

    def services(self):
        return max(self.steps + SETTLE + 1, self.z_first * (2 * self.nz + 5))

    def service(self, s):
        @pl.when(s < self.steps)
        def _():
            self.xstep(s)

        @pl.when(s + self.ahead < self.steps)
        def _():
            self.xsend(s + self.ahead)

        @pl.when((s >= LAG) & (s - LAG < self.steps))
        def _():
            self.zstep(s - LAG)

        if self.z_first:

            @pl.when((lax.rem(s, 2) == 1) & (s // 2 < self.nz - 1))
            def _():
                self.fstep(s // 2)

            @pl.when(s == 2 * self.nz - 1)
            def _():
                self.fend()

            @pl.when(s == 2 * self.nz + 4)
            def _():
                self.ffinal()

        @pl.when((s >= self.nz + SETTLE) & (lax.rem(s - SETTLE, self.nz) == 0) & (s - SETTLE <= self.steps))
        def _():
            self.final((s - SETTLE) // self.nz - 1)

    def drain(self):
        loop(self.ahead, lambda a: self.xcopy(self.steps - self.ahead + a).wait_send())

        def zdone(a):
            s = self.steps - self.ring + a
            k = lax.rem(s, self.nz)

            @pl.when(k < self.nz - 1)
            def _():
                self.zcopy(s, self.order(k)).wait_send()

        loop(self.ring, zdone)
        if self.z_first:
            loop(self.nz - 1, lambda q: self.fcopy(q, self.order(q)).wait_send())
            self.fxcopy().wait_send()


def meet(g, nz, every=False):
    if nz == 0:
        barrier = pltpu.get_barrier_semaphore()
        for device in (g.sibling, g.across):
            pl.semaphore_signal(barrier, inc=1, device_id=device, device_id_type=MESH)
        pl.semaphore_wait(barrier, 2)
        return
    z, x = g.dp // 2, lax.rem(g.dp, 2)
    barrier = pltpu.get_barrier_semaphore()

    def hello(device):
        pl.semaphore_signal(barrier, inc=1, device_id=device, device_id_type=MESH)

    hello(g.sibling)
    hello(g.across)
    hello((z * 2 + 1 - x, g.t))
    if every:
        loop(nz - 1, lambda k: hello((lax.rem(z + 1 + k, nz) * 2 + x, g.t)))
        pl.semaphore_wait(barrier, nz + 2)
        return

    @pl.when(z > 0)
    def _():
        hello(((z - 1) * 2 + x, g.t))

    @pl.when(z < nz - 1)
    def _():
        hello(((z + 1) * 2 + x, g.t))

    peers = 5 - jnp.where(z == 0, 1, 0) - jnp.where(z == nz - 1, 1, 0)
    pl.semaphore_wait(barrier, peers)


def turned(outs, turn, sem, halves, rn):
    def put(out, n, w, h):
        to = out.at[pl.ds(n, w)]
        if halves > 1:
            to = out.at[pl.ds(n, w), pl.ds(pl.multiple_of(h * rn, rn), rn)]
        copy = pltpu.make_async_copy(turn.at[pl.ds(0, w)], to, sem)
        copy.start()
        copy.wait()

    def emit(i, h, value):
        for n, w in pieces(outs[0].shape[0], 512):
            turn[:w] = value(n, w).T
            if len(outs) == 1:
                put(outs[0], n, w, h)
                continue
            for m, out in enumerate(outs):
                pl.when(i == m)(functools.partial(put, out, n, w, h))

    return emit


def block_of(lefts, rights, left_of, rows, halves):
    rn = rows // halves

    def block(i, zt, xt, h):
        li, right = left_of(i), rights.at[i]
        if rows % 128:
            cols = pl.ds(pl.multiple_of(zt * (2 * rows), 2 * rows), 2 * rows)
            both = dot(lefts[li, :, cols], right[...], TN)
            return jnp.where(xt == 0, both[:rows], both[rows:])
        cols = pl.ds(pl.multiple_of((zt * 2 + xt) * rows + h * rn, rn), rn)
        return dot(lefts[li, :, cols], right[...], TN)

    return block


def norm_parts(state):
    scale = lax.rsqrt(jnp.mean(state * state, axis=-1, keepdims=True) + 1e-06)
    return state * scale, scale


def mlp_kernel(
    dp_size,
    attended, w_out, gain, length, tokens_h, w_gate_h, w_up_h, w_down_h, cot_h,
    output, state_grad_h, gain_grad, state_all_h, down_h, gate_h, up_h, xrecv, zrecv, frecv, fxrecv,
    w_gate, w_up, w_down, lefts, rights, mid, sibsend, sibrecv, ysend, yrecv, total, spread_buf,
    xs, zs, zf, zfx, acc, facc, xtmp, ztmp, turn,
    load_sem, sib_s, sib_r, y_s, y_r, ag_s, ag_r,
    xs_s, xr_s, zs_s, zr_s, zf_s, zf_r, fx_s, fx_r, loc,
):
    g = Group()
    own_rows, width = tokens_h.shape
    tokens = spread_buf
    hidden_units = rights.shape[2]
    rows = width // dp_size
    loads = [
        pltpu.make_async_copy(src, dst, load_sem.at[n])
        for n, (src, dst) in enumerate(
            [(w_gate_h, w_gate), (w_up_h, w_up), (w_down_h, w_down), (cot_h, lefts.at[0]), (tokens_h, tokens)]
        )
    ]
    for copy in loads:
        copy.start()
    meet(g, dp_size // 2)
    bufs = (sibsend, sibrecv, ysend, yrecv, total)
    sems = (sib_s, sib_r, y_s, y_r)

    def attn_part(r, n, w):
        return dot(attended[r], w_out[:, n : n + w])

    sums = RowSums(g, own_rows, 0, 64, attn_part, bufs, sems)
    normed = Spread(g, own_rows, 64, None, lefts.at[1], (ag_s, ag_r), 0)
    own_first = pl.multiple_of(g.t * own_rows, own_rows)

    def first_state(r, summed):
        state = tokens[r].astype(f32) + summed
        mid[r] = state
        normal, _ = norm_parts(state)
        start = pl.multiple_of(own_first + r.start, STRIP)
        lefts[1, pl.ds(start, STRIP)] = (normal * gain[...]).astype(bf16)

    sums.give(1, 0)

    def far(j):
        @pl.when(j + 1 < sums.count)
        def _():
            sums.give(1, j + 1)

        sums.send(j)

    loop(sums.count, far)

    def near(j):
        sums.give(0, j)
        sums.hold(j)

    loop(sums.count, near)

    def feed(y, c, half):
        r = pl.ds(pl.multiple_of((y * 2 + c) * own_rows + half * 128, 128), 128)
        for n, w in pieces(hidden_units, 512):
            gate = dot(lefts[1, r], w_gate[n : n + w], NT)
            up = dot(lefts[1, r], w_up[n : n + w], NT)
            back = dot(lefts[0, r], w_down[n : n + w], NT)
            sig = jax.nn.sigmoid(gate)
            active = gate * sig
            rights[0, r, n : n + w] = (active * up).astype(bf16)
            rights[1, r, n : n + w] = (back * up * sig * (1.0 + gate * (1.0 - sig))).astype(bf16)
            rights[2, r, n : n + w] = (back * active).astype(bf16)

    def close(j):
        sums.finish(j, first_state)
        normed.start(j)

    loads[4].wait()

    def half_near(half):
        loop(2, lambda a: close(half * 2 + a))

        @pl.when(half == 0)
        def _():
            for copy in loads[:4]:
                copy.wait()

        feed(g.y, g.c, half)
        loop(2, lambda a: normed.sib_in(half * 2 + a))
        feed(g.y, 1 - g.c, half)

    loop(2, half_near)

    def half_far(half):
        loop(2, lambda a: normed.relay(half * 2 + a))
        feed(1 - g.y, g.c, half)
        loop(2, lambda a: normed.far_in(half * 2 + a))
        feed(1 - g.y, 1 - g.c, half)

    loop(2, half_far)
    sums.drain()

    halves = max(1, rows // 128)
    rn = rows // halves
    engine = WeightSums(
        g, dp_size, rows, 3, 1, block_of(lefts, rights, lambda i: jnp.minimum(i, 1), rows, halves),
        (xs, zs, acc, xtmp, ztmp, xrecv, zrecv, zf, zfx, facc, frecv, fxrecv),
        (xs_s, xr_s, zs_s, zr_s, loc, zf_s, zf_r, fx_s, fx_r), turned((down_h, gate_h, up_h), turn, loc.at[2], halves, rn),
    )
    engine.begin()

    def back_part(r, n, w):
        return dot(rights[1, r], w_gate[:, n : n + w]) + dot(rights[2, r], w_up[:, n : n + w])

    sums = RowSums(g, own_rows, 1, 128, back_part, bufs, sems)
    states = Spread(g, own_rows, 128, spread_buf, state_all_h, (ag_s, ag_r), 1)
    gain_grad[...] = jnp.zeros_like(gain_grad)

    def state_back(r, grad):
        normal, scale = norm_parts(mid[r])
        weighted = grad * gain[...]
        start = pl.multiple_of(own_first + r.start, STRIP)
        change = scale * (weighted - normal * jnp.mean(weighted * normal, axis=-1, keepdims=True))
        state = lefts[0, pl.ds(start, STRIP)].astype(f32) + change
        gain_grad[...] += jnp.sum(grad * normal, axis=0, keepdims=True)
        total[r] = state
        spread_buf[r] = state.astype(bf16)

    def far_back(j):
        sums.give(1, j)
        sums.send(j)

    loop(sums.count, far_back)

    def near_back(j):
        sums.give(0, j)
        engine.service(2 * j)
        sums.hold(j)
        engine.service(2 * j + 1)

    loop(sums.count, near_back)
    used = 2 * sums.count

    def own_copy(j):
        r = pl.ds(pl.multiple_of(j * 128, 128), 128)
        to = pl.ds(pl.multiple_of(own_first + j * 128, 128), 128)
        return (
            pltpu.make_async_copy(total.at[r], state_grad_h.at[r], load_sem.at[0]),
            pltpu.make_async_copy(spread_buf.at[r], state_all_h.at[to], load_sem.at[1]),
        )

    def close_back(j):
        sums.finish(j, state_back)
        states.start(j)
        copies = own_copy(j)
        for copy in copies:
            copy.start()
        engine.service(used + j)
        for copy in copies:
            copy.wait()

    loop(sums.count, close_back)
    used = used + sums.count

    def pass_back(j):
        states.relay(j)
        engine.service(used + j)

    loop(sums.count, pass_back)
    used = used + sums.count

    def arrive(j):
        states.sib_in(j)
        states.far_in(j)

    loop(sums.count, arrive)
    sums.drain()

    def down_part(r, n, w):
        return dot(rights[0, r], w_down[:, n : n + w])

    sums = RowSums(g, own_rows, 2, 128, down_part, bufs, sems)

    def far_down(j):
        sums.give(1, j)
        engine.service(used + 2 * j)
        sums.send(j)
        engine.service(used + 2 * j + 1)

    loop(sums.count, far_down)
    used = used + 2 * sums.count

    def near_down(j):
        sums.give(0, j)
        sums.hold(j)
        engine.service(used + j)

    loop(sums.count, near_down)
    used = used + sums.count

    def last_state(r, summed):
        position = own_first + r.start + lax.broadcasted_iota(jnp.int32, (STRIP, 1), 0)
        valid = (position < length[...]).astype(f32)
        output[r] = (valid * (mid[r] + summed)).astype(bf16)

    loop(sums.count, lambda j: sums.finish(j, last_state))
    loop(engine.services() - used, lambda n: engine.service(used + n))
    sums.drain()
    normed.drain()
    states.drain()
    engine.drain()


def mlp_call(attended, w_out, tokens, gain, length, w_gate, w_up, w_down, cot_all, collective_id):
    dp_size = lax.axis_size("dp")
    nz = dp_size // 2
    own_rows, width = tokens.shape
    bucket = cot_all.shape[0]
    units = w_down.shape[0]
    rows = width // dp_size
    halves = max(1, rows // 128)
    rn = rows // halves
    jobs = 3 * halves - 1
    steps = jobs * nz
    vm, hbm = pl.BlockSpec(memory_space=pltpu.VMEM), pl.BlockSpec(memory_space=pl.ANY)
    dma = lambda *shape: pltpu.SemaphoreType.DMA(shape)
    vmem = lambda shape, kind=bf16: pltpu.VMEM(shape, kind)
    sds = jax.ShapeDtypeStruct
    outs = pl.pallas_call(
        functools.partial(mlp_kernel, dp_size),
        out_shape=[
            sds((own_rows, width), bf16),
            sds((own_rows, width), f32),
            sds((1, width), f32),
            sds((bucket, width), bf16),
            *[sds((units, rows), f32)] * 3,
            sds((steps, rn, units), bf16),
            sds((jobs * (nz + 1), rn, units), bf16),
            sds((nz + 1, 2 * rn, units), bf16),
            sds((rn, units), bf16),
        ],
        in_specs=[vm] * 4 + [hbm] * 5,
        out_specs=[vm, hbm, vm] + [hbm] * 8,
        scratch_shapes=[
            vmem((units, width)), vmem((units, width)), vmem((units, width)),
            vmem((2, bucket, width)), vmem((3, bucket, units)), vmem((own_rows, width), f32),
            vmem((2, own_rows, width)), vmem((2, own_rows, width)), vmem((own_rows, width)), vmem((own_rows, width)),
            vmem((own_rows, width), f32), vmem((own_rows, width)),
            vmem((AHEAD, rn, units)), vmem((WeightSums.zs_slots(nz), rn, units)), vmem((nz - 1, 2 * rn, units)), vmem((rn, units)),
            vmem((2, rn, units), f32), vmem((2 * rn, units), f32), vmem((rn, units)), vmem((2 * rn, units)),
            vmem((512, rn), f32),
            dma(5), dma(3, 2, 4), dma(3, 2, 4), dma(3, 4), dma(3, 4), dma(2, 3, 4), dma(2, 3, 4),
            dma(AHEAD), dma(steps), dma(WeightSums.zs_slots(nz)), dma(jobs * (nz + 1)), dma(nz), dma(nz + 1), dma(1), dma(1), dma(3),
        ],
        compiler_params=pltpu.CompilerParams(
            collective_id=collective_id, has_side_effects=True, vmem_limit_bytes=62 << 20
        ),
        name="mlp",
    )(attended, w_out, gain, length, tokens, w_gate, w_up, w_down, cot_all)
    return outs[:7]


def head_lanes(h, feat, width):
    return (lax.broadcasted_iota(jnp.int32, (1, width), 1) // feat == h).astype(f32).astype(bf16)


def back_kernel(
    dp_size,
    state_all, attended, w_out, numer, denom, length, query, key, value, gain, mlp_gain, den_row,
    normed_h, w_query_h, w_key_h, w_value_h, tokens_h, grad_state_h,
    small_out, input_grad_h, out_h, value_h, qk_h, xrecv_o, zrecv_o, xrecv_a, zrecv_a,
    normed, w_query, w_key, w_value, tokens, grad_state, grad_numer, grad_den, key_t, rights,
    gv_acc, gk_acc, gq_acc, sibsend, sibrecv, ysend, yrecv, total,
    xs_o, zs_o, acc_o, xtmp_o, ztmp_o, xs_a, zs_a, acc_a, xtmp_a, ztmp_a, turn, gain_acc, smalls, small_got, small_z,
    load_sem, sib_s, sib_r, y_s, y_r,
    xs_so, xr_so, zs_so, zr_so, loc_o, xs_sa, xr_sa, zs_sa, zr_sa, loc_a, sm_s, sm_r, smz_s, smz_r,
):
    g = Group()
    nz = dp_size // 2
    own_rows, width = tokens_h.shape
    bucket = state_all.shape[1]
    head_width = 128
    feat_width = query.shape[1]
    heads = attended.shape[2] // head_width
    feat = feat_width // heads
    rows = width // dp_size
    halves = max(1, rows // 128)
    rn = rows // halves
    scale = 1.0 / math.sqrt(feat)
    loads = [
        pltpu.make_async_copy(src, dst, load_sem.at[n])
        for n, (src, dst) in enumerate(
            [
                (normed_h, normed.at[0]), (w_query_h, w_query), (w_key_h, w_key), (w_value_h, w_value),
                (tokens_h, tokens), (grad_state_h, grad_state),
            ]
        )
    ]
    for copy in loads:
        copy.start()
    meet(g, nz, every=True)

    first = WeightSums(
        g, dp_size, rows, 1, 0, block_of(state_all, attended, lambda i: i, rows, halves),
        (xs_o, zs_o, acc_o, xtmp_o, ztmp_o, xrecv_o, zrecv_o),
        (xs_so, xr_so, zs_so, zr_so, loc_o), turned((out_h,), turn, loc_o.at[2], halves, rn),
    )
    turn_qk = turned((qk_h,), turn, loc_a.at[2], halves, rn)

    def emit_attn(i, h, take):
        values = heads * head_width
        copy = pltpu.make_async_copy(
            total.at[pl.ds(0, rn), pl.ds(0, values)], value_h.at[pl.ds(pl.multiple_of(h * rn, rn), rn)], loc_a.at[2]
        )
        total[:rn, :values] = take(0, values)
        copy.start()
        copy.wait()
        turn_qk(i, h, lambda n, w: take(values + n, w))

    second = WeightSums(
        g, dp_size, rows, 1, 0, block_of(normed, rights, lambda i: i, rows, halves),
        (xs_a, zs_a, acc_a, xtmp_a, ztmp_a, xrecv_a, zrecv_a),
        (xs_sa, xr_sa, zs_sa, zr_sa, loc_a), emit_attn,
    )
    first.begin()
    key_t[...] = key[...].astype(f32).T.astype(bf16)

    def spread_grad(b):
        r = pl.ds(pl.multiple_of(b * 128, 128), 128)
        grad = dot(state_all[0, r], w_out[...], NT).astype(bf16).astype(f32)
        lane = lax.broadcasted_iota(jnp.int32, (128, 128), 1)
        dens = jnp.zeros((128, 128), f32)
        for h in range(heads):
            cols = slice(h * head_width, (h + 1) * head_width)
            den = denom[r, h : h + 1]
            part = grad[:, cols]
            grad_numer[r, cols] = (part / den).astype(bf16)
            back = -jnp.sum(part * numer[r, cols], axis=1, keepdims=True) / (den * den)
            dens = jnp.where(lane == h, back, dens)
        grad_den[:, r] = dens.T[: grad_den.shape[0]]

    loop(bucket // 128, spread_grad)
    gk_acc[...] = jnp.zeros_like(gk_acc)
    gq_acc[...] = jnp.zeros_like(gq_acc)
    gv_acc[...] = jnp.zeros_like(gv_acc)
    tile = 256

    def head(h):
        lanes = head_lanes(h, feat, feat_width)
        cols = pl.ds(pl.multiple_of(h * head_width, head_width), head_width)
        sub = lax.broadcasted_iota(jnp.int32, (feat_width, 1), 0) // feat == h
        for qb in range(bucket // tile):
            q0, nk = qb * tile, (qb + 1) * tile
            q_own = query[q0:nk] * lanes
            kept = key_t[:, :nk] * sub.astype(f32).astype(bf16)
            scores = dot(key[:nk], q_own, NT) * scale
            below = lax.broadcasted_iota(jnp.int32, (nk, tile), 0) <= q0 + lax.broadcasted_iota(
                jnp.int32, (nk, tile), 1
            )
            real = lax.broadcasted_iota(jnp.int32, (nk, 1), 0) < length[...]
            mask = below.astype(f32) * real.astype(f32)
            taylor = (1.0 + scores + 0.5 * scores * scores) * mask
            grads = grad_numer[q0:nk, cols]
            gv_acc[:nk, cols] += dot(taylor.astype(bf16), grads)
            back = dot(value[:nk, cols], grads, NT) + grad_den[pl.ds(h, 1), q0:nk]
            low = (back * mask * (1.0 + scores)).astype(bf16)
            gk_acc[:nk] += dot(low, q_own)
            gq_acc[:, q0:nk] += dot(kept, low)
        first.service(2 * h)
        first.service(2 * h + 1)

    loop(heads, head)
    used = 2 * heads
    values = heads * head_width
    rights[0, :, :values] = gv_acc[...].astype(bf16)
    rights[0, :, values:] = jnp.concatenate([gq_acc[...].T * scale, gk_acc[...] * scale], axis=1).astype(bf16)
    for copy in loads:
        copy.wait()
    second.begin()

    def part(r, n, w):
        out = dot(rights[0, r, :values], w_value[n : n + w], NT)
        out = out + dot(rights[0, r, values : values + feat_width], w_query[:, n : n + w])
        return out + dot(rights[0, r, values + feat_width :], w_key[:, n : n + w])

    sums = RowSums(g, own_rows, 0, 128, part, (sibsend, sibrecv, ysend, yrecv, total), (sib_s, sib_r, y_s, y_r))

    def far(j):
        sums.give(1, j)
        first.service(used + 2 * j)
        sums.send(j)
        first.service(used + 2 * j + 1)

    loop(sums.count, far)
    used = used + 2 * sums.count

    def near(j):
        sums.give(0, j)
        second.service(2 * j)
        sums.hold(j)
        second.service(2 * j + 1)

    loop(sums.count, near)
    gain_acc[...] = jnp.zeros_like(gain_acc)

    def last(r, grad):
        normal, inv = norm_parts(tokens[r].astype(f32))
        weighted = grad * gain[...]
        change = inv * (weighted - normal * jnp.mean(weighted * normal, axis=-1, keepdims=True))
        gain_acc[...] += jnp.sum(grad * normal, axis=0, keepdims=True)
        grad_state[r] += change

    def close(j):
        sums.finish(j, last)
        r = pl.ds(pl.multiple_of(j * sums.chunk, sums.chunk), sums.chunk)
        pltpu.make_async_copy(grad_state.at[r], input_grad_h.at[r], load_sem.at[0]).start()
        second.service(2 * sums.count + j)
        pltpu.make_async_copy(grad_state.at[r], input_grad_h.at[r], load_sem.at[0]).wait()

    loop(sums.count, close)
    done = 3 * sums.count

    smalls[0] = jnp.zeros(smalls.shape[1:], f32)
    smalls[0, 0:1] = gain_acc[...]
    smalls[0, 1:2] = mlp_gain[...]
    smalls[0, 2:3, : den_row.shape[1]] = den_row[...]
    z, x = second.z, second.x
    peers = (g.sibling, g.across, second.partner)
    for n, device in enumerate(peers):
        copy = remote(smalls.at[n], small_got.at[n], sm_s.at[n], sm_r.at[n], device)
        copy.start()
        second.service(done + n)
        copy.wait()
        smalls[n + 1] = smalls[n] + small_got[n]
    done = done + len(peers)

    def zsmall(k):
        return remote(
            smalls.at[3], small_z.at[z], smz_s.at[k], smz_r.at[k], (lax.rem(z + 1 + k, nz) * 2 + x, g.t)
        )

    loop(nz - 1, lambda k: zsmall(k).start())
    loop(max(0, second.services() - done), lambda n: second.service(done + n))
    loop(max(0, first.services() - used), lambda n: first.service(used + n))
    small_z[z] = smalls[3]

    def zgot(k):
        remote(
            smalls.at[3], small_z.at[lax.rem(z - 1 - k + nz, nz)], smz_s.at[k], smz_r.at[k], g.sibling
        ).wait_recv()

    loop(nz - 1, zgot)
    small_out[...] = jnp.zeros_like(small_out)

    def zadd(k):
        small_out[...] += small_z[k]

    loop(nz, zadd)
    loop(nz - 1, lambda k: zsmall(k).wait_send())
    sums.drain()
    first.drain()
    second.drain()


def back_call(
    state_all, attended, w_out, numer, denom, length, query, key, value, gain, mlp_gain, den_row, normed,
    w_query, w_key, w_value, tokens, grad_state, collective_id,
):
    dp_size = lax.axis_size("dp")
    nz = dp_size // 2
    own_rows, width = tokens.shape
    bucket, values = attended.shape
    feat_width = query.shape[1]
    all_width = values + 2 * feat_width
    rows = width // dp_size
    halves = max(1, rows // 128)
    rn = rows // halves
    steps = halves * nz
    zslots = halves * (nz + 1)
    ahead = min(8, steps)
    ring = WeightSums.zs_slots(nz)
    vm, hbm = pl.BlockSpec(memory_space=pltpu.VMEM), pl.BlockSpec(memory_space=pl.ANY)
    dma = lambda *shape: pltpu.SemaphoreType.DMA(shape)
    vmem = lambda shape, kind=bf16: pltpu.VMEM(shape, kind)
    sds = jax.ShapeDtypeStruct

    def buffers(w):
        return [
            vmem((ahead, rn, w)), vmem((ring, rn, w)), vmem((2, rn, w), f32), vmem((rn, w)), vmem((rn, w)),
        ]

    def engine_sems():
        return [dma(ahead), dma(steps), dma(ring), dma(zslots), dma(3)]

    outs = pl.pallas_call(
        functools.partial(back_kernel, dp_size),
        out_shape=[
            sds((8, width), f32),
            sds((own_rows, width), f32),
            sds((values, rows), f32),
            sds((rows, values), f32),
            sds((2 * feat_width, rows), f32),
            sds((steps, rn, values), bf16),
            sds((zslots, rn, values), bf16),
            sds((steps, rn, all_width), bf16),
            sds((zslots, rn, all_width), bf16),
        ],
        in_specs=[vm] * 12 + [hbm] * 6,
        out_specs=[vm] + [hbm] * 8,
        scratch_shapes=[
            vmem((1, bucket, width)), vmem((feat_width, width)), vmem((feat_width, width)), vmem((width, values)),
            vmem((own_rows, width)), vmem((own_rows, width), f32), vmem((bucket, values)), vmem((8, bucket), f32),
            vmem((feat_width, bucket)), vmem((1, bucket, all_width)),
            vmem((bucket, values), f32), vmem((bucket, feat_width), f32), vmem((feat_width, bucket), f32),
            vmem((2, own_rows, width)), vmem((2, own_rows, width)), vmem((own_rows, width)), vmem((own_rows, width)),
            vmem((own_rows, width), f32),
            *buffers(values), *buffers(all_width), vmem((512, rn), f32), vmem((1, width), f32),
            vmem((4, 8, width), f32), vmem((3, 8, width), f32), vmem((nz, 8, width), f32),
            dma(6), dma(1, 2, 4), dma(1, 2, 4), dma(1, 4), dma(1, 4),
            *engine_sems(), *engine_sems(), dma(3), dma(3), dma(nz), dma(nz),
        ],
        compiler_params=pltpu.CompilerParams(
            collective_id=collective_id, has_side_effects=True, vmem_limit_bytes=60 << 20
        ),
        name="attention_back",
    )(
        state_all[None], attended[None], w_out, numer, denom, length, query, key, value, gain, mlp_gain, den_row,
        normed, w_query, w_key, w_value, tokens, grad_state,
    )
    return outs[:5]


def front_kernel(
    tokens, cotangent, gain, length, w_query, w_key, w_value,
    query, key, value, numer, attended, denom, den_row, normed_h, cot_h,
    normed, cot_own, load_sem, ag_s, ag_r,
):
    g = Group()
    own_rows = tokens.shape[0]
    bucket = normed.shape[0]
    feat_width = query.shape[1]
    head_width = 128
    heads = value.shape[1] // head_width
    feat = feat_width // heads
    scale = 1.0 / math.sqrt(feat)
    own_first = pl.multiple_of(g.t * own_rows, own_rows)
    meet(g, 0)
    rows_out = Spread(g, own_rows, 64, None, normed, (ag_s, ag_r), 0)
    cots = Spread(g, own_rows, 64, cot_own, cot_h, (ag_s, ag_r), 1)

    def first_norm(j):
        for a in range(64 // STRIP):
            r = pl.ds(pl.multiple_of(j * 64 + a * STRIP, STRIP), STRIP)
            to = pl.ds(pl.multiple_of(own_first + j * 64 + a * STRIP, STRIP), STRIP)
            normal, _ = norm_parts(tokens[r].astype(f32))
            normed[to] = (normal * gain[...]).astype(bf16)
        rows_out.start(j)

    loop(rows_out.count, first_norm)
    position = own_first + lax.broadcasted_iota(jnp.int32, (own_rows, 1), 0)
    real_rows = (position < length[...]).astype(f32)
    cot_own[...] = (cotangent[...].astype(f32) * real_rows).astype(bf16)
    own_cot = pltpu.make_async_copy(cot_own, cot_h.at[pl.ds(own_first, own_rows)], load_sem.at[0])
    own_cot.start()

    def project(y, c, half):
        r = pl.ds(pl.multiple_of((y * 2 + c) * own_rows + half * 128, 128), 128)
        value[r] = dot(normed[r], w_value[...]).astype(bf16)
        query[r] = dot(normed[r], w_query[...], NT).astype(bf16)
        key[r] = dot(normed[r], w_key[...], NT).astype(bf16)

    def near(half):
        project(g.y, g.c, half)
        loop(2, lambda a: rows_out.sib_in(half * 2 + a))
        project(g.y, 1 - g.c, half)

    loop(2, near)

    def far(half):
        loop(2, lambda a: rows_out.relay(half * 2 + a))
        project(1 - g.y, g.c, half)
        loop(2, lambda a: rows_out.far_in(half * 2 + a))
        project(1 - g.y, 1 - g.c, half)

    loop(1, far)
    loop(2, lambda a: rows_out.relay(2 + a))
    loop(cots.count, cots.start)
    project(1 - g.y, g.c, 1)
    loop(2, lambda a: rows_out.far_in(2 + a))
    project(1 - g.y, 1 - g.c, 1)
    keep = pltpu.make_async_copy(normed, normed_h, load_sem.at[1])
    keep.start()
    denom[...] = jnp.zeros_like(denom)
    tile = 256

    def head(h):
        lanes = head_lanes(h, feat, feat_width)
        cols = pl.ds(pl.multiple_of(h * head_width, head_width), head_width)
        for qb in range(bucket // tile):
            q0, nk = qb * tile, (qb + 1) * tile
            scores = dot(query[q0:nk] * lanes, key[:nk], NT) * scale
            spot = lax.broadcasted_iota(jnp.int32, (tile, nk), 1)
            below = spot <= q0 + lax.broadcasted_iota(jnp.int32, (tile, nk), 0)
            real = lax.broadcasted_iota(jnp.int32, (1, nk), 1) < length[...]
            taylor = (1.0 + scores + 0.5 * scores * scores) * (below.astype(f32) * real.astype(f32))
            den = jnp.sum(taylor, axis=1, keepdims=True)
            top = dot(taylor.astype(bf16), value[:nk, cols])
            numer[q0:nk, cols] = top
            attended[q0:nk, cols] = (top / den).astype(bf16)
            lane = lax.broadcasted_iota(jnp.int32, (tile, denom.shape[1]), 1)
            denom[q0:nk] = jnp.where(lane == h, den, denom[q0:nk])

    for h in range(heads):
        head(h)
        if h < cots.count:
            cots.relay(h)
    for h in range(heads, cots.count):
        cots.relay(h)
    place = lax.broadcasted_iota(jnp.int32, (bucket, 1), 0)
    weight = (place < length[...]).astype(f32) / (place.astype(f32) + 1.0)
    den_row[...] = jnp.sum(denom[...] * weight, axis=0, keepdims=True)

    def arrive(j):
        cots.sib_in(j)
        cots.far_in(j)

    loop(cots.count, arrive)
    own_cot.wait()
    keep.wait()
    rows_out.drain()
    cots.drain()


def front_call(tokens, cotangent, gain, length, w_query, w_key, w_value, collective_id):
    own_rows, width = tokens.shape
    bucket = own_rows * lax.axis_size("tensor")
    feat_width, values = w_query.shape[0], w_value.shape[1]
    vm, hbm = pl.BlockSpec(memory_space=pltpu.VMEM), pl.BlockSpec(memory_space=pl.ANY)
    dma = lambda *shape: pltpu.SemaphoreType.DMA(shape)
    sds = jax.ShapeDtypeStruct
    return pl.pallas_call(
        front_kernel,
        out_shape=[
            sds((bucket, feat_width), bf16), sds((bucket, feat_width), bf16), sds((bucket, values), bf16),
            sds((bucket, values), f32), sds((bucket, values), bf16), sds((bucket, 128), f32), sds((1, 128), f32),
            sds((bucket, width), bf16), sds((bucket, width), bf16),
        ],
        in_specs=[vm] * 7,
        out_specs=[vm] * 7 + [hbm] * 2,
        scratch_shapes=[
            pltpu.VMEM((bucket, width), bf16), pltpu.VMEM((own_rows, width), bf16), dma(2), dma(2, 3, 4), dma(2, 3, 4),
        ],
        compiler_params=pltpu.CompilerParams(
            collective_id=collective_id, has_side_effects=True, vmem_limit_bytes=48 << 20
        ),
        name="front",
    )(tokens, cotangent, gain, length, w_query, w_key, w_value)


def per_device(
    tokens,
    gain_attn,
    gain_mlp,
    w_query,
    w_key,
    w_value,
    w_out,
    w_gate,
    w_up,
    w_down,
    cotangent,
    lengths,
):
    groups = lax.axis_size("tensor")
    length = lax.dynamic_slice(lengths, (lax.axis_index("dp"),), (1,))[None]
    w_query_t, w_key_t, w_gate_t, w_up_t = w_query.T, w_key.T, w_gate.T, w_up.T
    query, key, value, numer, attended, denom, den_row, normed_all, cot_all = front_call(
        tokens, cotangent, gain_attn[None], length, w_query_t, w_key_t, w_value, 3
    )
    output, grad_state, mlp_gain, state_all, down_total, gate_total, up_total = mlp_call(
        attended, w_out, tokens, gain_mlp[None], length, w_gate_t, w_up_t, w_down, cot_all, 1
    )
    small, input_grad, out_total, value_total, qk_total = back_call(
        state_all, attended, w_out, numer, denom, length, query, key, value, gain_attn[None], mlp_gain, den_row,
        normed_all, w_query_t, w_key_t, w_value, tokens, grad_state, 2,
    )
    gain_attn_total, gain_mlp_total = small[0], small[1]
    feat_width = w_query.shape[1]
    query_total, key_total = qk_total[:feat_width].T, qk_total[feat_width:].T
    gate_total, up_total = gate_total.T, up_total.T
    heads = feat_width // FEAT * groups
    den_mean = jnp.sum(small[2, :128]) / (heads * jnp.sum(lengths).astype(f32))
    return (
        output,
        input_grad,
        gain_attn_total,
        gain_mlp_total,
        query_total,
        key_total,
        value_total,
        out_total,
        gate_total,
        up_total,
        down_total,
        den_mean,
    )


def solution(mesh):
    return jax.shard_map(
        per_device,
        mesh=mesh,
        in_specs=(
            P(("dp", "tensor"), None),
            P(),
            P(),
            P(None, "tensor"),
            P(None, "tensor"),
            P(None, "tensor"),
            P("tensor", None),
            P(None, "tensor"),
            P(None, "tensor"),
            P("tensor", None),
            P(("dp", "tensor"), None),
            P(),
        ),
        out_specs=(
            P(("dp", "tensor"), None),
            P(("dp", "tensor"), None),
            P(),
            P(),
            P("dp", "tensor"),
            P("dp", "tensor"),
            P("dp", "tensor"),
            P("tensor", "dp"),
            P("dp", "tensor"),
            P("dp", "tensor"),
            P("tensor", "dp"),
            P(),
        ),
        check_vma=False,
    )
```

```python
import functools
import math

import jax
import jax.numpy as jnp
from jax import lax
from jax.experimental import pallas as pl
from jax.experimental.pallas import tpu as pltpu
from jax.sharding import PartitionSpec as P

FEAT = 16
MESH = pl.DeviceIdType.MESH
f32 = jnp.float32
bf16 = jnp.bfloat16
NT = (((1,), (1,)), ((), ()))
TN = (((0,), (0,)), ((), ()))
AHEAD = 4
LAG = 3
SETTLE = 3
STRIP = 16
VMEM_MB = 63


def dot(a, b, dims=(((1,), (0,)), ((), ()))):
    return lax.dot_general(a, b, dims, preferred_element_type=f32)


def loop(count, body):
    def step(i, carry):
        body(i)
        return carry

    lax.fori_loop(0, count, step, 0)


def pieces(width, size):
    return [(start, min(size, width - start)) for start in range(0, width, size)]


class Group:
    def __init__(self):
        self.dp = lax.axis_index("dp")
        self.t = lax.axis_index("tensor")
        self.y, self.c = self.t // 2, lax.rem(self.t, 2)
        self.sibling = (self.dp, self.y * 2 + 1 - self.c)
        self.across = (self.dp, (1 - self.y) * 2 + self.c)


def remote(src, dst, send, recv, device):
    return pltpu.make_async_remote_copy(src, dst, send, recv, device_id=device, device_id_type=MESH)


class RowSums:
    def __init__(self, g, own_rows, phase, chunk, part, bufs, sems, piece=512):
        self.piece = piece
        self.g, self.own, self.p, self.chunk, self.part = g, own_rows, phase, chunk, part
        self.sibsend, self.sibrecv, self.ysend, self.yrecv, self.total = bufs
        self.sib_s, self.sib_r, self.y_s, self.y_r = sems
        self.count = own_rows // chunk

    def at(self, j):
        return pl.ds(pl.multiple_of(j * self.chunk, self.chunk), self.chunk)

    def rows(self, y, c, j):
        return pl.ds(pl.multiple_of((y * 2 + c) * self.own + j * self.chunk, self.chunk), self.chunk)

    def sib(self, far, j):
        return remote(
            self.sibsend.at[far, self.at(j)], self.sibrecv.at[far, self.at(j)],
            self.sib_s.at[self.p, far, j], self.sib_r.at[self.p, far, j], self.g.sibling,
        )

    def ycopy(self, j):
        return remote(
            self.ysend.at[self.at(j)], self.yrecv.at[self.at(j)],
            self.y_s.at[self.p, j], self.y_r.at[self.p, j], self.g.across,
        )

    def give(self, far, j):
        y = 1 - self.g.y if far else self.g.y
        for n, w in pieces(self.total.shape[1], self.piece):
            self.sibsend[far, self.at(j), n : n + w] = self.part(self.rows(y, 1 - self.g.c, j), n, w).astype(bf16)
        self.sib(far, j).start()

    def send(self, j):
        g = self.g
        for n, w in pieces(self.total.shape[1], self.piece):
            self.total[self.at(j), n : n + w] = self.part(self.rows(1 - g.y, g.c, j), n, w)
        self.sib(1, j).wait_recv()
        self.ysend[self.at(j)] = (self.total[self.at(j)] + self.sibrecv[1, self.at(j)].astype(f32)).astype(bf16)
        self.ycopy(j).start()

    def hold(self, j):
        for n, w in pieces(self.total.shape[1], self.piece):
            self.total[self.at(j), n : n + w] = self.part(self.rows(self.g.y, self.g.c, j), n, w)

    def finish(self, j, use):
        self.sib(0, j).wait_recv()
        self.ycopy(j).wait_recv()

        def strip(i):
            r = pl.ds(pl.multiple_of(j * self.chunk + i * STRIP, STRIP), STRIP)
            use(r, self.total[r] + self.sibrecv[0, r].astype(f32) + self.yrecv[r].astype(f32))

        loop(self.chunk // STRIP, strip)

    def drain(self):
        def body(j):
            self.sib(0, j).wait_send()
            self.sib(1, j).wait_send()
            self.ycopy(j).wait_send()

        loop(self.count, body)


class Spread:
    def __init__(self, g, own_rows, chunk, src, full, sems, phase):
        self.g, self.own, self.chunk, self.src, self.full, self.p = g, own_rows, chunk, src, full, phase
        self.s, self.r = sems
        self.count = own_rows // chunk

    def rows(self, y, c, j):
        return pl.ds(pl.multiple_of((y * 2 + c) * self.own + j * self.chunk, self.chunk), self.chunk)

    def copy(self, kind, j):
        g = self.g
        rows = self.rows(g.y, g.c, j)
        if kind == 2:
            rows = self.rows(1 - g.y, g.c, j)
            src = self.full.at[rows]
        elif self.src is None:
            src = self.full.at[rows]
        else:
            src = self.src.at[pl.ds(pl.multiple_of(j * self.chunk, self.chunk), self.chunk)]
        return remote(
            src, self.full.at[rows], self.s.at[self.p, kind, j], self.r.at[self.p, kind, j],
            g.across if kind == 1 else g.sibling,
        )

    def start(self, j):
        self.copy(1, j).start()
        self.copy(0, j).start()

    def relay(self, j):
        self.copy(1, j).wait_recv()
        self.copy(2, j).start()

    def sib_in(self, j):
        self.copy(0, j).wait_recv()

    def far_in(self, j):
        self.copy(2, j).wait_recv()

    def drain(self):
        def body(j):
            for kind in range(3):
                self.copy(kind, j).wait_send()

        loop(self.count, body)


class WeightSums:
    def __init__(self, g, dp_size, rows, weights, widths, write, refs, sems, emit):
        self.g, self.rows, self.widths, self.write, self.emit = g, rows, widths, write, emit
        self.weights = weights
        self.nz = dp_size // 2
        self.z, self.x = g.dp // 2, lax.rem(g.dp, 2)
        self.halves = max(1, rows // 128)
        self.rn = rows // self.halves
        self.ring = self.zs_slots(self.nz)
        self.jobs = weights * self.halves - 1
        self.steps = self.jobs * self.nz
        (self.xs, self.zs, self.acc, self.xtmp, self.ztmp, self.xrecv, self.zrecv,
         self.zf, self.zfx, self.facc, self.frecv, self.fxrecv) = refs
        (self.xs_s, self.xr_s, self.zs_s, self.zr_s, self.loc, self.zf_s, self.zf_r, self.fx_s, self.fx_r) = sems
        self.ahead = self.xs.shape[0]
        self.partner = (self.z * 2 + 1 - self.x, g.t)

    @staticmethod
    def zs_slots(nz):
        return 2 * nz if nz <= 4 else nz

    def job(self, s):
        lin = s // self.nz + 1
        return lin // self.halves, lax.rem(lin, self.halves)

    def by_kind(self, allowed, s, body):
        i, _ = self.job(s)

        @pl.when(allowed & (i < self.weights - 1))
        def _():
            body(s, 0)

        @pl.when(allowed & (i == self.weights - 1))
        def _():
            body(s, 1)

    def order(self, k):
        last = self.nz - 1
        upper = self.z >= self.nz // 2
        z = jnp.where(upper, last - self.z, self.z)
        zt = jnp.where(k < last - z, last - k, jnp.where(k < last, last - 1 - k, z))
        return jnp.where(upper, last - zt, zt)

    def coming(self, zt):
        return jnp.where(zt > self.z, self.z > 0, self.z < self.nz - 1)

    def towards(self, zt):
        return (jnp.where(zt > self.z, self.z + 1, self.z - 1) * 2 + self.x, self.g.t)

    def slot(self, zt):
        return jnp.where(zt == self.z - 1, self.nz, zt)

    def part(self, ref, index, kind):
        return ref.at[index] if kind == 0 else ref.at[index, :, pl.ds(0, self.widths[1])]

    def small(self, ref, kind):
        return ref.at[pl.ds(0, self.rn)] if kind == 0 else ref.at[pl.ds(0, self.rn), pl.ds(0, self.widths[1])]

    def xcopy(self, s, kind):
        slot = lax.rem(s, self.ahead)
        return remote(
            self.part(self.xs, slot, kind), self.part(self.xrecv, s, kind), self.xs_s.at[slot], self.xr_s.at[s],
            self.partner,
        )

    def zcopy(self, s, zt, kind):
        ring = lax.rem(s, self.ring)
        j = s // self.nz * (self.nz + 1) + self.slot(zt)
        return remote(
            self.part(self.zs, ring, kind), self.part(self.zrecv, j, kind), self.zs_s.at[ring], self.zr_s.at[j],
            self.towards(zt),
        )

    def zwait(self, j, kind):
        remote(
            self.part(self.zs, 0, kind), self.part(self.zrecv, j, kind), self.zs_s.at[0], self.zr_s.at[j],
            self.partner,
        ).wait_recv()

    def fetch(self, src, dst, k):
        copy = pltpu.make_async_copy(src, dst, self.loc.at[k])
        copy.start()
        return copy

    def xsend(self, s, kind):
        self.by_kind(s >= self.ahead, s - self.ahead, lambda a, old: self.xcopy(a, old).wait_send())
        i, h = self.job(s)
        slot = lax.rem(s, self.ahead)

        def store(n, w, value):
            self.xs[slot, :, n : n + w] = value.astype(bf16)

        self.write(store, kind, i, self.order(lax.rem(s, self.nz)), 1 - self.x, h)
        self.xcopy(s, kind).start()

    def zsent(self, s):
        k = lax.rem(s, self.nz)
        self.by_kind(
            (s >= 0) & (k < self.nz - 1), s, lambda a, old: self.zcopy(a, self.order(k), old).wait_send()
        )

    def xstep(self, s, kind):
        w = self.widths[kind]
        k = lax.rem(s, self.nz)
        zt = self.order(k)
        i, h = self.job(s)
        self.xcopy(s, kind).wait_recv()
        copy = self.fetch(self.part(self.xrecv, s, kind), self.small(self.xtmp, kind), 0)
        slot = lax.rem(s // self.nz, 2)
        ring = lax.rem(s, self.ring)
        self.zsent(s - self.ring)

        def store(n, w, value):
            self.acc[slot, :, n : n + w] = value

        self.write(store, kind, i, zt, self.x, h)
        copy.wait()
        total = self.acc[slot, :, :w] + self.xtmp[:, :w].astype(f32)

        @pl.when(k == self.nz - 1)
        def _():
            self.acc[slot, :, :w] = total

        @pl.when(k < self.nz - 1)
        def _():
            self.zs[ring, :, :w] = total.astype(bf16)

            @pl.when(jnp.logical_not(self.coming(zt)))
            def _():
                self.zcopy(s, zt, kind).start()

    def zstep(self, s, kind):
        w = self.widths[kind]
        k = lax.rem(s, self.nz)
        zt = self.order(k)
        ring = lax.rem(s, self.ring)

        @pl.when((k < self.nz - 1) & self.coming(zt))
        def _():
            j = s // self.nz * (self.nz + 1) + zt
            self.zwait(j, kind)
            self.fetch(self.part(self.zrecv, j, kind), self.small(self.ztmp, kind), 1).wait()
            self.zs[ring, :, :w] = (
                self.zs[ring, :, :w].astype(f32) + self.ztmp[: self.rn, :w].astype(f32)
            ).astype(bf16)
            self.zcopy(s, zt, kind).start()

    def final(self, s, kind):
        w = self.widths[kind]
        jx = s // self.nz
        slot = lax.rem(jx, 2)

        def take(j):
            self.zwait(j, kind)
            self.fetch(self.part(self.zrecv, j, kind), self.small(self.ztmp, kind), 1).wait()
            self.acc[slot, :, :w] += self.ztmp[: self.rn, :w].astype(f32)

        @pl.when(self.z > 0)
        def _():
            take(jx * (self.nz + 1) + self.z)

        @pl.when(self.z < self.nz - 1)
        def _():
            take(jx * (self.nz + 1) + self.nz)

        i, h = self.job(s)
        self.emit(kind, i, h, self.acc.at[slot])

    def fcopy(self, q, zt):
        slot = self.slot(zt)
        return remote(self.zf.at[q], self.frecv.at[slot], self.zf_s.at[q], self.zf_r.at[slot], self.towards(zt))

    def fwait(self, slot):
        remote(self.zf.at[0], self.frecv.at[slot], self.zf_s.at[0], self.zf_r.at[slot], self.partner).wait_recv()

    def fstart(self, q):
        zt = self.order(q)
        for xt in range(2):

            def store(n, w, value):
                self.zf[q, xt * self.rn : (xt + 1) * self.rn, n : n + w] = value.astype(bf16)

            self.write(store, 0, 0, zt, xt, 0)

        @pl.when(jnp.logical_not(self.coming(zt)))
        def _():
            self.fcopy(q, zt).start()

    def fstep(self, q):
        zt = self.order(q)

        @pl.when(self.coming(zt))
        def _():
            self.fwait(zt)
            self.fetch(self.frecv.at[zt], self.ztmp, 1).wait()
            self.zf[q] = (self.zf[q].astype(f32) + self.ztmp[...].astype(f32)).astype(bf16)
            self.fcopy(q, zt).start()

    def fxcopy(self):
        return remote(self.zfx, self.fxrecv, self.fx_s.at[0], self.fx_r.at[0], self.partner)

    def fend(self):
        for xt in range(2):

            def store(n, w, value):
                self.facc[xt * self.rn : (xt + 1) * self.rn, n : n + w] = value

            self.write(store, 0, 0, self.z, xt, 0)

        def take(slot):
            self.fwait(slot)
            self.fetch(self.frecv.at[slot], self.ztmp, 1).wait()
            self.facc[...] += self.ztmp[...].astype(f32)

        @pl.when(self.z > 0)
        def _():
            take(self.z)

        @pl.when(self.z < self.nz - 1)
        def _():
            take(self.nz)

        away = pl.ds(pl.multiple_of((1 - self.x) * self.rn, self.rn), self.rn)
        self.zfx[...] = self.facc[away].astype(bf16)
        self.fxcopy().start()

    def ffinal(self):
        self.fxcopy().wait_recv()
        self.fetch(self.fxrecv, self.xtmp, 1).wait()
        own = pl.ds(pl.multiple_of(self.x * self.rn, self.rn), self.rn)
        self.facc[own] += self.xtmp[...].astype(f32)
        self.emit(0, 0, 0, self.facc.at[own])

    def begin(self):
        loop(self.ahead, lambda s: self.xsend(s, 0))
        loop(self.nz - 1, self.fstart)

    def services(self):
        return max(self.steps + SETTLE + 1, 2 * self.nz + 5)

    def service(self, s):
        self.by_kind(s < self.steps, s, self.xstep)
        self.by_kind(s + self.ahead < self.steps, s + self.ahead, self.xsend)
        self.by_kind((s >= LAG) & (s - LAG < self.steps), s - LAG, self.zstep)

        @pl.when((lax.rem(s, 2) == 1) & (s // 2 < self.nz - 1))
        def _():
            self.fstep(s // 2)

        @pl.when(s == 2 * self.nz - 1)
        def _():
            self.fend()

        @pl.when(s == 2 * self.nz + 4)
        def _():
            self.ffinal()

        due = (s >= self.nz + SETTLE) & (lax.rem(s - SETTLE, self.nz) == 0) & (s - SETTLE <= self.steps)
        self.by_kind(due, s - SETTLE - self.nz, self.final)

    def drain(self):
        loop(
            self.ahead,
            lambda a: self.by_kind(
                a >= 0, self.steps - self.ahead + a, lambda s, kind: self.xcopy(s, kind).wait_send()
            ),
        )
        loop(self.ring, lambda a: self.zsent(self.steps - self.ring + a))
        loop(self.nz - 1, lambda q: self.fcopy(q, self.order(q)).wait_send())
        self.fxcopy().wait_send()


def meet(g, nz, every=False):
    if nz == 0:
        barrier = pltpu.get_barrier_semaphore()
        for device in (g.sibling, g.across):
            pl.semaphore_signal(barrier, inc=1, device_id=device, device_id_type=MESH)
        pl.semaphore_wait(barrier, 2)
        return
    z, x = g.dp // 2, lax.rem(g.dp, 2)
    barrier = pltpu.get_barrier_semaphore()

    def hello(device):
        pl.semaphore_signal(barrier, inc=1, device_id=device, device_id_type=MESH)

    hello(g.sibling)
    hello(g.across)
    hello((z * 2 + 1 - x, g.t))
    if every:
        loop(nz - 1, lambda k: hello((lax.rem(z + 1 + k, nz) * 2 + x, g.t)))
        pl.semaphore_wait(barrier, nz + 2)
        return

    @pl.when(z > 0)
    def _():
        hello(((z - 1) * 2 + x, g.t))

    @pl.when(z < nz - 1)
    def _():
        hello(((z + 1) * 2 + x, g.t))

    peers = 5 - jnp.where(z == 0, 1, 0) - jnp.where(z == nz - 1, 1, 0)
    pl.semaphore_wait(barrier, peers)


def owner_dot(load, right, rows, zt, xt, h):
    if rows % 128:
        both = dot(load(pl.ds(pl.multiple_of(zt * (2 * rows), 2 * rows), 2 * rows)), right, TN)
        return jnp.where(xt == 0, both[:rows], both[rows:])
    rn = min(rows, 128)
    return dot(load(pl.ds(pl.multiple_of((zt * 2 + xt) * rows + h * rn, rn), rn)), right, TN)


def head_lanes(h, feat, width):
    return (lax.broadcasted_iota(jnp.int32, (1, width), 1) // feat == h).astype(f32).astype(bf16)


def norm_parts(state):
    scale = lax.rsqrt(jnp.mean(state * state, axis=-1, keepdims=True) + 1e-06)
    return state * scale, scale


def layer_kernel(
    dp_size,
    attended, w_out, gain, gain_attn, length, denom, den_row,
    tokens_h, w_gate_h, w_up_h, w_down_h, cot_h, normed_h, query_h, key_h, value_h, w_query_h, w_key_h, w_value_h,
    small_out, output_h, state_grad_h, state_all_h, down_h, gate_h, up_h, input_grad_h, out_h, value_grad_h, qk_h,
    xrecv, zrecv, frecv, fxrecv,
    w_gate, w_up, w_down, lefts, rights, mid, sibsend, sibrecv, ysend, yrecv, total, spread_buf,
    xs, zs, zf, zfx, acc, facc, xtmp, ztmp, turn,
    grad_den, gk_acc, gq_acc, gain_grad, gain_acc, smalls, small_got, small_z,
    load_sem, sib_s, sib_r, y_s, y_r, ag_s, ag_r,
    xs_s, xr_s, zs_s, zr_s, zf_s, zf_r, fx_s, fx_r, loc, sm_s, sm_r, smz_s, smz_r, ready,
):
    g = Group()
    own_rows, width = tokens_h.shape
    tokens = spread_buf
    hidden_units = rights.shape[2]
    rows = width // dp_size
    loads = [
        pltpu.make_async_copy(src, dst, load_sem.at[n])
        for n, (src, dst) in enumerate(
            [(w_gate_h, w_gate), (w_up_h, w_up), (w_down_h, w_down), (cot_h, lefts.at[0]), (tokens_h, tokens)]
        )
    ]
    for copy in loads:
        copy.start()
    nz = dp_size // 2
    meet(g, nz, every=True)
    bufs = (sibsend, sibrecv, ysend, yrecv, total)
    sems = (sib_s, sib_r, y_s, y_r)

    def attn_part(r, n, w):
        return dot(attended[r], w_out[:, n : n + w])

    sums = RowSums(g, own_rows, 0, 64, attn_part, bufs, sems)
    normed = Spread(g, own_rows, 64, None, lefts.at[1], (ag_s, ag_r), 0)
    own_first = pl.multiple_of(g.t * own_rows, own_rows)

    def first_state(r, summed):
        state = tokens[r].astype(f32) + summed
        mid[r] = state
        normal, _ = norm_parts(state)
        start = pl.multiple_of(own_first + r.start, STRIP)
        lefts[1, pl.ds(start, STRIP)] = (normal * gain[...]).astype(bf16)

    sums.give(1, 0)

    def far(j):
        @pl.when(j + 1 < sums.count)
        def _():
            sums.give(1, j + 1)

        sums.send(j)

    loop(sums.count, far)

    def near(j):
        sums.give(0, j)
        sums.hold(j)

    loop(sums.count, near)

    def feed(y, c, half):
        r = pl.ds(pl.multiple_of((y * 2 + c) * own_rows + half * 128, 128), 128)
        for n, w in pieces(hidden_units, 512):
            gate = dot(lefts[1, r], w_gate[n : n + w], NT)
            up = dot(lefts[1, r], w_up[n : n + w], NT)
            back = dot(lefts[0, r], w_down[n : n + w], NT)
            sig = jax.nn.sigmoid(gate)
            active = gate * sig
            rights[0, r, n : n + w] = (active * up).astype(bf16)
            rights[1, r, n : n + w] = (back * up * sig * (1.0 + gate * (1.0 - sig))).astype(bf16)
            rights[2, r, n : n + w] = (back * active).astype(bf16)

    def close(j):
        sums.finish(j, first_state)
        normed.start(j)

    loads[4].wait()

    def half_near(half):
        loop(2, lambda a: close(half * 2 + a))

        @pl.when(half == 0)
        def _():
            for copy in loads[:4]:
                copy.wait()

        feed(g.y, g.c, half)
        loop(2, lambda a: normed.sib_in(half * 2 + a))
        feed(g.y, 1 - g.c, half)

    loop(2, half_near)

    def half_far(half):
        loop(2, lambda a: normed.relay(half * 2 + a))
        feed(1 - g.y, g.c, half)
        loop(2, lambda a: normed.far_in(half * 2 + a))
        feed(1 - g.y, 1 - g.c, half)

    loop(2, half_far)
    sums.drain()

    bucket, values = attended.shape
    head_width, feat_pad = 128, 128
    heads = values // head_width
    feat_width = w_query_h.shape[0]
    feat = feat_width // heads
    halves = max(1, rows // 128)
    rn = rows // halves
    grads_at, value_at, sums_at = 0, values, 2 * values
    query_at = sums_at + values + 2 * feat_width
    key_at = query_at + feat_pad
    sums_end = query_at
    kept_query, kept_key, turned_key = bucket, bucket + feat_width, bucket + 2 * feat_width

    def write(store, kind, i, zt, xt, h):
        if kind == 0:
            left = jnp.minimum(i, 1)
            store(0, hidden_units, owner_dot(lambda cols: lefts[left, :, cols], rights[i], rows, zt, xt, h))
            return
        store(0, values, owner_dot(lambda cols: w_gate[:bucket, cols], attended[...], rows, zt, xt, h))
        store(
            values, sums_end - sums_at,
            owner_dot(lambda cols: w_up[:bucket, cols], w_down[:bucket, sums_at:sums_end], rows, zt, xt, h),
        )

    def put(src, out, n, w, h):
        to = out.at[pl.ds(n, w)]
        if halves > 1:
            to = out.at[pl.ds(n, w), pl.ds(pl.multiple_of(h * rn, rn), rn)]
        copy = pltpu.make_async_copy(src.at[pl.ds(0, w)], to, loc.at[2])
        copy.start()
        copy.wait()

    def emit(kind, i, h, block):
        if kind == 0:
            for n, w in pieces(hidden_units, 512):
                turn[:w] = block[:, n : n + w].T
                for m, out in enumerate((down_h, gate_h, up_h)):
                    pl.when(i == m)(functools.partial(put, turn, out, n, w, h))
            return
        for n, w in pieces(values, 512):
            turn[:w] = block[:, n : n + w].T
            put(turn, out_h, n, w, h)
        copy = pltpu.make_async_copy(
            block.at[:, pl.ds(values, values)], value_grad_h.at[pl.ds(pl.multiple_of(h * rn, rn), rn)], loc.at[2]
        )
        copy.start()
        turn[: 2 * feat_width] = block[:, 2 * values : 2 * values + 2 * feat_width].T
        copy.wait()
        put(turn, qk_h, 0, 2 * feat_width, h)

    engine = WeightSums(
        g, dp_size, rows, 4, (hidden_units, 2 * values + 2 * feat_width), write,
        (xs, zs, acc, xtmp, ztmp, xrecv, zrecv, zf, zfx, facc, frecv, fxrecv),
        (xs_s, xr_s, zs_s, zr_s, loc, zf_s, zf_r, fx_s, fx_r), emit,
    )
    engine.begin()

    def back_part(r, n, w):
        return dot(rights[1, r], w_gate[:, n : n + w]) + dot(rights[2, r], w_up[:, n : n + w])

    sums = RowSums(g, own_rows, 1, 128, back_part, bufs, sems)
    states = Spread(g, own_rows, 128, spread_buf, state_all_h, (ag_s, ag_r), 1)
    gain_grad[...] = jnp.zeros_like(gain_grad)

    def state_back(r, grad):
        normal, scale = norm_parts(mid[r])
        weighted = grad * gain[...]
        start = pl.multiple_of(own_first + r.start, STRIP)
        change = scale * (weighted - normal * jnp.mean(weighted * normal, axis=-1, keepdims=True))
        state = lefts[0, pl.ds(start, STRIP)].astype(f32) + change
        gain_grad[...] += jnp.sum(grad * normal, axis=0, keepdims=True)
        total[r] = state
        spread_buf[r] = state.astype(bf16)

    def far_back(j):
        sums.give(1, j)
        sums.send(j)

    loop(sums.count, far_back)

    def near_back(j):
        sums.give(0, j)
        engine.service(2 * j)
        sums.hold(j)
        engine.service(2 * j + 1)

    loop(sums.count, near_back)
    used = 2 * sums.count

    def own_copy(j):
        r = pl.ds(pl.multiple_of(j * 128, 128), 128)
        to = pl.ds(pl.multiple_of(own_first + j * 128, 128), 128)
        return (
            pltpu.make_async_copy(total.at[r], state_grad_h.at[r], load_sem.at[0]),
            pltpu.make_async_copy(spread_buf.at[r], state_all_h.at[to], load_sem.at[1]),
        )

    def close_back(j):
        sums.finish(j, state_back)
        states.start(j)
        copies = own_copy(j)
        for copy in copies:
            copy.start()
        engine.service(used + j)
        for copy in copies:
            copy.wait()

    loop(sums.count, close_back)
    used = used + sums.count

    def pass_back(j):
        states.relay(j)
        engine.service(used + j)

    loop(sums.count, pass_back)
    used = used + sums.count

    def arrive(j):
        states.sib_in(j)
        states.far_in(j)

    loop(sums.count, arrive)
    sums.drain()

    def down_part(r, n, w):
        return dot(rights[0, r], w_down[:, n : n + w])

    sums = RowSums(g, own_rows, 2, 128, down_part, bufs, sems)

    def far_down(j):
        sums.give(1, j)
        sums.send(j)
        engine.service(used + j)

    loop(sums.count, far_down)
    used = used + sums.count

    def near_down(j):
        sums.give(0, j)
        sums.hold(j)

    loop(sums.count, near_down)

    fetches = [
        (state_all_h, w_gate.at[pl.ds(0, bucket)]), (normed_h, w_up.at[pl.ds(0, bucket)]),
        (value_h, w_down.at[pl.ds(0, bucket), pl.ds(value_at, values)]),
        (query_h, w_down.at[pl.ds(0, bucket), pl.ds(query_at, feat_pad)]),
        (key_h, w_down.at[pl.ds(0, bucket), pl.ds(key_at, feat_pad)]),
        (w_query_h, w_down.at[pl.ds(kept_query, feat_width)]), (w_key_h, w_down.at[pl.ds(kept_key, feat_width)]),
    ]
    span = 256
    chunks = [(width // span // 2, w_gate), (width // span // 2, w_up)]
    row = 0
    for count, home in chunks:
        for m in range(count):
            fetches.append(
                (w_value_h.at[pl.ds(row, span)], home.at[pl.ds(bucket, span), pl.ds(m * values, values)])
            )
            row += span
    fetches = [pltpu.make_async_copy(src, dst, load_sem.at[n]) for n, (src, dst) in enumerate(fetches)]
    for copy in fetches:
        copy.start()
    for copy in fetches:
        copy.wait()
    w_down[turned_key : turned_key + feat_pad, :bucket] = (
        w_down[:bucket, key_at : key_at + feat_pad].astype(f32).T.astype(bf16)
    )

    def spread_grad(b):
        r = pl.ds(pl.multiple_of(b * 128, 128), 128)
        grad = dot(w_gate[r], w_out[...], NT).astype(bf16).astype(f32)
        lane = lax.broadcasted_iota(jnp.int32, (128, 128), 1)
        dens = jnp.zeros((128, 128), f32)
        turned_den = denom[:, r].T
        for h in range(heads):
            cols = slice(h * head_width, (h + 1) * head_width)
            den = turned_den[:, h : h + 1]
            piece = grad[:, cols]
            w_down[r, grads_at + h * head_width : grads_at + (h + 1) * head_width] = (piece / den).astype(bf16)
            back = -jnp.sum(piece * attended[r, cols].astype(f32), axis=1, keepdims=True) / den
            dens = jnp.where(lane == h, back, dens)
        grad_den[:, r] = dens.T[: grad_den.shape[0]]

    loop(bucket // 128, spread_grad)
    engine.service(used)
    used = used + 1
    states.drain()

    def last_state(r, summed):
        position = own_first + r.start + lax.broadcasted_iota(jnp.int32, (STRIP, 1), 0)
        valid = (position < length[...]).astype(f32)
        spread_buf[r] = (valid * (mid[r] + summed)).astype(bf16)

    loop(sums.count, lambda j: sums.finish(j, last_state))
    pl.semaphore_signal(ready.at[0], inc=1, device_id=g.sibling, device_id_type=MESH)
    pl.semaphore_signal(ready.at[1], inc=1, device_id=g.across, device_id_type=MESH)
    keep = pltpu.make_async_copy(spread_buf, output_h, loc.at[2])
    keep.start()
    keep.wait()
    refills = [
        pltpu.make_async_copy(tokens_h, tokens, load_sem.at[15]),
        pltpu.make_async_copy(state_grad_h, mid, load_sem.at[16]),
    ]
    for copy in refills:
        copy.start()
    engine.service(used)
    used = used + 1
    gk_acc[...] = jnp.zeros_like(gk_acc)
    gq_acc[...] = jnp.zeros_like(gq_acc)
    total[...] = jnp.zeros_like(total)
    qk_scale = 1.0 / math.sqrt(feat)
    tile = 256

    def head(h):
        lanes = head_lanes(h, feat, feat_pad)
        sub = (lax.broadcasted_iota(jnp.int32, (feat_pad, 1), 0) // feat == h).astype(f32).astype(bf16)
        offset = pl.multiple_of(h * head_width, head_width)
        for qb in range(bucket // tile):
            q0, nk = qb * tile, (qb + 1) * tile
            q_own = w_down[q0:nk, query_at : query_at + feat_pad] * lanes
            grads = w_down[q0:nk, pl.ds(grads_at + offset, head_width)]
            for k0, count in pieces(nk, 2 * tile):
                keys = slice(k0, k0 + count)
                kept = w_down[turned_key : turned_key + feat_pad, keys] * sub
                scores = dot(w_down[keys, key_at : key_at + feat_pad], q_own, NT) * qk_scale
                spot = k0 + lax.broadcasted_iota(jnp.int32, (count, tile), 0)
                below = spot <= q0 + lax.broadcasted_iota(jnp.int32, (count, tile), 1)
                real = k0 + lax.broadcasted_iota(jnp.int32, (count, 1), 0) < length[...]
                mask = below.astype(f32) * real.astype(f32)
                taylor = (1.0 + scores + 0.5 * scores * scores) * mask
                moved = dot(taylor.astype(bf16), grads)
                for kb in range(count // tile):
                    at = (k0 // tile + kb) * values
                    total[:, pl.ds(at + offset, head_width)] += moved[kb * tile : (kb + 1) * tile]
                back = dot(w_down[keys, pl.ds(value_at + offset, head_width)], grads, NT)
                back = back + grad_den[pl.ds(h, 1), q0:nk]
                low = (back * mask * (1.0 + scores)).astype(bf16)
                gk_acc[keys] += dot(low, q_own)
                gq_acc[:, q0:nk] += dot(kept, low)

        @pl.when(lax.rem(h, 2) == 1)
        def _():
            engine.service(used + h // 2)

    loop(heads, head)
    used = used + heads // 2
    for kb in range(bucket // tile):
        r = slice(kb * tile, (kb + 1) * tile)
        w_down[r, sums_at : sums_at + values] = total[:, kb * values : (kb + 1) * values].astype(bf16)
        pair = jnp.concatenate([gq_acc[:feat_width, r].T, gk_acc[r, :feat_width]], axis=1) * qk_scale
        w_down[r, sums_at + values : sums_end] = pair.astype(bf16)
    sums.drain()

    def attn_back_part(r, n, w):
        count, home = chunks[0] if n < width // 2 else chunks[1]
        m = n // span % count
        out = dot(
            w_down[r, sums_at : sums_at + values], home[bucket : bucket + span, m * values : (m + 1) * values], NT
        )
        out = out + dot(
            w_down[r, sums_at + values : sums_end], w_down[kept_query : kept_query + 2 * feat_width, n : n + w]
        )
        return out

    sums = RowSums(g, own_rows, 3, 128, attn_back_part, bufs, sems, span)
    pl.semaphore_wait(ready.at[0], 1)
    pl.semaphore_wait(ready.at[1], 1)

    def far_last(j):
        sums.give(1, j)
        sums.send(j)
        engine.service(used + j)

    loop(sums.count, far_last)
    used = used + sums.count

    def near_last(j):
        sums.give(0, j)
        sums.hold(j)
        engine.service(used + j)

    loop(sums.count, near_last)
    used = used + sums.count
    gain_acc[...] = jnp.zeros_like(gain_acc)
    for copy in refills:
        copy.wait()

    def input_back(r, grad):
        normal, inv = norm_parts(tokens[r].astype(f32))
        weighted = grad * gain_attn[...]
        change = inv * (weighted - normal * jnp.mean(weighted * normal, axis=-1, keepdims=True))
        gain_acc[...] += jnp.sum(grad * normal, axis=0, keepdims=True)
        mid[r] += change

    def close_last(j):
        sums.finish(j, input_back)
        engine.service(used + j)

    loop(sums.count, close_last)
    used = used + sums.count
    result = pltpu.make_async_copy(mid, input_grad_h, load_sem.at[0])
    result.start()

    smalls[0] = jnp.zeros(smalls.shape[1:], f32)
    quarter = width // 4
    for m in range(4):
        smalls[0, m : m + 1, :quarter] = gain_acc[:, m * quarter : (m + 1) * quarter]
        smalls[0, 4 + m : 5 + m, :quarter] = gain_grad[:, m * quarter : (m + 1) * quarter]
    smalls[0, 0:1, quarter:] = den_row[...]
    z, x = engine.z, engine.x
    peers = (g.sibling, g.across, engine.partner)
    for n, device in enumerate(peers):
        copy = remote(smalls.at[n], small_got.at[n], sm_s.at[n], sm_r.at[n], device)
        copy.start()
        engine.service(used + n)
        copy.wait()
        smalls[n + 1] = smalls[n] + small_got[n]
    used = used + len(peers)

    def zsmall(k):
        return remote(
            smalls.at[3], small_z.at[z], smz_s.at[k], smz_r.at[k], (lax.rem(z + 1 + k, nz) * 2 + x, g.t)
        )

    loop(nz - 1, lambda k: zsmall(k).start())
    loop(engine.services() - used, lambda n: engine.service(used + n))
    small_z[z] = smalls[3]

    def zgot(k):
        remote(
            smalls.at[3], small_z.at[lax.rem(z - 1 - k + nz, nz)], smz_s.at[k], smz_r.at[k], g.sibling
        ).wait_recv()

    loop(nz - 1, zgot)
    small_out[...] = jnp.zeros_like(small_out)

    def zadd(k):
        small_out[...] += small_z[k]

    loop(nz, zadd)
    loop(nz - 1, lambda k: zsmall(k).wait_send())
    result.wait()
    sums.drain()
    normed.drain()
    engine.drain()


def layer_call(
    attended, w_out, gain, gain_attn, length, denom, den_row, tokens, w_gate, w_up, w_down, cot_all,
    normed, query, key, value, w_query, w_key, w_value, collective_id,
):
    dp_size = lax.axis_size("dp")
    nz = dp_size // 2
    own_rows, width = tokens.shape
    bucket, values = attended.shape
    units = w_down.shape[0]
    feat_width = w_query.shape[0]
    small = (8, width // 4 + den_row.shape[1])
    rows = width // dp_size
    halves = max(1, rows // 128)
    rn = rows // halves
    jobs = 4 * halves - 1
    steps = jobs * nz
    ring = WeightSums.zs_slots(nz)
    vm, hbm = pl.BlockSpec(memory_space=pltpu.VMEM), pl.BlockSpec(memory_space=pl.ANY)
    dma = lambda *shape: pltpu.SemaphoreType.DMA(shape)
    vmem = lambda shape, kind=bf16: pltpu.VMEM(shape, kind)
    sds = jax.ShapeDtypeStruct
    outs = pl.pallas_call(
        functools.partial(layer_kernel, dp_size),
        out_shape=[
            sds(small, f32),
            sds((own_rows, width), bf16),
            sds((own_rows, width), f32),
            sds((bucket, width), bf16),
            *[sds((units, rows), f32)] * 3,
            sds((own_rows, width), f32),
            sds((values, rows), f32),
            sds((rows, values), f32),
            sds((2 * feat_width, rows), f32),
            sds((steps, rn, units), bf16),
            sds((jobs * (nz + 1), rn, units), bf16),
            sds((nz + 1, 2 * rn, units), bf16),
            sds((rn, units), bf16),
        ],
        in_specs=[vm] * 7 + [hbm] * 12,
        out_specs=[vm] + [hbm] * 14,
        scratch_shapes=[
            vmem((units, width)), vmem((units, width)), vmem((units, width)),
            vmem((2, bucket, width)), vmem((3, bucket, units)), vmem((own_rows, width), f32),
            vmem((2, own_rows, width)), vmem((2, own_rows, width)), vmem((own_rows, width)), vmem((own_rows, width)),
            vmem((own_rows, width), f32), vmem((own_rows, width)),
            vmem((AHEAD, rn, units)), vmem((ring, rn, units)), vmem((nz - 1, 2 * rn, units)), vmem((rn, units)),
            vmem((2, rn, units), f32), vmem((2 * rn, units), f32), vmem((rn, units)), vmem((2 * rn, units)),
            vmem((512, rn), f32),
            vmem((8, bucket), f32), vmem((bucket, 128), f32), vmem((128, bucket), f32),
            vmem((1, width), f32), vmem((1, width), f32),
            vmem((4, *small), f32), vmem((3, *small), f32), vmem((nz, *small), f32),
            dma(17), dma(4, 2, 4), dma(4, 2, 4), dma(4, 4), dma(4, 4), dma(2, 3, 4), dma(2, 3, 4),
            dma(AHEAD), dma(steps), dma(ring), dma(jobs * (nz + 1)), dma(nz), dma(nz + 1), dma(1), dma(1), dma(3),
            dma(3), dma(3), dma(nz), dma(nz), pltpu.SemaphoreType.REGULAR((2,)),
        ],
        compiler_params=pltpu.CompilerParams(
            collective_id=collective_id, has_side_effects=True, vmem_limit_bytes=VMEM_MB << 20
        ),
        name="layer",
    )(
        attended, w_out, gain, gain_attn, length, denom, den_row, tokens, w_gate, w_up, w_down, cot_all,
        normed, query, key, value, w_query, w_key, w_value,
    )
    return outs[:11]


def front_kernel(
    tokens, cotangent, gain, length, w_query, w_key, w_value,
    query, key, value, attended, denom_t, den_row, normed_h, cot_h,
    denom, normed, cot_own, load_sem, ag_s, ag_r,
):
    g = Group()
    own_rows = tokens.shape[0]
    bucket = normed.shape[0]
    feat_width, feat_pad = w_query.shape[0], query.shape[1]
    head_width = 128
    heads = value.shape[1] // head_width
    feat = feat_width // heads
    scale = 1.0 / math.sqrt(feat)
    own_first = pl.multiple_of(g.t * own_rows, own_rows)
    meet(g, 0)
    rows_out = Spread(g, own_rows, 64, None, normed, (ag_s, ag_r), 0)
    cots = Spread(g, own_rows, 64, cot_own, cot_h, (ag_s, ag_r), 1)

    def first_norm(j):
        for a in range(64 // STRIP):
            r = pl.ds(pl.multiple_of(j * 64 + a * STRIP, STRIP), STRIP)
            to = pl.ds(pl.multiple_of(own_first + j * 64 + a * STRIP, STRIP), STRIP)
            normal, _ = norm_parts(tokens[r].astype(f32))
            normed[to] = (normal * gain[...]).astype(bf16)
        rows_out.start(j)

    loop(rows_out.count, first_norm)
    position = own_first + lax.broadcasted_iota(jnp.int32, (own_rows, 1), 0)
    real_rows = (position < length[...]).astype(f32)
    cot_own[...] = (cotangent[...].astype(f32) * real_rows).astype(bf16)
    own_cot = pltpu.make_async_copy(cot_own, cot_h.at[pl.ds(own_first, own_rows)], load_sem.at[0])
    own_cot.start()

    def project(y, c, half):
        r = pl.ds(pl.multiple_of((y * 2 + c) * own_rows + half * 128, 128), 128)
        value[r] = dot(normed[r], w_value[...]).astype(bf16)
        for out, weight in ((query, w_query), (key, w_key)):
            out[r] = jnp.zeros((128, feat_pad), bf16)
            out[r, :feat_width] = dot(normed[r], weight[...], NT).astype(bf16)

    def near(half):
        project(g.y, g.c, half)
        loop(2, lambda a: rows_out.sib_in(half * 2 + a))
        project(g.y, 1 - g.c, half)

    loop(2, near)

    def far(half):
        loop(2, lambda a: rows_out.relay(half * 2 + a))
        project(1 - g.y, g.c, half)
        loop(2, lambda a: rows_out.far_in(half * 2 + a))
        project(1 - g.y, 1 - g.c, half)

    loop(1, far)
    loop(2, lambda a: rows_out.relay(2 + a))
    loop(cots.count, cots.start)
    project(1 - g.y, g.c, 1)
    loop(2, lambda a: rows_out.far_in(2 + a))
    project(1 - g.y, 1 - g.c, 1)
    keep = pltpu.make_async_copy(normed, normed_h, load_sem.at[1])
    keep.start()
    denom[...] = jnp.zeros_like(denom)
    tile = 256

    def head(h):
        lanes = head_lanes(h, feat, feat_pad)
        cols = pl.ds(pl.multiple_of(h * head_width, head_width), head_width)
        for qb in range(bucket // tile):
            q0, nk = qb * tile, (qb + 1) * tile
            scores = dot(query[q0:nk] * lanes, key[:nk], NT) * scale
            spot = lax.broadcasted_iota(jnp.int32, (tile, nk), 1)
            below = spot <= q0 + lax.broadcasted_iota(jnp.int32, (tile, nk), 0)
            real = lax.broadcasted_iota(jnp.int32, (1, nk), 1) < length[...]
            taylor = (1.0 + scores + 0.5 * scores * scores) * (below.astype(f32) * real.astype(f32))
            den = jnp.sum(taylor, axis=1, keepdims=True)
            top = dot(taylor.astype(bf16), value[:nk, cols])
            attended[q0:nk, cols] = (top / den).astype(bf16)
            lane = lax.broadcasted_iota(jnp.int32, (tile, denom.shape[1]), 1)
            denom[q0:nk] = jnp.where(lane == h, den, denom[q0:nk])

    for h in range(heads):
        head(h)
        if h < cots.count:
            cots.relay(h)
    for h in range(heads, cots.count):
        cots.relay(h)
    place = lax.broadcasted_iota(jnp.int32, (bucket, 1), 0)
    weight = (place < length[...]).astype(f32) / (place.astype(f32) + 1.0)
    denom_t[...] = denom[...].T[: denom_t.shape[0]]
    den_row[...] = jnp.sum(denom[...] * weight, axis=0, keepdims=True)

    def arrive(j):
        cots.sib_in(j)
        cots.far_in(j)

    loop(cots.count, arrive)
    own_cot.wait()
    keep.wait()
    rows_out.drain()
    cots.drain()


def front_call(tokens, cotangent, gain, length, w_query, w_key, w_value, collective_id):
    own_rows, width = tokens.shape
    bucket = own_rows * lax.axis_size("tensor")
    values = w_value.shape[1]
    vm, hbm = pl.BlockSpec(memory_space=pltpu.VMEM), pl.BlockSpec(memory_space=pl.ANY)
    dma = lambda *shape: pltpu.SemaphoreType.DMA(shape)
    sds = jax.ShapeDtypeStruct
    return pl.pallas_call(
        front_kernel,
        out_shape=[
            sds((bucket, 128), bf16), sds((bucket, 128), bf16), sds((bucket, values), bf16),
            sds((bucket, values), bf16), sds((8, bucket), f32), sds((1, 128), f32),
            sds((bucket, width), bf16), sds((bucket, width), bf16),
        ],
        in_specs=[vm] * 7,
        out_specs=[vm] * 6 + [hbm] * 2,
        scratch_shapes=[
            pltpu.VMEM((bucket, 128), f32), pltpu.VMEM((bucket, width), bf16), pltpu.VMEM((own_rows, width), bf16), dma(2), dma(2, 3, 4), dma(2, 3, 4),
        ],
        compiler_params=pltpu.CompilerParams(
            collective_id=collective_id, has_side_effects=True, vmem_limit_bytes=48 << 20
        ),
        name="front",
    )(tokens, cotangent, gain, length, w_query, w_key, w_value)


def per_device(
    tokens,
    gain_attn,
    gain_mlp,
    w_query,
    w_key,
    w_value,
    w_out,
    w_gate,
    w_up,
    w_down,
    cotangent,
    lengths,
):
    groups = lax.axis_size("tensor")
    length = lax.dynamic_slice(lengths, (lax.axis_index("dp"),), (1,))[None]
    w_query_t, w_key_t, w_gate_t, w_up_t = w_query.T, w_key.T, w_gate.T, w_up.T
    query, key, value, attended, denom, den_row, normed_all, cot_all = front_call(
        tokens, cotangent, gain_attn[None], length, w_query_t, w_key_t, w_value, 1
    )
    small, output, _, _, down_total, gate_total, up_total, input_grad, out_total, value_total, qk_total = layer_call(
        attended, w_out, gain_mlp[None], gain_attn[None], length, denom, den_row, tokens, w_gate_t, w_up_t, w_down,
        cot_all, normed_all, query, key, value, w_query_t, w_key_t, w_value, 2,
    )
    quarter = w_query.shape[0] // 4
    gain_attn_total, gain_mlp_total = small[:4, :quarter].reshape(-1), small[4:, :quarter].reshape(-1)
    feat_width = w_query.shape[1]
    query_total, key_total = qk_total[:feat_width].T, qk_total[feat_width:].T
    gate_total, up_total = gate_total.T, up_total.T
    heads = feat_width // FEAT * groups
    den_mean = jnp.sum(small[0, quarter:]) / (heads * jnp.sum(lengths).astype(f32))
    return (
        output,
        input_grad,
        gain_attn_total,
        gain_mlp_total,
        query_total,
        key_total,
        value_total,
        out_total,
        gate_total,
        up_total,
        down_total,
        den_mean,
    )


def solution(mesh):
    return jax.shard_map(
        per_device,
        mesh=mesh,
        in_specs=(
            P(("dp", "tensor"), None),
            P(),
            P(),
            P(None, "tensor"),
            P(None, "tensor"),
            P(None, "tensor"),
            P("tensor", None),
            P(None, "tensor"),
            P(None, "tensor"),
            P("tensor", None),
            P(("dp", "tensor"), None),
            P(),
        ),
        out_specs=(
            P(("dp", "tensor"), None),
            P(("dp", "tensor"), None),
            P(),
            P(),
            P("dp", "tensor"),
            P("dp", "tensor"),
            P("dp", "tensor"),
            P("tensor", "dp"),
            P("dp", "tensor"),
            P("dp", "tensor"),
            P("tensor", "dp"),
            P(),
        ),
        check_vma=False,
    )
```

```python
import functools
import math

import jax
import jax.numpy as jnp
from jax import lax
from jax.experimental import pallas as pl
from jax.experimental.pallas import tpu as pltpu
from jax.sharding import PartitionSpec as P

FEAT = 16
MESH = pl.DeviceIdType.MESH
f32 = jnp.float32
bf16 = jnp.bfloat16
NT = (((1,), (1,)), ((), ()))
TN = (((0,), (0,)), ((), ()))
AHEAD = 4
LAG = 3
SETTLE = 3
STRIP = 16
VMEM_MB = 63


def dot(a, b, dims=(((1,), (0,)), ((), ()))):
    return lax.dot_general(a, b, dims, preferred_element_type=f32)


def loop(count, body):
    def step(i, carry):
        body(i)
        return carry

    lax.fori_loop(0, count, step, 0)


def pieces(width, size):
    return [(start, min(size, width - start)) for start in range(0, width, size)]


class Group:
    def __init__(self):
        self.dp = lax.axis_index("dp")
        self.t = lax.axis_index("tensor")
        self.y, self.c = self.t // 2, lax.rem(self.t, 2)
        self.sibling = (self.dp, self.y * 2 + 1 - self.c)
        self.across = (self.dp, (1 - self.y) * 2 + self.c)


def remote(src, dst, send, recv, device):
    return pltpu.make_async_remote_copy(src, dst, send, recv, device_id=device, device_id_type=MESH)


class RowSums:
    def __init__(self, g, own_rows, phase, chunk, part, bufs, sems, piece=512):
        self.piece = piece
        self.g, self.own, self.p, self.chunk, self.part = g, own_rows, phase, chunk, part
        self.sibsend, self.sibrecv, self.ysend, self.yrecv, self.total = bufs
        self.sib_s, self.sib_r, self.y_s, self.y_r = sems
        self.count = own_rows // chunk

    def at(self, j):
        return pl.ds(pl.multiple_of(j * self.chunk, self.chunk), self.chunk)

    def rows(self, y, c, j):
        return pl.ds(pl.multiple_of((y * 2 + c) * self.own + j * self.chunk, self.chunk), self.chunk)

    def sib(self, far, j):
        return remote(
            self.sibsend.at[far, self.at(j)], self.sibrecv.at[far, self.at(j)],
            self.sib_s.at[self.p, far, j], self.sib_r.at[self.p, far, j], self.g.sibling,
        )

    def ycopy(self, j):
        return remote(
            self.ysend.at[self.at(j)], self.yrecv.at[self.at(j)],
            self.y_s.at[self.p, j], self.y_r.at[self.p, j], self.g.across,
        )

    def give(self, far, j):
        y = 1 - self.g.y if far else self.g.y
        for n, w in pieces(self.total.shape[1], self.piece):
            self.sibsend[far, self.at(j), n : n + w] = self.part(self.rows(y, 1 - self.g.c, j), n, w).astype(bf16)
        self.sib(far, j).start()

    def send(self, j):
        g = self.g
        for n, w in pieces(self.total.shape[1], self.piece):
            self.total[self.at(j), n : n + w] = self.part(self.rows(1 - g.y, g.c, j), n, w)
        self.sib(1, j).wait_recv()
        self.ysend[self.at(j)] = (self.total[self.at(j)] + self.sibrecv[1, self.at(j)].astype(f32)).astype(bf16)
        self.ycopy(j).start()

    def hold(self, j):
        for n, w in pieces(self.total.shape[1], self.piece):
            self.total[self.at(j), n : n + w] = self.part(self.rows(self.g.y, self.g.c, j), n, w)

    def finish(self, j, use):
        self.sib(0, j).wait_recv()
        self.ycopy(j).wait_recv()

        def strip(i):
            r = pl.ds(pl.multiple_of(j * self.chunk + i * STRIP, STRIP), STRIP)
            use(r, self.total[r] + self.sibrecv[0, r].astype(f32) + self.yrecv[r].astype(f32))

        loop(self.chunk // STRIP, strip)

    def drain(self):
        def body(j):
            self.sib(0, j).wait_send()
            self.sib(1, j).wait_send()
            self.ycopy(j).wait_send()

        loop(self.count, body)


class Spread:
    def __init__(self, g, own_rows, chunk, src, full, sems, phase):
        self.g, self.own, self.chunk, self.src, self.full, self.p = g, own_rows, chunk, src, full, phase
        self.s, self.r = sems
        self.count = own_rows // chunk

    def rows(self, y, c, j):
        return pl.ds(pl.multiple_of((y * 2 + c) * self.own + j * self.chunk, self.chunk), self.chunk)

    def copy(self, kind, j):
        g = self.g
        rows = self.rows(g.y, g.c, j)
        if kind == 2:
            rows = self.rows(1 - g.y, g.c, j)
            src = self.full.at[rows]
        elif self.src is None:
            src = self.full.at[rows]
        else:
            src = self.src.at[pl.ds(pl.multiple_of(j * self.chunk, self.chunk), self.chunk)]
        return remote(
            src, self.full.at[rows], self.s.at[self.p, kind, j], self.r.at[self.p, kind, j],
            g.across if kind == 1 else g.sibling,
        )

    def start(self, j):
        self.copy(1, j).start()
        self.copy(0, j).start()

    def relay(self, j):
        self.copy(1, j).wait_recv()
        self.copy(2, j).start()

    def sib_in(self, j):
        self.copy(0, j).wait_recv()

    def far_in(self, j):
        self.copy(2, j).wait_recv()

    def drain(self):
        def body(j):
            for kind in range(3):
                self.copy(kind, j).wait_send()

        loop(self.count, body)


class WeightSums:
    def __init__(self, g, dp_size, rows, weights, widths, write, refs, sems, emit):
        self.g, self.rows, self.widths, self.write, self.emit = g, rows, widths, write, emit
        self.weights = weights
        self.nz = dp_size // 2
        self.z, self.x = g.dp // 2, lax.rem(g.dp, 2)
        self.halves = max(1, rows // 128)
        self.rn = rows // self.halves
        self.ring = self.zs_slots(self.nz)
        self.jobs = weights * self.halves - 1
        self.steps = self.jobs * self.nz
        (self.xs, self.zs, self.acc, self.xtmp, self.ztmp, self.xrecv, self.zrecv,
         self.zf, self.zfx, self.facc, self.frecv, self.fxrecv) = refs
        (self.xs_s, self.xr_s, self.zs_s, self.zr_s, self.loc, self.zf_s, self.zf_r, self.fx_s, self.fx_r) = sems
        self.ahead = self.xs.shape[0]
        self.gap = max(1, (self.steps - 8) // self.nz)
        self.partner = (self.z * 2 + 1 - self.x, g.t)

    @staticmethod
    def zs_slots(nz):
        return 2 * nz if nz <= 4 else nz

    def job(self, s):
        lin = s // self.nz + 1
        return lin // self.halves, lax.rem(lin, self.halves)

    def by_kind(self, allowed, s, body):
        i, _ = self.job(s)

        @pl.when(allowed & (i < self.weights - 1))
        def _():
            body(s, 0)

        @pl.when(allowed & (i == self.weights - 1))
        def _():
            body(s, 1)

    def order(self, k):
        last = self.nz - 1
        upper = self.z >= self.nz // 2
        z = jnp.where(upper, last - self.z, self.z)
        zt = jnp.where(k < last - z, last - k, jnp.where(k < last, last - 1 - k, z))
        return jnp.where(upper, last - zt, zt)

    def coming(self, zt):
        return jnp.where(zt > self.z, self.z > 0, self.z < self.nz - 1)

    def towards(self, zt):
        return (jnp.where(zt > self.z, self.z + 1, self.z - 1) * 2 + self.x, self.g.t)

    def slot(self, zt):
        return jnp.where(zt == self.z - 1, self.nz, zt)

    def part(self, ref, index, kind):
        return ref.at[index] if kind == 0 else ref.at[index, :, pl.ds(0, self.widths[1])]

    def small(self, ref, kind):
        return ref.at[pl.ds(0, self.rn)] if kind == 0 else ref.at[pl.ds(0, self.rn), pl.ds(0, self.widths[1])]

    def xcopy(self, s, kind):
        slot = lax.rem(s, self.ahead)
        return remote(
            self.part(self.xs, slot, kind), self.part(self.xrecv, s, kind), self.xs_s.at[slot], self.xr_s.at[s],
            self.partner,
        )

    def zcopy(self, s, zt, kind):
        ring = lax.rem(s, self.ring)
        j = s // self.nz * (self.nz + 1) + self.slot(zt)
        return remote(
            self.part(self.zs, ring, kind), self.part(self.zrecv, j, kind), self.zs_s.at[ring], self.zr_s.at[j],
            self.towards(zt),
        )

    def zwait(self, j, kind):
        remote(
            self.part(self.zs, 0, kind), self.part(self.zrecv, j, kind), self.zs_s.at[0], self.zr_s.at[j],
            self.partner,
        ).wait_recv()

    def fetch(self, src, dst, k):
        copy = pltpu.make_async_copy(src, dst, self.loc.at[k])
        copy.start()
        return copy

    def xsend(self, s, kind):
        self.by_kind(s >= self.ahead, s - self.ahead, lambda a, old: self.xcopy(a, old).wait_send())
        i, h = self.job(s)
        slot = lax.rem(s, self.ahead)

        def store(n, w, value):
            self.xs[slot, :, n : n + w] = value.astype(bf16)

        self.write(store, kind, i, self.order(lax.rem(s, self.nz)), 1 - self.x, h)
        self.xcopy(s, kind).start()

    def zsent(self, s):
        k = lax.rem(s, self.nz)
        self.by_kind(
            (s >= 0) & (k < self.nz - 1), s, lambda a, old: self.zcopy(a, self.order(k), old).wait_send()
        )

    def xstep(self, s, kind):
        w = self.widths[kind]
        k = lax.rem(s, self.nz)
        zt = self.order(k)
        i, h = self.job(s)
        self.xcopy(s, kind).wait_recv()
        copy = self.fetch(self.part(self.xrecv, s, kind), self.small(self.xtmp, kind), 0)
        slot = lax.rem(s // self.nz, 2)
        ring = lax.rem(s, self.ring)
        self.zsent(s - self.ring)

        def store(n, w, value):
            self.acc[slot, :, n : n + w] = value

        self.write(store, kind, i, zt, self.x, h)
        copy.wait()
        total = self.acc[slot, :, :w] + self.xtmp[:, :w].astype(f32)

        @pl.when(k == self.nz - 1)
        def _():
            self.acc[slot, :, :w] = total

        @pl.when(k < self.nz - 1)
        def _():
            self.zs[ring, :, :w] = total.astype(bf16)

            @pl.when(jnp.logical_not(self.coming(zt)))
            def _():
                self.zcopy(s, zt, kind).start()

    def zstep(self, s, kind):
        w = self.widths[kind]
        k = lax.rem(s, self.nz)
        zt = self.order(k)
        ring = lax.rem(s, self.ring)

        @pl.when((k < self.nz - 1) & self.coming(zt))
        def _():
            j = s // self.nz * (self.nz + 1) + zt
            self.zwait(j, kind)
            self.fetch(self.part(self.zrecv, j, kind), self.small(self.ztmp, kind), 1).wait()
            self.zs[ring, :, :w] = (
                self.zs[ring, :, :w].astype(f32) + self.ztmp[: self.rn, :w].astype(f32)
            ).astype(bf16)
            self.zcopy(s, zt, kind).start()

    def final(self, s, kind):
        w = self.widths[kind]
        jx = s // self.nz
        slot = lax.rem(jx, 2)

        def take(j):
            self.zwait(j, kind)
            self.fetch(self.part(self.zrecv, j, kind), self.small(self.ztmp, kind), 1).wait()
            self.acc[slot, :, :w] += self.ztmp[: self.rn, :w].astype(f32)

        @pl.when(self.z > 0)
        def _():
            take(jx * (self.nz + 1) + self.z)

        @pl.when(self.z < self.nz - 1)
        def _():
            take(jx * (self.nz + 1) + self.nz)

        i, h = self.job(s)
        self.emit(kind, i, h, self.acc.at[slot])

    def fcopy(self, q, zt):
        slot = self.slot(zt)
        return remote(self.zf.at[q], self.frecv.at[slot], self.zf_s.at[q], self.zf_r.at[slot], self.towards(zt))

    def fwait(self, slot):
        remote(self.zf.at[0], self.frecv.at[slot], self.zf_s.at[0], self.zf_r.at[slot], self.partner).wait_recv()

    def fstart(self, q):
        zt = self.order(q)
        for xt in range(2):

            def store(n, w, value):
                self.zf[q, xt * self.rn : (xt + 1) * self.rn, n : n + w] = value.astype(bf16)

            self.write(store, 0, 0, zt, xt, 0)

        @pl.when(jnp.logical_not(self.coming(zt)))
        def _():
            self.fcopy(q, zt).start()

    def fstep(self, q):
        zt = self.order(q)

        @pl.when(self.coming(zt))
        def _():
            self.fwait(zt)
            self.fetch(self.frecv.at[zt], self.ztmp, 1).wait()
            self.zf[q] = (self.zf[q].astype(f32) + self.ztmp[...].astype(f32)).astype(bf16)
            self.fcopy(q, zt).start()

    def fxcopy(self):
        return remote(self.zfx, self.fxrecv, self.fx_s.at[0], self.fx_r.at[0], self.partner)

    def fend(self):
        for xt in range(2):

            def store(n, w, value):
                self.facc[xt * self.rn : (xt + 1) * self.rn, n : n + w] = value

            self.write(store, 0, 0, self.z, xt, 0)

        def take(slot):
            self.fwait(slot)
            self.fetch(self.frecv.at[slot], self.ztmp, 1).wait()
            self.facc[...] += self.ztmp[...].astype(f32)

        @pl.when(self.z > 0)
        def _():
            take(self.z)

        @pl.when(self.z < self.nz - 1)
        def _():
            take(self.nz)

        away = pl.ds(pl.multiple_of((1 - self.x) * self.rn, self.rn), self.rn)
        self.zfx[...] = self.facc[away].astype(bf16)
        self.fxcopy().start()

    def ffinal(self):
        self.fxcopy().wait_recv()
        self.fetch(self.fxrecv, self.xtmp, 1).wait()
        own = pl.ds(pl.multiple_of(self.x * self.rn, self.rn), self.rn)
        self.facc[own] += self.xtmp[...].astype(f32)
        self.emit(0, 0, 0, self.facc.at[own])

    def begin(self):
        loop(self.ahead, lambda s: self.xsend(s, 0))

    def services(self):
        return max(self.steps + SETTLE + 1, self.gap * (self.nz - 1) + 9)

    def service(self, s):
        self.by_kind(s < self.steps, s, self.xstep)
        self.by_kind(s + self.ahead < self.steps, s + self.ahead, self.xsend)
        self.by_kind((s >= LAG) & (s - LAG < self.steps), s - LAG, self.zstep)

        @pl.when((s >= 1) & (lax.rem(s - 1, self.gap) == 0) & ((s - 1) // self.gap < self.nz - 1))
        def _():
            self.fstart((s - 1) // self.gap)

        @pl.when((s >= 4) & (lax.rem(s - 4, self.gap) == 0) & ((s - 4) // self.gap < self.nz - 1))
        def _():
            self.fstep((s - 4) // self.gap)

        @pl.when(s == self.gap * (self.nz - 1) + 4)
        def _():
            self.fend()

        @pl.when(s == self.gap * (self.nz - 1) + 8)
        def _():
            self.ffinal()

        due = (s >= self.nz + SETTLE) & (lax.rem(s - SETTLE, self.nz) == 0) & (s - SETTLE <= self.steps)
        self.by_kind(due, s - SETTLE - self.nz, self.final)

    def drain(self):
        loop(
            self.ahead,
            lambda a: self.by_kind(
                a >= 0, self.steps - self.ahead + a, lambda s, kind: self.xcopy(s, kind).wait_send()
            ),
        )
        loop(self.ring, lambda a: self.zsent(self.steps - self.ring + a))
        loop(self.nz - 1, lambda q: self.fcopy(q, self.order(q)).wait_send())
        self.fxcopy().wait_send()


def meet(g, nz, every=False):
    if nz == 0:
        barrier = pltpu.get_barrier_semaphore()
        for device in (g.sibling, g.across):
            pl.semaphore_signal(barrier, inc=1, device_id=device, device_id_type=MESH)
        pl.semaphore_wait(barrier, 2)
        return
    z, x = g.dp // 2, lax.rem(g.dp, 2)
    barrier = pltpu.get_barrier_semaphore()

    def hello(device):
        pl.semaphore_signal(barrier, inc=1, device_id=device, device_id_type=MESH)

    hello(g.sibling)
    hello(g.across)
    hello((z * 2 + 1 - x, g.t))
    if every:
        loop(nz - 1, lambda k: hello((lax.rem(z + 1 + k, nz) * 2 + x, g.t)))
        pl.semaphore_wait(barrier, nz + 2)
        return

    @pl.when(z > 0)
    def _():
        hello(((z - 1) * 2 + x, g.t))

    @pl.when(z < nz - 1)
    def _():
        hello(((z + 1) * 2 + x, g.t))

    peers = 5 - jnp.where(z == 0, 1, 0) - jnp.where(z == nz - 1, 1, 0)
    pl.semaphore_wait(barrier, peers)


def owner_dot(load, right, rows, zt, xt, h):
    if rows % 128:
        both = dot(load(pl.ds(pl.multiple_of(zt * (2 * rows), 2 * rows), 2 * rows)), right, TN)
        return jnp.where(xt == 0, both[:rows], both[rows:])
    rn = min(rows, 128)
    return dot(load(pl.ds(pl.multiple_of((zt * 2 + xt) * rows + h * rn, rn), rn)), right, TN)


def head_lanes(h, feat, width):
    return (lax.broadcasted_iota(jnp.int32, (1, width), 1) // feat == h).astype(f32).astype(bf16)


def norm_parts(state):
    scale = lax.rsqrt(jnp.mean(state * state, axis=-1, keepdims=True) + 1e-06)
    return state * scale, scale


def layer_kernel(
    dp_size,
    gain, gain_attn, length, den_row,
    attended_h, w_out_h, denom_h, tokens_h, w_gate_h, w_up_h, w_down_h, cot_h, normed_h, query_h, key_h, value_h, w_query_h, w_key_h, w_value_h,
    small_out, output_h, state_grad_h, state_all_h, down_h, gate_h, up_h, input_grad_h, out_h, value_grad_h, qk_h,
    xrecv, zrecv, frecv, fxrecv,
    w_gate, w_up, w_down, lefts, rights, mid, sibsend, sibrecv, ysend, yrecv, total, spread_buf,
    xs, zs, zf, zfx, acc, facc, xtmp, ztmp, turn,
    attended, w_out, denom, grad_den, gk_acc, gq_acc, gain_grad, gain_acc, smalls, small_got, small_z,
    load_sem, sib_s, sib_r, y_s, y_r, ag_s, ag_r,
    xs_s, xr_s, zs_s, zr_s, zf_s, zf_r, fx_s, fx_r, loc, sm_s, sm_r, smz_s, smz_r, ready,
):
    g = Group()
    own_rows, width = tokens_h.shape
    tokens = spread_buf
    hidden_units = rights.shape[2]
    rows = width // dp_size
    loads = [
        pltpu.make_async_copy(src, dst, load_sem.at[n])
        for n, (src, dst) in enumerate(
            [(w_gate_h, w_gate), (w_up_h, w_up), (w_down_h, w_down), (cot_h, lefts.at[0]), (tokens_h, tokens),
             (attended_h, attended), (w_out_h, w_out), (denom_h, denom)]
        )
    ]
    for copy in loads[5:] + loads[:5]:
        copy.start()
    nz = dp_size // 2
    meet(g, nz, every=True)
    for copy in loads[5:]:
        copy.wait()
    bufs = (sibsend, sibrecv, ysend, yrecv, total)
    sems = (sib_s, sib_r, y_s, y_r)

    def attn_part(r, n, w):
        return dot(attended[r], w_out[:, n : n + w])

    sums = RowSums(g, own_rows, 0, 64, attn_part, bufs, sems)
    normed = Spread(g, own_rows, 64, None, lefts.at[1], (ag_s, ag_r), 0)
    own_first = pl.multiple_of(g.t * own_rows, own_rows)

    def first_state(r, summed):
        state = tokens[r].astype(f32) + summed
        mid[r] = state
        normal, _ = norm_parts(state)
        start = pl.multiple_of(own_first + r.start, STRIP)
        lefts[1, pl.ds(start, STRIP)] = (normal * gain[...]).astype(bf16)

    sums.give(1, 0)

    def far(j):
        @pl.when(j + 1 < sums.count)
        def _():
            sums.give(1, j + 1)

        sums.send(j)

    loop(sums.count, far)

    def near(j):
        sums.give(0, j)
        sums.hold(j)

    loop(sums.count, near)

    def feed(y, c, half):
        r = pl.ds(pl.multiple_of((y * 2 + c) * own_rows + half * 128, 128), 128)
        for n, w in pieces(hidden_units, 512):
            gate = dot(lefts[1, r], w_gate[n : n + w], NT)
            up = dot(lefts[1, r], w_up[n : n + w], NT)
            back = dot(lefts[0, r], w_down[n : n + w], NT)
            sig = jax.nn.sigmoid(gate)
            active = gate * sig
            rights[0, r, n : n + w] = (active * up).astype(bf16)
            rights[1, r, n : n + w] = (back * up * sig * (1.0 + gate * (1.0 - sig))).astype(bf16)
            rights[2, r, n : n + w] = (back * active).astype(bf16)

    def close(j):
        sums.finish(j, first_state)
        normed.start(j)

    loads[4].wait()

    def half_near(half):
        loop(2, lambda a: close(half * 2 + a))

        @pl.when(half == 0)
        def _():
            for copy in loads[:4]:
                copy.wait()

        feed(g.y, g.c, half)
        loop(2, lambda a: normed.sib_in(half * 2 + a))
        feed(g.y, 1 - g.c, half)

    loop(2, half_near)

    def half_far(half):
        loop(2, lambda a: normed.relay(half * 2 + a))
        feed(1 - g.y, g.c, half)
        loop(2, lambda a: normed.far_in(half * 2 + a))
        feed(1 - g.y, 1 - g.c, half)

    loop(2, half_far)
    sums.drain()

    bucket, values = attended.shape
    head_width, feat_pad = 128, 128
    heads = values // head_width
    feat_width = w_query_h.shape[0]
    feat = feat_width // heads
    halves = max(1, rows // 128)
    rn = rows // halves
    grads_at, value_at, sums_at = 0, values, 2 * values
    query_at = sums_at + values + 2 * feat_width
    key_at = query_at + feat_pad
    sums_end = query_at
    kept_query, kept_key, turned_key = bucket, bucket + feat_width, bucket + 2 * feat_width

    def write(store, kind, i, zt, xt, h):
        if kind == 0:
            left = jnp.minimum(i, 1)
            store(0, hidden_units, owner_dot(lambda cols: lefts[left, :, cols], rights[i], rows, zt, xt, h))
            return
        store(0, values, owner_dot(lambda cols: w_gate[:bucket, cols], attended[...], rows, zt, xt, h))
        store(
            values, sums_end - sums_at,
            owner_dot(lambda cols: w_up[:bucket, cols], w_down[:bucket, sums_at:sums_end], rows, zt, xt, h),
        )

    def put(src, out, n, w, h):
        to = out.at[pl.ds(n, w)]
        if halves > 1:
            to = out.at[pl.ds(n, w), pl.ds(pl.multiple_of(h * rn, rn), rn)]
        copy = pltpu.make_async_copy(src.at[pl.ds(0, w)], to, loc.at[2])
        copy.start()
        copy.wait()

    def emit(kind, i, h, block):
        if kind == 0:
            for n, w in pieces(hidden_units, 512):
                turn[:w] = block[:, n : n + w].T
                for m, out in enumerate((down_h, gate_h, up_h)):
                    pl.when(i == m)(functools.partial(put, turn, out, n, w, h))
            return
        for n, w in pieces(values, 512):
            turn[:w] = block[:, n : n + w].T
            put(turn, out_h, n, w, h)
        copy = pltpu.make_async_copy(
            block.at[:, pl.ds(values, values)], value_grad_h.at[pl.ds(pl.multiple_of(h * rn, rn), rn)], loc.at[2]
        )
        copy.start()
        turn[: 2 * feat_width] = block[:, 2 * values : 2 * values + 2 * feat_width].T
        copy.wait()
        put(turn, qk_h, 0, 2 * feat_width, h)

    engine = WeightSums(
        g, dp_size, rows, 4, (hidden_units, 2 * values + 2 * feat_width), write,
        (xs, zs, acc, xtmp, ztmp, xrecv, zrecv, zf, zfx, facc, frecv, fxrecv),
        (xs_s, xr_s, zs_s, zr_s, loc, zf_s, zf_r, fx_s, fx_r), emit,
    )
    engine.begin()

    def back_part(r, n, w):
        return dot(rights[1, r], w_gate[:, n : n + w]) + dot(rights[2, r], w_up[:, n : n + w])

    sums = RowSums(g, own_rows, 1, 128, back_part, bufs, sems)
    states = Spread(g, own_rows, 128, spread_buf, state_all_h, (ag_s, ag_r), 1)
    gain_grad[...] = jnp.zeros_like(gain_grad)

    def state_back(r, grad):
        normal, scale = norm_parts(mid[r])
        weighted = grad * gain[...]
        start = pl.multiple_of(own_first + r.start, STRIP)
        change = scale * (weighted - normal * jnp.mean(weighted * normal, axis=-1, keepdims=True))
        state = lefts[0, pl.ds(start, STRIP)].astype(f32) + change
        gain_grad[...] += jnp.sum(grad * normal, axis=0, keepdims=True)
        total[r] = state
        spread_buf[r] = state.astype(bf16)

    def far_back(j):
        sums.give(1, j)
        sums.send(j)

    loop(sums.count, far_back)

    def near_back(j):
        sums.give(0, j)
        engine.service(2 * j)
        sums.hold(j)
        engine.service(2 * j + 1)

    loop(sums.count, near_back)
    used = 2 * sums.count

    def own_copy(j):
        r = pl.ds(pl.multiple_of(j * 128, 128), 128)
        to = pl.ds(pl.multiple_of(own_first + j * 128, 128), 128)
        return (
            pltpu.make_async_copy(total.at[r], state_grad_h.at[r], load_sem.at[0]),
            pltpu.make_async_copy(spread_buf.at[r], state_all_h.at[to], load_sem.at[1]),
        )

    def close_back(j):
        sums.finish(j, state_back)
        states.start(j)
        copies = own_copy(j)
        for copy in copies:
            copy.start()
        engine.service(used + j)
        for copy in copies:
            copy.wait()

    loop(sums.count, close_back)
    used = used + sums.count

    def pass_back(j):
        states.relay(j)
        engine.service(used + j)

    loop(sums.count, pass_back)
    used = used + sums.count

    def arrive(j):
        states.sib_in(j)
        states.far_in(j)

    loop(sums.count, arrive)
    sums.drain()

    def down_part(r, n, w):
        return dot(rights[0, r], w_down[:, n : n + w])

    sums = RowSums(g, own_rows, 2, 128, down_part, bufs, sems)

    def far_down(j):
        sums.give(1, j)
        sums.send(j)
        engine.service(used + j)

    loop(sums.count, far_down)
    used = used + sums.count

    def near_down(j):
        sums.give(0, j)
        sums.hold(j)

    loop(sums.count, near_down)

    fetches = [
        (state_all_h, w_gate.at[pl.ds(0, bucket)]), (normed_h, w_up.at[pl.ds(0, bucket)]),
        (value_h, w_down.at[pl.ds(0, bucket), pl.ds(value_at, values)]),
        (query_h, w_down.at[pl.ds(0, bucket), pl.ds(query_at, feat_pad)]),
        (key_h, w_down.at[pl.ds(0, bucket), pl.ds(key_at, feat_pad)]),
        (w_query_h, w_down.at[pl.ds(kept_query, feat_width)]), (w_key_h, w_down.at[pl.ds(kept_key, feat_width)]),
    ]
    span = 256
    chunks = [(width // span // 2, w_gate), (width // span // 2, w_up)]
    row = 0
    for count, home in chunks:
        for m in range(count):
            fetches.append(
                (w_value_h.at[pl.ds(row, span)], home.at[pl.ds(bucket, span), pl.ds(m * values, values)])
            )
            row += span
    fetches = [pltpu.make_async_copy(src, dst, load_sem.at[n]) for n, (src, dst) in enumerate(fetches)]
    for copy in fetches:
        copy.start()
    for copy in fetches:
        copy.wait()
    w_down[turned_key : turned_key + feat_pad, :bucket] = (
        w_down[:bucket, key_at : key_at + feat_pad].astype(f32).T.astype(bf16)
    )

    def spread_grad(b):
        r = pl.ds(pl.multiple_of(b * 128, 128), 128)
        grad = dot(w_gate[r], w_out[...], NT).astype(bf16).astype(f32)
        lane = lax.broadcasted_iota(jnp.int32, (128, 128), 1)
        dens = jnp.zeros((128, 128), f32)
        turned_den = denom[:, r].T
        for h in range(heads):
            cols = slice(h * head_width, (h + 1) * head_width)
            den = turned_den[:, h : h + 1]
            piece = grad[:, cols]
            w_down[r, grads_at + h * head_width : grads_at + (h + 1) * head_width] = (piece / den).astype(bf16)
            back = -jnp.sum(piece * attended[r, cols].astype(f32), axis=1, keepdims=True) / den
            dens = jnp.where(lane == h, back, dens)
        grad_den[:, r] = dens.T[: grad_den.shape[0]]

    loop(bucket // 128, spread_grad)
    engine.service(used)
    used = used + 1
    states.drain()

    def last_state(r, summed):
        position = own_first + r.start + lax.broadcasted_iota(jnp.int32, (STRIP, 1), 0)
        valid = (position < length[...]).astype(f32)
        spread_buf[r] = (valid * (mid[r] + summed)).astype(bf16)

    loop(sums.count, lambda j: sums.finish(j, last_state))
    pl.semaphore_signal(ready.at[0], inc=1, device_id=g.sibling, device_id_type=MESH)
    pl.semaphore_signal(ready.at[1], inc=1, device_id=g.across, device_id_type=MESH)
    keep = pltpu.make_async_copy(spread_buf, output_h, loc.at[2])
    keep.start()
    keep.wait()
    refills = [
        pltpu.make_async_copy(tokens_h, tokens, load_sem.at[15]),
        pltpu.make_async_copy(state_grad_h, mid, load_sem.at[16]),
    ]
    for copy in refills:
        copy.start()
    engine.service(used)
    used = used + 1
    gk_acc[...] = jnp.zeros_like(gk_acc)
    gq_acc[...] = jnp.zeros_like(gq_acc)
    total[...] = jnp.zeros_like(total)
    qk_scale = 1.0 / math.sqrt(feat)
    tile = 256

    def head(h):
        lanes = head_lanes(h, feat, feat_pad)
        sub = (lax.broadcasted_iota(jnp.int32, (feat_pad, 1), 0) // feat == h).astype(f32).astype(bf16)
        offset = pl.multiple_of(h * head_width, head_width)
        for qb in range(bucket // tile):
            q0, nk = qb * tile, (qb + 1) * tile
            q_own = w_down[q0:nk, query_at : query_at + feat_pad] * lanes
            grads = w_down[q0:nk, pl.ds(grads_at + offset, head_width)]
            for k0, count in pieces(nk, 2 * tile):
                keys = slice(k0, k0 + count)
                kept = w_down[turned_key : turned_key + feat_pad, keys] * sub
                scores = dot(w_down[keys, key_at : key_at + feat_pad], q_own, NT) * qk_scale
                spot = k0 + lax.broadcasted_iota(jnp.int32, (count, tile), 0)
                below = spot <= q0 + lax.broadcasted_iota(jnp.int32, (count, tile), 1)
                real = k0 + lax.broadcasted_iota(jnp.int32, (count, 1), 0) < length[...]
                mask = below.astype(f32) * real.astype(f32)
                taylor = (1.0 + scores + 0.5 * scores * scores) * mask
                moved = dot(taylor.astype(bf16), grads)
                for kb in range(count // tile):
                    at = (k0 // tile + kb) * values
                    total[:, pl.ds(at + offset, head_width)] += moved[kb * tile : (kb + 1) * tile]
                back = dot(w_down[keys, pl.ds(value_at + offset, head_width)], grads, NT)
                back = back + grad_den[pl.ds(h, 1), q0:nk]
                low = (back * mask * (1.0 + scores)).astype(bf16)
                gk_acc[keys] += dot(low, q_own)
                gq_acc[:, q0:nk] += dot(kept, low)

        @pl.when(lax.rem(h, 2) == 1)
        def _():
            engine.service(used + h // 2)

    loop(heads, head)
    used = used + heads // 2
    for kb in range(bucket // tile):
        r = slice(kb * tile, (kb + 1) * tile)
        w_down[r, sums_at : sums_at + values] = total[:, kb * values : (kb + 1) * values].astype(bf16)
        pair = jnp.concatenate([gq_acc[:feat_width, r].T, gk_acc[r, :feat_width]], axis=1) * qk_scale
        w_down[r, sums_at + values : sums_end] = pair.astype(bf16)
    sums.drain()

    def attn_back_part(r, n, w):
        count, home = chunks[0] if n < width // 2 else chunks[1]
        m = n // span % count
        out = dot(
            w_down[r, sums_at : sums_at + values], home[bucket : bucket + span, m * values : (m + 1) * values], NT
        )
        out = out + dot(
            w_down[r, sums_at + values : sums_end], w_down[kept_query : kept_query + 2 * feat_width, n : n + w]
        )
        return out

    sums = RowSums(g, own_rows, 3, 128, attn_back_part, bufs, sems, span)
    pl.semaphore_wait(ready.at[0], 1)
    pl.semaphore_wait(ready.at[1], 1)

    def far_last(j):
        sums.give(1, j)
        sums.send(j)
        engine.service(used + j)

    loop(sums.count, far_last)
    used = used + sums.count

    def near_last(j):
        sums.give(0, j)
        sums.hold(j)
        engine.service(used + j)

    loop(sums.count, near_last)
    used = used + sums.count
    gain_acc[...] = jnp.zeros_like(gain_acc)
    for copy in refills:
        copy.wait()

    def input_back(r, grad):
        normal, inv = norm_parts(tokens[r].astype(f32))
        weighted = grad * gain_attn[...]
        change = inv * (weighted - normal * jnp.mean(weighted * normal, axis=-1, keepdims=True))
        gain_acc[...] += jnp.sum(grad * normal, axis=0, keepdims=True)
        mid[r] += change

    def close_last(j):
        sums.finish(j, input_back)
        engine.service(used + j)

    loop(sums.count, close_last)
    used = used + sums.count
    result = pltpu.make_async_copy(mid, input_grad_h, load_sem.at[0])
    result.start()

    smalls[0] = jnp.zeros(smalls.shape[1:], f32)
    quarter = width // 4
    for m in range(4):
        smalls[0, m : m + 1, :quarter] = gain_acc[:, m * quarter : (m + 1) * quarter]
        smalls[0, 4 + m : 5 + m, :quarter] = gain_grad[:, m * quarter : (m + 1) * quarter]
    smalls[0, 0:1, quarter:] = den_row[...]
    z, x = engine.z, engine.x
    peers = (g.sibling, g.across, engine.partner)
    for n, device in enumerate(peers):
        copy = remote(smalls.at[n], small_got.at[n], sm_s.at[n], sm_r.at[n], device)
        copy.start()
        engine.service(used + n)
        copy.wait()
        smalls[n + 1] = smalls[n] + small_got[n]
    used = used + len(peers)

    def zsmall(k):
        return remote(
            smalls.at[3], small_z.at[z], smz_s.at[k], smz_r.at[k], (lax.rem(z + 1 + k, nz) * 2 + x, g.t)
        )

    loop(nz - 1, lambda k: zsmall(k).start())
    loop(engine.services() - used, lambda n: engine.service(used + n))
    small_z[z] = smalls[3]

    def zgot(k):
        remote(
            smalls.at[3], small_z.at[lax.rem(z - 1 - k + nz, nz)], smz_s.at[k], smz_r.at[k], g.sibling
        ).wait_recv()

    loop(nz - 1, zgot)
    small_out[...] = jnp.zeros_like(small_out)

    def zadd(k):
        small_out[...] += small_z[k]

    loop(nz, zadd)
    loop(nz - 1, lambda k: zsmall(k).wait_send())
    result.wait()
    sums.drain()
    normed.drain()
    engine.drain()


def layer_call(
    attended, w_out, gain, gain_attn, length, denom, den_row, tokens, w_gate, w_up, w_down, cot_all,
    normed, query, key, value, w_query, w_key, w_value, collective_id,
):
    dp_size = lax.axis_size("dp")
    nz = dp_size // 2
    own_rows, width = tokens.shape
    bucket, values = attended.shape
    units = w_down.shape[0]
    feat_width = w_query.shape[0]
    small = (8, width // 4 + den_row.shape[1])
    rows = width // dp_size
    halves = max(1, rows // 128)
    rn = rows // halves
    jobs = 4 * halves - 1
    steps = jobs * nz
    ring = WeightSums.zs_slots(nz)
    vm, hbm = pl.BlockSpec(memory_space=pltpu.VMEM), pl.BlockSpec(memory_space=pl.ANY)
    dma = lambda *shape: pltpu.SemaphoreType.DMA(shape)
    vmem = lambda shape, kind=bf16: pltpu.VMEM(shape, kind)
    sds = jax.ShapeDtypeStruct
    outs = pl.pallas_call(
        functools.partial(layer_kernel, dp_size),
        out_shape=[
            sds(small, f32),
            sds((own_rows, width), bf16),
            sds((own_rows, width), f32),
            sds((bucket, width), bf16),
            *[sds((units, rows), f32)] * 3,
            sds((own_rows, width), f32),
            sds((values, rows), f32),
            sds((rows, values), f32),
            sds((2 * feat_width, rows), f32),
            sds((steps, rn, units), bf16),
            sds((jobs * (nz + 1), rn, units), bf16),
            sds((nz + 1, 2 * rn, units), bf16),
            sds((rn, units), bf16),
        ],
        in_specs=[vm] * 4 + [hbm] * 15,
        out_specs=[vm] + [hbm] * 14,
        scratch_shapes=[
            vmem((units, width)), vmem((units, width)), vmem((units, width)),
            vmem((2, bucket, width)), vmem((3, bucket, units)), vmem((own_rows, width), f32),
            vmem((2, own_rows, width)), vmem((2, own_rows, width)), vmem((own_rows, width)), vmem((own_rows, width)),
            vmem((own_rows, width), f32), vmem((own_rows, width)),
            vmem((AHEAD, rn, units)), vmem((ring, rn, units)), vmem((nz - 1, 2 * rn, units)), vmem((rn, units)),
            vmem((2, rn, units), f32), vmem((2 * rn, units), f32), vmem((rn, units)), vmem((2 * rn, units)),
            vmem((512, rn), f32),
            vmem((bucket, values)), vmem((values, width)), vmem((8, bucket), f32),
            vmem((8, bucket), f32), vmem((bucket, 128), f32), vmem((128, bucket), f32),
            vmem((1, width), f32), vmem((1, width), f32),
            vmem((4, *small), f32), vmem((3, *small), f32), vmem((nz, *small), f32),
            dma(17), dma(4, 2, 4), dma(4, 2, 4), dma(4, 4), dma(4, 4), dma(2, 3, 4), dma(2, 3, 4),
            dma(AHEAD), dma(steps), dma(ring), dma(jobs * (nz + 1)), dma(nz), dma(nz + 1), dma(1), dma(1), dma(3),
            dma(3), dma(3), dma(nz), dma(nz), pltpu.SemaphoreType.REGULAR((2,)),
        ],
        compiler_params=pltpu.CompilerParams(
            collective_id=collective_id, has_side_effects=True, vmem_limit_bytes=VMEM_MB << 20
        ),
        name="layer",
    )(
        gain, gain_attn, length, den_row, attended, w_out, denom, tokens, w_gate, w_up, w_down, cot_all,
        normed, query, key, value, w_query, w_key, w_value,
    )
    return outs[:11]


def front_kernel(
    gain, length, tokens_h, cotangent_h, w_query_h, w_key_h, w_value_h,
    query, key, value, attended, denom_t, den_row, normed_h, cot_h,
    tokens, w_query, w_key, w_value, denom, normed, cot_own, load_sem, ag_s, ag_r,
):
    g = Group()
    own_rows = tokens.shape[0]
    loads = [
        pltpu.make_async_copy(src, dst, load_sem.at[2 + n])
        for n, (src, dst) in enumerate(
            [(tokens_h, tokens), (cotangent_h, cot_own), (w_value_h, w_value), (w_query_h, w_query), (w_key_h, w_key)]
        )
    ]
    for copy in loads:
        copy.start()
    bucket = normed.shape[0]
    feat_width, feat_pad = w_query.shape[0], query.shape[1]
    head_width = 128
    heads = value.shape[1] // head_width
    feat = feat_width // heads
    scale = 1.0 / math.sqrt(feat)
    own_first = pl.multiple_of(g.t * own_rows, own_rows)
    meet(g, 0)
    rows_out = Spread(g, own_rows, 64, None, normed, (ag_s, ag_r), 0)
    cots = Spread(g, own_rows, 64, cot_own, cot_h, (ag_s, ag_r), 1)

    def first_norm(j):
        for a in range(64 // STRIP):
            r = pl.ds(pl.multiple_of(j * 64 + a * STRIP, STRIP), STRIP)
            to = pl.ds(pl.multiple_of(own_first + j * 64 + a * STRIP, STRIP), STRIP)
            normal, _ = norm_parts(tokens[r].astype(f32))
            normed[to] = (normal * gain[...]).astype(bf16)
        rows_out.start(j)

    loads[0].wait()
    loop(rows_out.count, first_norm)
    for copy in loads[1:]:
        copy.wait()
    position = own_first + lax.broadcasted_iota(jnp.int32, (own_rows, 1), 0)
    real_rows = (position < length[...]).astype(f32)
    cot_own[...] = (cot_own[...].astype(f32) * real_rows).astype(bf16)
    own_cot = pltpu.make_async_copy(cot_own, cot_h.at[pl.ds(own_first, own_rows)], load_sem.at[0])
    own_cot.start()

    def project(y, c, half):
        r = pl.ds(pl.multiple_of((y * 2 + c) * own_rows + half * 128, 128), 128)
        value[r] = dot(normed[r], w_value[...]).astype(bf16)
        for out, weight in ((query, w_query), (key, w_key)):
            out[r] = jnp.zeros((128, feat_pad), bf16)
            out[r, :feat_width] = dot(normed[r], weight[...], NT).astype(bf16)

    def near(half):
        project(g.y, g.c, half)
        loop(2, lambda a: rows_out.sib_in(half * 2 + a))
        project(g.y, 1 - g.c, half)

    loop(2, near)

    def far(half):
        loop(2, lambda a: rows_out.relay(half * 2 + a))
        project(1 - g.y, g.c, half)
        loop(2, lambda a: rows_out.far_in(half * 2 + a))
        project(1 - g.y, 1 - g.c, half)

    loop(1, far)
    loop(2, lambda a: rows_out.relay(2 + a))
    loop(cots.count, cots.start)
    project(1 - g.y, g.c, 1)
    loop(2, lambda a: rows_out.far_in(2 + a))
    project(1 - g.y, 1 - g.c, 1)
    keep = pltpu.make_async_copy(normed, normed_h, load_sem.at[1])
    keep.start()
    denom[...] = jnp.zeros_like(denom)
    tile = 256

    def head(h):
        lanes = head_lanes(h, feat, feat_pad)
        cols = pl.ds(pl.multiple_of(h * head_width, head_width), head_width)
        for qb in range(bucket // tile):
            q0, nk = qb * tile, (qb + 1) * tile
            scores = dot(query[q0:nk] * lanes, key[:nk], NT) * scale
            spot = lax.broadcasted_iota(jnp.int32, (tile, nk), 1)
            below = spot <= q0 + lax.broadcasted_iota(jnp.int32, (tile, nk), 0)
            real = lax.broadcasted_iota(jnp.int32, (1, nk), 1) < length[...]
            taylor = (1.0 + scores + 0.5 * scores * scores) * (below.astype(f32) * real.astype(f32))
            den = jnp.sum(taylor, axis=1, keepdims=True)
            top = dot(taylor.astype(bf16), value[:nk, cols])
            attended[q0:nk, cols] = (top / den).astype(bf16)
            lane = lax.broadcasted_iota(jnp.int32, (tile, denom.shape[1]), 1)
            denom[q0:nk] = jnp.where(lane == h, den, denom[q0:nk])

    for h in range(heads):
        head(h)
        if h < cots.count:
            cots.relay(h)
    for h in range(heads, cots.count):
        cots.relay(h)
    place = lax.broadcasted_iota(jnp.int32, (bucket, 1), 0)
    weight = (place < length[...]).astype(f32) / (place.astype(f32) + 1.0)
    denom_t[...] = denom[...].T[: denom_t.shape[0]]
    den_row[...] = jnp.sum(denom[...] * weight, axis=0, keepdims=True)

    def arrive(j):
        cots.sib_in(j)
        cots.far_in(j)

    loop(cots.count, arrive)
    own_cot.wait()
    keep.wait()
    rows_out.drain()
    cots.drain()


def front_call(tokens, cotangent, gain, length, w_query, w_key, w_value, collective_id):
    own_rows, width = tokens.shape
    bucket = own_rows * lax.axis_size("tensor")
    values = w_value.shape[1]
    vm, hbm = pl.BlockSpec(memory_space=pltpu.VMEM), pl.BlockSpec(memory_space=pl.ANY)
    dma = lambda *shape: pltpu.SemaphoreType.DMA(shape)
    sds = jax.ShapeDtypeStruct
    return pl.pallas_call(
        front_kernel,
        out_shape=[
            sds((bucket, 128), bf16), sds((bucket, 128), bf16), sds((bucket, values), bf16),
            sds((bucket, values), bf16), sds((8, bucket), f32), sds((1, 128), f32),
            sds((bucket, width), bf16), sds((bucket, width), bf16),
        ],
        in_specs=[vm] * 2 + [hbm] * 5,
        out_specs=[vm] * 6 + [hbm] * 2,
        scratch_shapes=[
            pltpu.VMEM((own_rows, width), bf16), pltpu.VMEM(w_query.shape, bf16), pltpu.VMEM(w_key.shape, bf16),
            pltpu.VMEM(w_value.shape, bf16),
            pltpu.VMEM((bucket, 128), f32), pltpu.VMEM((bucket, width), bf16), pltpu.VMEM((own_rows, width), bf16), dma(7), dma(2, 3, 4), dma(2, 3, 4),
        ],
        compiler_params=pltpu.CompilerParams(
            collective_id=collective_id, has_side_effects=True, vmem_limit_bytes=48 << 20
        ),
        name="front",
    )(gain, length, tokens, cotangent, w_query, w_key, w_value)


def per_device(
    tokens,
    gain_attn,
    gain_mlp,
    w_query,
    w_key,
    w_value,
    w_out,
    w_gate,
    w_up,
    w_down,
    cotangent,
    lengths,
):
    groups = lax.axis_size("tensor")
    length = lax.dynamic_slice(lengths, (lax.axis_index("dp"),), (1,))[None]
    w_query_t, w_key_t, w_gate_t, w_up_t = w_query.T, w_key.T, w_gate.T, w_up.T
    query, key, value, attended, denom, den_row, normed_all, cot_all = front_call(
        tokens, cotangent, gain_attn[None], length, w_query_t, w_key_t, w_value, 1
    )
    small, output, _, _, down_total, gate_total, up_total, input_grad, out_total, value_total, qk_total = layer_call(
        attended, w_out, gain_mlp[None], gain_attn[None], length, denom, den_row, tokens, w_gate_t, w_up_t, w_down,
        cot_all, normed_all, query, key, value, w_query_t, w_key_t, w_value, 2,
    )
    quarter = w_query.shape[0] // 4
    gain_attn_total, gain_mlp_total = small[:4, :quarter].reshape(-1), small[4:, :quarter].reshape(-1)
    feat_width = w_query.shape[1]
    query_total, key_total = qk_total[:feat_width].T, qk_total[feat_width:].T
    gate_total, up_total = gate_total.T, up_total.T
    heads = feat_width // FEAT * groups
    den_mean = jnp.sum(small[0, quarter:]) / (heads * jnp.sum(lengths).astype(f32))
    return (
        output,
        input_grad,
        gain_attn_total,
        gain_mlp_total,
        query_total,
        key_total,
        value_total,
        out_total,
        gate_total,
        up_total,
        down_total,
        den_mean,
    )


def solution(mesh):
    return jax.shard_map(
        per_device,
        mesh=mesh,
        in_specs=(
            P(("dp", "tensor"), None),
            P(),
            P(),
            P(None, "tensor"),
            P(None, "tensor"),
            P(None, "tensor"),
            P("tensor", None),
            P(None, "tensor"),
            P(None, "tensor"),
            P("tensor", None),
            P(("dp", "tensor"), None),
            P(),
        ),
        out_specs=(
            P(("dp", "tensor"), None),
            P(("dp", "tensor"), None),
            P(),
            P(),
            P("dp", "tensor"),
            P("dp", "tensor"),
            P("dp", "tensor"),
            P("tensor", "dp"),
            P("dp", "tensor"),
            P("dp", "tensor"),
            P("tensor", "dp"),
            P(),
        ),
        check_vma=False,
    )
```

```python
import functools
import math

import jax
import jax.numpy as jnp
from jax import lax
from jax.experimental import pallas as pl
from jax.experimental.pallas import tpu as pltpu
from jax.sharding import PartitionSpec as P

FEAT = 16
MESH = pl.DeviceIdType.MESH
f32 = jnp.float32
bf16 = jnp.bfloat16
NT = (((1,), (1,)), ((), ()))
TN = (((0,), (0,)), ((), ()))
AHEAD = 4
LAG = 3
SETTLE = 3
STRIP = 16
VMEM_MB = 63


def dot(a, b, dims=(((1,), (0,)), ((), ()))):
    return lax.dot_general(a, b, dims, preferred_element_type=f32)


def loop(count, body):
    def step(i, carry):
        body(i)
        return carry

    lax.fori_loop(0, count, step, 0)


def pieces(width, size):
    return [(start, min(size, width - start)) for start in range(0, width, size)]


class Group:
    def __init__(self):
        self.dp = lax.axis_index("dp")
        self.t = lax.axis_index("tensor")
        self.y, self.c = self.t // 2, lax.rem(self.t, 2)
        self.sibling = (self.dp, self.y * 2 + 1 - self.c)
        self.across = (self.dp, (1 - self.y) * 2 + self.c)


def remote(src, dst, send, recv, device):
    return pltpu.make_async_remote_copy(src, dst, send, recv, device_id=device, device_id_type=MESH)


class RowSums:
    def __init__(self, g, own_rows, phase, chunk, part, bufs, sems, piece=512):
        self.piece = piece
        self.g, self.own, self.p, self.chunk, self.part = g, own_rows, phase, chunk, part
        self.sibsend, self.sibrecv, self.ysend, self.yrecv, self.total = bufs
        self.sib_s, self.sib_r, self.y_s, self.y_r = sems
        self.count = own_rows // chunk

    def at(self, j):
        return pl.ds(pl.multiple_of(j * self.chunk, self.chunk), self.chunk)

    def rows(self, y, c, j):
        return pl.ds(pl.multiple_of((y * 2 + c) * self.own + j * self.chunk, self.chunk), self.chunk)

    def sib(self, far, j):
        return remote(
            self.sibsend.at[far, self.at(j)], self.sibrecv.at[far, self.at(j)],
            self.sib_s.at[self.p, far, j], self.sib_r.at[self.p, far, j], self.g.sibling,
        )

    def ycopy(self, j):
        return remote(
            self.ysend.at[self.at(j)], self.yrecv.at[self.at(j)],
            self.y_s.at[self.p, j], self.y_r.at[self.p, j], self.g.across,
        )

    def give(self, far, j):
        y = 1 - self.g.y if far else self.g.y
        for n, w in pieces(self.total.shape[1], self.piece):
            self.sibsend[far, self.at(j), n : n + w] = self.part(self.rows(y, 1 - self.g.c, j), n, w).astype(bf16)
        self.sib(far, j).start()

    def send(self, j):
        g = self.g
        for n, w in pieces(self.total.shape[1], self.piece):
            self.total[self.at(j), n : n + w] = self.part(self.rows(1 - g.y, g.c, j), n, w)
        self.sib(1, j).wait_recv()
        self.ysend[self.at(j)] = (self.total[self.at(j)] + self.sibrecv[1, self.at(j)].astype(f32)).astype(bf16)
        self.ycopy(j).start()

    def hold(self, j):
        for n, w in pieces(self.total.shape[1], self.piece):
            self.total[self.at(j), n : n + w] = self.part(self.rows(self.g.y, self.g.c, j), n, w)

    def finish(self, j, use):
        self.sib(0, j).wait_recv()
        self.ycopy(j).wait_recv()

        def strip(i):
            r = pl.ds(pl.multiple_of(j * self.chunk + i * STRIP, STRIP), STRIP)
            use(r, self.total[r] + self.sibrecv[0, r].astype(f32) + self.yrecv[r].astype(f32))

        loop(self.chunk // STRIP, strip)

    def drain(self):
        def body(j):
            self.sib(0, j).wait_send()
            self.sib(1, j).wait_send()
            self.ycopy(j).wait_send()

        loop(self.count, body)


class Spread:
    def __init__(self, g, own_rows, chunk, src, full, sems, phase):
        self.g, self.own, self.chunk, self.src, self.full, self.p = g, own_rows, chunk, src, full, phase
        self.s, self.r = sems
        self.count = own_rows // chunk

    def rows(self, y, c, j):
        return pl.ds(pl.multiple_of((y * 2 + c) * self.own + j * self.chunk, self.chunk), self.chunk)

    def copy(self, kind, j):
        g = self.g
        rows = self.rows(g.y, g.c, j)
        if kind == 2:
            rows = self.rows(1 - g.y, g.c, j)
            src = self.full.at[rows]
        elif self.src is None:
            src = self.full.at[rows]
        else:
            src = self.src.at[pl.ds(pl.multiple_of(j * self.chunk, self.chunk), self.chunk)]
        return remote(
            src, self.full.at[rows], self.s.at[self.p, kind, j], self.r.at[self.p, kind, j],
            g.across if kind == 1 else g.sibling,
        )

    def start(self, j):
        self.copy(1, j).start()
        self.copy(0, j).start()

    def relay(self, j):
        self.copy(1, j).wait_recv()
        self.copy(2, j).start()

    def sib_in(self, j):
        self.copy(0, j).wait_recv()

    def far_in(self, j):
        self.copy(2, j).wait_recv()

    def drain(self):
        def body(j):
            for kind in range(3):
                self.copy(kind, j).wait_send()

        loop(self.count, body)


class WeightSums:
    def __init__(self, g, dp_size, rows, weights, widths, write, refs, sems, emit):
        self.g, self.rows, self.widths, self.write, self.emit = g, rows, widths, write, emit
        self.weights = weights
        self.nz = dp_size // 2
        self.z, self.x = g.dp // 2, lax.rem(g.dp, 2)
        self.halves = max(1, rows // 128)
        self.rn = rows // self.halves
        self.ring = self.zs_slots(self.nz)
        self.jobs = weights * self.halves - 1
        self.steps = self.jobs * self.nz
        (self.xs, self.zs, self.acc, self.xtmp, self.ztmp, self.xrecv, self.zrecv,
         self.zf, self.zfx, self.facc, self.frecv, self.fxrecv) = refs
        (self.xs_s, self.xr_s, self.zs_s, self.zr_s, self.loc, self.zf_s, self.zf_r, self.fx_s, self.fx_r) = sems
        self.ahead = self.xs.shape[0]
        self.gap = max(1, (self.steps - 8) // self.nz)
        self.partner = (self.z * 2 + 1 - self.x, g.t)

    @staticmethod
    def zs_slots(nz):
        return 2 * nz if nz <= 4 else nz

    def job(self, s):
        lin = s // self.nz + 1
        return lin // self.halves, lax.rem(lin, self.halves)

    def by_kind(self, allowed, s, body):
        i, _ = self.job(s)

        @pl.when(allowed & (i < self.weights - 1))
        def _():
            body(s, 0)

        @pl.when(allowed & (i == self.weights - 1))
        def _():
            body(s, 1)

    def order(self, k):
        last = self.nz - 1
        upper = self.z >= self.nz // 2
        z = jnp.where(upper, last - self.z, self.z)
        zt = jnp.where(k < last - z, last - k, jnp.where(k < last, last - 1 - k, z))
        return jnp.where(upper, last - zt, zt)

    def coming(self, zt):
        return jnp.where(zt > self.z, self.z > 0, self.z < self.nz - 1)

    def towards(self, zt):
        return (jnp.where(zt > self.z, self.z + 1, self.z - 1) * 2 + self.x, self.g.t)

    def slot(self, zt):
        return jnp.where(zt == self.z - 1, self.nz, zt)

    def part(self, ref, index, kind):
        return ref.at[index] if kind == 0 else ref.at[index, :, pl.ds(0, self.widths[1])]

    def small(self, ref, kind):
        return ref.at[pl.ds(0, self.rn)] if kind == 0 else ref.at[pl.ds(0, self.rn), pl.ds(0, self.widths[1])]

    def xcopy(self, s, kind):
        slot = lax.rem(s, self.ahead)
        return remote(
            self.part(self.xs, slot, kind), self.part(self.xrecv, s, kind), self.xs_s.at[slot], self.xr_s.at[s],
            self.partner,
        )

    def zcopy(self, s, zt, kind):
        ring = lax.rem(s, self.ring)
        j = s // self.nz * (self.nz + 1) + self.slot(zt)
        return remote(
            self.part(self.zs, ring, kind), self.part(self.zrecv, j, kind), self.zs_s.at[ring], self.zr_s.at[j],
            self.towards(zt),
        )

    def zwait(self, j, kind):
        remote(
            self.part(self.zs, 0, kind), self.part(self.zrecv, j, kind), self.zs_s.at[0], self.zr_s.at[j],
            self.partner,
        ).wait_recv()

    def fetch(self, src, dst, k):
        copy = pltpu.make_async_copy(src, dst, self.loc.at[k])
        copy.start()
        return copy

    def xsend(self, s, kind):
        self.by_kind(s >= self.ahead, s - self.ahead, lambda a, old: self.xcopy(a, old).wait_send())
        i, h = self.job(s)
        slot = lax.rem(s, self.ahead)

        def store(n, w, value):
            self.xs[slot, :, n : n + w] = value.astype(bf16)

        self.write(store, kind, i, self.order(lax.rem(s, self.nz)), 1 - self.x, h)
        self.xcopy(s, kind).start()

    def zsent(self, s):
        k = lax.rem(s, self.nz)
        self.by_kind(
            (s >= 0) & (k < self.nz - 1), s, lambda a, old: self.zcopy(a, self.order(k), old).wait_send()
        )

    def xstep(self, s, kind):
        w = self.widths[kind]
        k = lax.rem(s, self.nz)
        zt = self.order(k)
        i, h = self.job(s)
        self.xcopy(s, kind).wait_recv()
        copy = self.fetch(self.part(self.xrecv, s, kind), self.small(self.xtmp, kind), 0)
        slot = lax.rem(s // self.nz, 2)
        ring = lax.rem(s, self.ring)
        self.zsent(s - self.ring)

        def store(n, w, value):
            self.acc[slot, :, n : n + w] = value

        self.write(store, kind, i, zt, self.x, h)
        copy.wait()
        total = self.acc[slot, :, :w] + self.xtmp[:, :w].astype(f32)

        @pl.when(k == self.nz - 1)
        def _():
            self.acc[slot, :, :w] = total

        @pl.when(k < self.nz - 1)
        def _():
            self.zs[ring, :, :w] = total.astype(bf16)

            @pl.when(jnp.logical_not(self.coming(zt)))
            def _():
                self.zcopy(s, zt, kind).start()

    def zstep(self, s, kind):
        w = self.widths[kind]
        k = lax.rem(s, self.nz)
        zt = self.order(k)
        ring = lax.rem(s, self.ring)

        @pl.when((k < self.nz - 1) & self.coming(zt))
        def _():
            j = s // self.nz * (self.nz + 1) + zt
            self.zwait(j, kind)
            self.fetch(self.part(self.zrecv, j, kind), self.small(self.ztmp, kind), 1).wait()
            self.zs[ring, :, :w] = (
                self.zs[ring, :, :w].astype(f32) + self.ztmp[: self.rn, :w].astype(f32)
            ).astype(bf16)
            self.zcopy(s, zt, kind).start()

    def final(self, s, kind):
        w = self.widths[kind]
        jx = s // self.nz
        slot = lax.rem(jx, 2)

        def take(j):
            self.zwait(j, kind)
            self.fetch(self.part(self.zrecv, j, kind), self.small(self.ztmp, kind), 1).wait()
            self.acc[slot, :, :w] += self.ztmp[: self.rn, :w].astype(f32)

        @pl.when(self.z > 0)
        def _():
            take(jx * (self.nz + 1) + self.z)

        @pl.when(self.z < self.nz - 1)
        def _():
            take(jx * (self.nz + 1) + self.nz)

        i, h = self.job(s)
        self.emit(kind, i, h, self.acc.at[slot])

    def fcopy(self, q, zt):
        slot = self.slot(zt)
        return remote(self.zf.at[q], self.frecv.at[slot], self.zf_s.at[q], self.zf_r.at[slot], self.towards(zt))

    def fwait(self, slot):
        remote(self.zf.at[0], self.frecv.at[slot], self.zf_s.at[0], self.zf_r.at[slot], self.partner).wait_recv()

    def fstart(self, q):
        zt = self.order(q)
        for xt in range(2):

            def store(n, w, value):
                self.zf[q, xt * self.rn : (xt + 1) * self.rn, n : n + w] = value.astype(bf16)

            self.write(store, 0, 0, zt, xt, 0)

        @pl.when(jnp.logical_not(self.coming(zt)))
        def _():
            self.fcopy(q, zt).start()

    def fstep(self, q):
        zt = self.order(q)

        @pl.when(self.coming(zt))
        def _():
            self.fwait(zt)
            self.fetch(self.frecv.at[zt], self.ztmp, 1).wait()
            self.zf[q] = (self.zf[q].astype(f32) + self.ztmp[...].astype(f32)).astype(bf16)
            self.fcopy(q, zt).start()

    def fxcopy(self):
        return remote(self.zfx, self.fxrecv, self.fx_s.at[0], self.fx_r.at[0], self.partner)

    def fend(self):
        for xt in range(2):

            def store(n, w, value):
                self.facc[xt * self.rn : (xt + 1) * self.rn, n : n + w] = value

            self.write(store, 0, 0, self.z, xt, 0)

        def take(slot):
            self.fwait(slot)
            self.fetch(self.frecv.at[slot], self.ztmp, 1).wait()
            self.facc[...] += self.ztmp[...].astype(f32)

        @pl.when(self.z > 0)
        def _():
            take(self.z)

        @pl.when(self.z < self.nz - 1)
        def _():
            take(self.nz)

        away = pl.ds(pl.multiple_of((1 - self.x) * self.rn, self.rn), self.rn)
        self.zfx[...] = self.facc[away].astype(bf16)
        self.fxcopy().start()

    def ffinal(self):
        self.fxcopy().wait_recv()
        self.fetch(self.fxrecv, self.xtmp, 1).wait()
        own = pl.ds(pl.multiple_of(self.x * self.rn, self.rn), self.rn)
        self.facc[own] += self.xtmp[...].astype(f32)
        self.emit(0, 0, 0, self.facc.at[own])

    def begin(self):
        loop(self.ahead, lambda s: self.xsend(s, 0))

    def services(self):
        return max(self.steps + SETTLE + 1, self.gap * (self.nz - 1) + 9)

    def service(self, s):
        self.by_kind(s < self.steps, s, self.xstep)
        self.by_kind(s + self.ahead < self.steps, s + self.ahead, self.xsend)
        last = self.steps - self.nz
        self.by_kind((s >= LAG) & (s - LAG < last), s - LAG, self.zstep)

        @pl.when((s - 1 >= last) & (s - 1 < self.steps))
        def _():
            self.zstep(s - 1, 1)

        @pl.when((s >= 1) & (lax.rem(s - 1, self.gap) == 0) & ((s - 1) // self.gap < self.nz - 1))
        def _():
            self.fstart((s - 1) // self.gap)

        @pl.when((s >= 4) & (lax.rem(s - 4, self.gap) == 0) & ((s - 4) // self.gap < self.nz - 1))
        def _():
            self.fstep((s - 4) // self.gap)

        @pl.when(s == self.gap * (self.nz - 1) + 4)
        def _():
            self.fend()

        @pl.when(s == self.gap * (self.nz - 1) + 8)
        def _():
            self.ffinal()

        due = (s >= self.nz + SETTLE) & (lax.rem(s - SETTLE, self.nz) == 0) & (s - SETTLE <= self.steps)
        self.by_kind(due, s - SETTLE - self.nz, self.final)

    def drain(self):
        loop(
            self.ahead,
            lambda a: self.by_kind(
                a >= 0, self.steps - self.ahead + a, lambda s, kind: self.xcopy(s, kind).wait_send()
            ),
        )
        loop(self.ring, lambda a: self.zsent(self.steps - self.ring + a))
        loop(self.nz - 1, lambda q: self.fcopy(q, self.order(q)).wait_send())
        self.fxcopy().wait_send()


def meet(g, nz, every=False):
    if nz == 0:
        barrier = pltpu.get_barrier_semaphore()
        for device in (g.sibling, g.across):
            pl.semaphore_signal(barrier, inc=1, device_id=device, device_id_type=MESH)
        pl.semaphore_wait(barrier, 2)
        return
    z, x = g.dp // 2, lax.rem(g.dp, 2)
    barrier = pltpu.get_barrier_semaphore()

    def hello(device):
        pl.semaphore_signal(barrier, inc=1, device_id=device, device_id_type=MESH)

    hello(g.sibling)
    hello(g.across)
    hello((z * 2 + 1 - x, g.t))
    if every:
        loop(nz - 1, lambda k: hello((lax.rem(z + 1 + k, nz) * 2 + x, g.t)))
        pl.semaphore_wait(barrier, nz + 2)
        return

    @pl.when(z > 0)
    def _():
        hello(((z - 1) * 2 + x, g.t))

    @pl.when(z < nz - 1)
    def _():
        hello(((z + 1) * 2 + x, g.t))

    peers = 5 - jnp.where(z == 0, 1, 0) - jnp.where(z == nz - 1, 1, 0)
    pl.semaphore_wait(barrier, peers)


def owner_dot(load, right, rows, zt, xt, h):
    if rows % 128:
        both = dot(load(pl.ds(pl.multiple_of(zt * (2 * rows), 2 * rows), 2 * rows)), right, TN)
        return jnp.where(xt == 0, both[:rows], both[rows:])
    rn = min(rows, 128)
    return dot(load(pl.ds(pl.multiple_of((zt * 2 + xt) * rows + h * rn, rn), rn)), right, TN)


def head_lanes(h, feat, width):
    return (lax.broadcasted_iota(jnp.int32, (1, width), 1) // feat == h).astype(f32).astype(bf16)


def norm_parts(state):
    scale = lax.rsqrt(jnp.mean(state * state, axis=-1, keepdims=True) + 1e-06)
    return state * scale, scale


def layer_kernel(
    dp_size,
    gain, gain_attn, length, den_row,
    attended_h, w_out_h, denom_h, tokens_h, w_gate_h, w_up_h, w_down_h, cot_h, normed_h, query_h, key_h, value_h, w_query_h, w_key_h, w_value_h,
    small_out, output_h, state_grad_h, state_all_h, down_h, gate_h, up_h, input_grad_h, out_h, value_grad_h, qk_h,
    xrecv, zrecv, frecv, fxrecv,
    w_gate, w_up, w_down, lefts, rights, mid, sibsend, sibrecv, ysend, yrecv, total, spread_buf,
    xs, zs, zf, zfx, acc, facc, xtmp, ztmp, turn,
    attended, w_out, denom, grad_den, gk_acc, gq_acc, gain_grad, gain_acc, smalls, small_got, small_z,
    load_sem, sib_s, sib_r, y_s, y_r, ag_s, ag_r,
    xs_s, xr_s, zs_s, zr_s, zf_s, zf_r, fx_s, fx_r, loc, sm_s, sm_r, smz_s, smz_r, ready,
):
    g = Group()
    own_rows, width = tokens_h.shape
    tokens = spread_buf
    hidden_units = rights.shape[2]
    rows = width // dp_size
    loads = [
        pltpu.make_async_copy(src, dst, load_sem.at[n])
        for n, (src, dst) in enumerate(
            [(w_gate_h, w_gate), (w_up_h, w_up), (w_down_h, w_down), (cot_h, lefts.at[0]), (tokens_h, tokens),
             (attended_h, attended), (w_out_h, w_out), (denom_h, denom)]
        )
    ]
    for copy in loads[5:] + loads[:5]:
        copy.start()
    nz = dp_size // 2
    meet(g, nz, every=True)
    for copy in loads[5:]:
        copy.wait()
    bufs = (sibsend, sibrecv, ysend, yrecv, total)
    sems = (sib_s, sib_r, y_s, y_r)

    def attn_part(r, n, w):
        return dot(attended[r], w_out[:, n : n + w])

    sums = RowSums(g, own_rows, 0, 64, attn_part, bufs, sems)
    normed = Spread(g, own_rows, 64, None, lefts.at[1], (ag_s, ag_r), 0)
    own_first = pl.multiple_of(g.t * own_rows, own_rows)

    def first_state(r, summed):
        state = tokens[r].astype(f32) + summed
        mid[r] = state
        normal, _ = norm_parts(state)
        start = pl.multiple_of(own_first + r.start, STRIP)
        lefts[1, pl.ds(start, STRIP)] = (normal * gain[...]).astype(bf16)

    sums.give(1, 0)

    def far(j):
        @pl.when(j + 1 < sums.count)
        def _():
            sums.give(1, j + 1)

        sums.send(j)

    loop(sums.count, far)

    def near(j):
        sums.give(0, j)
        sums.hold(j)

    loop(sums.count, near)

    def feed(y, c, half):
        r = pl.ds(pl.multiple_of((y * 2 + c) * own_rows + half * 128, 128), 128)
        for n, w in pieces(hidden_units, 512):
            gate = dot(lefts[1, r], w_gate[n : n + w], NT)
            up = dot(lefts[1, r], w_up[n : n + w], NT)
            back = dot(lefts[0, r], w_down[n : n + w], NT)
            sig = jax.nn.sigmoid(gate)
            active = gate * sig
            rights[0, r, n : n + w] = (active * up).astype(bf16)
            rights[1, r, n : n + w] = (back * up * sig * (1.0 + gate * (1.0 - sig))).astype(bf16)
            rights[2, r, n : n + w] = (back * active).astype(bf16)

    def close(j):
        sums.finish(j, first_state)
        normed.start(j)

    loads[4].wait()

    def half_near(half):
        loop(2, lambda a: close(half * 2 + a))

        @pl.when(half == 0)
        def _():
            for copy in loads[:4]:
                copy.wait()

        feed(g.y, g.c, half)
        loop(2, lambda a: normed.sib_in(half * 2 + a))
        feed(g.y, 1 - g.c, half)

    loop(2, half_near)

    def half_far(half):
        loop(2, lambda a: normed.relay(half * 2 + a))
        feed(1 - g.y, g.c, half)
        loop(2, lambda a: normed.far_in(half * 2 + a))
        feed(1 - g.y, 1 - g.c, half)

    loop(2, half_far)
    sums.drain()

    bucket, values = attended.shape
    head_width, feat_pad = 128, 128
    heads = values // head_width
    feat_width = w_query_h.shape[0]
    feat = feat_width // heads
    halves = max(1, rows // 128)
    rn = rows // halves
    grads_at, value_at, sums_at = 0, values, 2 * values
    query_at = sums_at + values + 2 * feat_width
    key_at = query_at + feat_pad
    sums_end = query_at
    kept_query, kept_key, turned_key = bucket, bucket + feat_width, bucket + 2 * feat_width

    def write(store, kind, i, zt, xt, h):
        if kind == 0:
            left = jnp.minimum(i, 1)
            store(0, hidden_units, owner_dot(lambda cols: lefts[left, :, cols], rights[i], rows, zt, xt, h))
            return
        store(0, values, owner_dot(lambda cols: w_gate[:bucket, cols], attended[...], rows, zt, xt, h))
        store(
            values, sums_end - sums_at,
            owner_dot(lambda cols: w_up[:bucket, cols], w_down[:bucket, sums_at:sums_end], rows, zt, xt, h),
        )

    def put(src, out, n, w, h):
        to = out.at[pl.ds(n, w)]
        if halves > 1:
            to = out.at[pl.ds(n, w), pl.ds(pl.multiple_of(h * rn, rn), rn)]
        copy = pltpu.make_async_copy(src.at[pl.ds(0, w)], to, loc.at[2])
        copy.start()
        copy.wait()

    def emit(kind, i, h, block):
        if kind == 0:
            for n, w in pieces(hidden_units, 512):
                turn[:w] = block[:, n : n + w].T
                for m, out in enumerate((down_h, gate_h, up_h)):
                    pl.when(i == m)(functools.partial(put, turn, out, n, w, h))
            return
        for n, w in pieces(values, 512):
            turn[:w] = block[:, n : n + w].T
            put(turn, out_h, n, w, h)
        copy = pltpu.make_async_copy(
            block.at[:, pl.ds(values, values)], value_grad_h.at[pl.ds(pl.multiple_of(h * rn, rn), rn)], loc.at[2]
        )
        copy.start()
        turn[: 2 * feat_width] = block[:, 2 * values : 2 * values + 2 * feat_width].T
        copy.wait()
        put(turn, qk_h, 0, 2 * feat_width, h)

    engine = WeightSums(
        g, dp_size, rows, 4, (hidden_units, 2 * values + 2 * feat_width), write,
        (xs, zs, acc, xtmp, ztmp, xrecv, zrecv, zf, zfx, facc, frecv, fxrecv),
        (xs_s, xr_s, zs_s, zr_s, loc, zf_s, zf_r, fx_s, fx_r), emit,
    )
    engine.begin()

    def back_part(r, n, w):
        return dot(rights[1, r], w_gate[:, n : n + w]) + dot(rights[2, r], w_up[:, n : n + w])

    sums = RowSums(g, own_rows, 1, 128, back_part, bufs, sems)
    states = Spread(g, own_rows, 128, spread_buf, state_all_h, (ag_s, ag_r), 1)
    gain_grad[...] = jnp.zeros_like(gain_grad)

    def state_back(r, grad):
        normal, scale = norm_parts(mid[r])
        weighted = grad * gain[...]
        start = pl.multiple_of(own_first + r.start, STRIP)
        change = scale * (weighted - normal * jnp.mean(weighted * normal, axis=-1, keepdims=True))
        state = lefts[0, pl.ds(start, STRIP)].astype(f32) + change
        gain_grad[...] += jnp.sum(grad * normal, axis=0, keepdims=True)
        total[r] = state
        spread_buf[r] = state.astype(bf16)

    def far_back(j):
        sums.give(1, j)
        sums.send(j)

    loop(sums.count, far_back)

    def near_back(j):
        sums.give(0, j)
        engine.service(2 * j)
        sums.hold(j)
        engine.service(2 * j + 1)

    loop(sums.count, near_back)
    used = 2 * sums.count

    def own_copy(j):
        r = pl.ds(pl.multiple_of(j * 128, 128), 128)
        to = pl.ds(pl.multiple_of(own_first + j * 128, 128), 128)
        return (
            pltpu.make_async_copy(total.at[r], state_grad_h.at[r], load_sem.at[0]),
            pltpu.make_async_copy(spread_buf.at[r], state_all_h.at[to], load_sem.at[1]),
        )

    def close_back(j):
        sums.finish(j, state_back)
        states.start(j)
        copies = own_copy(j)
        for copy in copies:
            copy.start()
        engine.service(used + j)
        for copy in copies:
            copy.wait()

    loop(sums.count, close_back)
    used = used + sums.count

    def pass_back(j):
        engine.service(used + 2 * j)
        states.relay(j)
        engine.service(used + 2 * j + 1)

    loop(sums.count, pass_back)
    used = used + 2 * sums.count

    def arrive(j):
        states.sib_in(j)
        states.far_in(j)

    loop(sums.count, arrive)
    sums.drain()

    def down_part(r, n, w):
        return dot(rights[0, r], w_down[:, n : n + w])

    sums = RowSums(g, own_rows, 2, 128, down_part, bufs, sems)

    def far_down(j):
        sums.give(1, j)
        sums.send(j)
        engine.service(used + j)

    loop(sums.count, far_down)
    used = used + sums.count

    def near_down(j):
        sums.give(0, j)
        sums.hold(j)

    loop(sums.count, near_down)

    fetches = [
        (state_all_h, w_gate.at[pl.ds(0, bucket)]), (normed_h, w_up.at[pl.ds(0, bucket)]),
        (value_h, w_down.at[pl.ds(0, bucket), pl.ds(value_at, values)]),
        (query_h, w_down.at[pl.ds(0, bucket), pl.ds(query_at, feat_pad)]),
        (key_h, w_down.at[pl.ds(0, bucket), pl.ds(key_at, feat_pad)]),
        (w_query_h, w_down.at[pl.ds(kept_query, feat_width)]), (w_key_h, w_down.at[pl.ds(kept_key, feat_width)]),
    ]
    span = 256
    chunks = [(width // span // 2, w_gate), (width // span // 2, w_up)]
    row = 0
    for count, home in chunks:
        for m in range(count):
            fetches.append(
                (w_value_h.at[pl.ds(row, span)], home.at[pl.ds(bucket, span), pl.ds(m * values, values)])
            )
            row += span
    fetches = [pltpu.make_async_copy(src, dst, load_sem.at[n]) for n, (src, dst) in enumerate(fetches)]
    for copy in fetches:
        copy.start()
    for copy in fetches:
        copy.wait()
    w_down[turned_key : turned_key + feat_pad, :bucket] = (
        w_down[:bucket, key_at : key_at + feat_pad].astype(f32).T.astype(bf16)
    )

    def spread_grad(b):
        r = pl.ds(pl.multiple_of(b * 128, 128), 128)
        grad = dot(w_gate[r], w_out[...], NT).astype(bf16).astype(f32)
        lane = lax.broadcasted_iota(jnp.int32, (128, 128), 1)
        dens = jnp.zeros((128, 128), f32)
        turned_den = denom[:, r].T
        for h in range(heads):
            cols = slice(h * head_width, (h + 1) * head_width)
            den = turned_den[:, h : h + 1]
            piece = grad[:, cols]
            w_down[r, grads_at + h * head_width : grads_at + (h + 1) * head_width] = (piece / den).astype(bf16)
            back = -jnp.sum(piece * attended[r, cols].astype(f32), axis=1, keepdims=True) / den
            dens = jnp.where(lane == h, back, dens)
        grad_den[:, r] = dens.T[: grad_den.shape[0]]

    loop(bucket // 128, spread_grad)
    engine.service(used)
    used = used + 1
    states.drain()

    def last_state(r, summed):
        position = own_first + r.start + lax.broadcasted_iota(jnp.int32, (STRIP, 1), 0)
        valid = (position < length[...]).astype(f32)
        spread_buf[r] = (valid * (mid[r] + summed)).astype(bf16)

    loop(sums.count, lambda j: sums.finish(j, last_state))
    pl.semaphore_signal(ready.at[0], inc=1, device_id=g.sibling, device_id_type=MESH)
    pl.semaphore_signal(ready.at[1], inc=1, device_id=g.across, device_id_type=MESH)
    keep = pltpu.make_async_copy(spread_buf, output_h, loc.at[2])
    keep.start()
    keep.wait()
    refills = [
        pltpu.make_async_copy(tokens_h, tokens, load_sem.at[15]),
        pltpu.make_async_copy(state_grad_h, mid, load_sem.at[16]),
    ]
    for copy in refills:
        copy.start()
    engine.service(used)
    used = used + 1
    gk_acc[...] = jnp.zeros_like(gk_acc)
    gq_acc[...] = jnp.zeros_like(gq_acc)
    total[...] = jnp.zeros_like(total)
    qk_scale = 1.0 / math.sqrt(feat)
    tile = 256

    def head(h):
        lanes = head_lanes(h, feat, feat_pad)
        sub = (lax.broadcasted_iota(jnp.int32, (feat_pad, 1), 0) // feat == h).astype(f32).astype(bf16)
        offset = pl.multiple_of(h * head_width, head_width)
        for qb in range(bucket // tile):
            q0, nk = qb * tile, (qb + 1) * tile
            q_own = w_down[q0:nk, query_at : query_at + feat_pad] * lanes
            grads = w_down[q0:nk, pl.ds(grads_at + offset, head_width)]
            for k0, count in pieces(nk, 2 * tile):
                keys = slice(k0, k0 + count)
                kept = w_down[turned_key : turned_key + feat_pad, keys] * sub
                scores = dot(w_down[keys, key_at : key_at + feat_pad], q_own, NT) * qk_scale
                spot = k0 + lax.broadcasted_iota(jnp.int32, (count, tile), 0)
                below = spot <= q0 + lax.broadcasted_iota(jnp.int32, (count, tile), 1)
                real = k0 + lax.broadcasted_iota(jnp.int32, (count, 1), 0) < length[...]
                mask = below.astype(f32) * real.astype(f32)
                taylor = (1.0 + scores + 0.5 * scores * scores) * mask
                moved = dot(taylor.astype(bf16), grads)
                for kb in range(count // tile):
                    at = (k0 // tile + kb) * values
                    total[:, pl.ds(at + offset, head_width)] += moved[kb * tile : (kb + 1) * tile]
                back = dot(w_down[keys, pl.ds(value_at + offset, head_width)], grads, NT)
                back = back + grad_den[pl.ds(h, 1), q0:nk]
                low = (back * mask * (1.0 + scores)).astype(bf16)
                gk_acc[keys] += dot(low, q_own)
                gq_acc[:, q0:nk] += dot(kept, low)

        @pl.when(lax.rem(h, 2) == 1)
        def _():
            engine.service(used + h // 2)

    loop(heads, head)
    used = used + heads // 2
    for kb in range(bucket // tile):
        r = slice(kb * tile, (kb + 1) * tile)
        w_down[r, sums_at : sums_at + values] = total[:, kb * values : (kb + 1) * values].astype(bf16)
        pair = jnp.concatenate([gq_acc[:feat_width, r].T, gk_acc[r, :feat_width]], axis=1) * qk_scale
        w_down[r, sums_at + values : sums_end] = pair.astype(bf16)
    sums.drain()

    def attn_back_part(r, n, w):
        count, home = chunks[0] if n < width // 2 else chunks[1]
        m = n // span % count
        out = dot(
            w_down[r, sums_at : sums_at + values], home[bucket : bucket + span, m * values : (m + 1) * values], NT
        )
        out = out + dot(
            w_down[r, sums_at + values : sums_end], w_down[kept_query : kept_query + 2 * feat_width, n : n + w]
        )
        return out

    sums = RowSums(g, own_rows, 3, 128, attn_back_part, bufs, sems, span)
    pl.semaphore_wait(ready.at[0], 1)
    pl.semaphore_wait(ready.at[1], 1)

    def far_last(j):
        sums.give(1, j)
        sums.send(j)
        engine.service(used + j)

    loop(sums.count, far_last)
    used = used + sums.count

    def near_last(j):
        sums.give(0, j)
        sums.hold(j)
        engine.service(used + j)

    loop(sums.count, near_last)
    used = used + sums.count
    gain_acc[...] = jnp.zeros_like(gain_acc)
    for copy in refills:
        copy.wait()

    def input_back(r, grad):
        normal, inv = norm_parts(tokens[r].astype(f32))
        weighted = grad * gain_attn[...]
        change = inv * (weighted - normal * jnp.mean(weighted * normal, axis=-1, keepdims=True))
        gain_acc[...] += jnp.sum(grad * normal, axis=0, keepdims=True)
        mid[r] += change

    def close_last(j):
        engine.service(used + j)
        sums.finish(j, input_back)

    loop(sums.count, close_last)
    used = used + sums.count
    result = pltpu.make_async_copy(mid, input_grad_h, load_sem.at[0])
    result.start()

    smalls[0] = jnp.zeros(smalls.shape[1:], f32)
    quarter = width // 4
    for m in range(4):
        smalls[0, m : m + 1, :quarter] = gain_acc[:, m * quarter : (m + 1) * quarter]
        smalls[0, 4 + m : 5 + m, :quarter] = gain_grad[:, m * quarter : (m + 1) * quarter]
    smalls[0, 0:1, quarter:] = den_row[...]
    z, x = engine.z, engine.x
    peers = (g.sibling, g.across, engine.partner)
    for n, device in enumerate(peers):
        copy = remote(smalls.at[n], small_got.at[n], sm_s.at[n], sm_r.at[n], device)
        copy.start()
        engine.service(used + n)
        copy.wait()
        smalls[n + 1] = smalls[n] + small_got[n]
    used = used + len(peers)

    def zsmall(k):
        return remote(
            smalls.at[3], small_z.at[z], smz_s.at[k], smz_r.at[k], (lax.rem(z + 1 + k, nz) * 2 + x, g.t)
        )

    loop(nz - 1, lambda k: zsmall(k).start())
    loop(engine.services() - used, lambda n: engine.service(used + n))
    small_z[z] = smalls[3]

    def zgot(k):
        remote(
            smalls.at[3], small_z.at[lax.rem(z - 1 - k + nz, nz)], smz_s.at[k], smz_r.at[k], g.sibling
        ).wait_recv()

    loop(nz - 1, zgot)
    small_out[...] = jnp.zeros_like(small_out)

    def zadd(k):
        small_out[...] += small_z[k]

    loop(nz, zadd)
    loop(nz - 1, lambda k: zsmall(k).wait_send())
    result.wait()
    sums.drain()
    normed.drain()
    engine.drain()


def layer_call(
    attended, w_out, gain, gain_attn, length, denom, den_row, tokens, w_gate, w_up, w_down, cot_all,
    normed, query, key, value, w_query, w_key, w_value, collective_id,
):
    dp_size = lax.axis_size("dp")
    nz = dp_size // 2
    own_rows, width = tokens.shape
    bucket, values = attended.shape
    units = w_down.shape[0]
    feat_width = w_query.shape[0]
    small = (8, width // 4 + den_row.shape[1])
    rows = width // dp_size
    halves = max(1, rows // 128)
    rn = rows // halves
    jobs = 4 * halves - 1
    steps = jobs * nz
    ring = WeightSums.zs_slots(nz)
    vm, hbm = pl.BlockSpec(memory_space=pltpu.VMEM), pl.BlockSpec(memory_space=pl.ANY)
    dma = lambda *shape: pltpu.SemaphoreType.DMA(shape)
    vmem = lambda shape, kind=bf16: pltpu.VMEM(shape, kind)
    sds = jax.ShapeDtypeStruct
    outs = pl.pallas_call(
        functools.partial(layer_kernel, dp_size),
        out_shape=[
            sds(small, f32),
            sds((own_rows, width), bf16),
            sds((own_rows, width), f32),
            sds((bucket, width), bf16),
            *[sds((units, rows), f32)] * 3,
            sds((own_rows, width), f32),
            sds((values, rows), f32),
            sds((rows, values), f32),
            sds((2 * feat_width, rows), f32),
            sds((steps, rn, units), bf16),
            sds((jobs * (nz + 1), rn, units), bf16),
            sds((nz + 1, 2 * rn, units), bf16),
            sds((rn, units), bf16),
        ],
        in_specs=[vm] * 4 + [hbm] * 15,
        out_specs=[vm] + [hbm] * 14,
        scratch_shapes=[
            vmem((units, width)), vmem((units, width)), vmem((units, width)),
            vmem((2, bucket, width)), vmem((3, bucket, units)), vmem((own_rows, width), f32),
            vmem((2, own_rows, width)), vmem((2, own_rows, width)), vmem((own_rows, width)), vmem((own_rows, width)),
            vmem((own_rows, width), f32), vmem((own_rows, width)),
            vmem((AHEAD, rn, units)), vmem((ring, rn, units)), vmem((nz - 1, 2 * rn, units)), vmem((rn, units)),
            vmem((2, rn, units), f32), vmem((2 * rn, units), f32), vmem((rn, units)), vmem((2 * rn, units)),
            vmem((512, rn), f32),
            vmem((bucket, values)), vmem((values, width)), vmem((8, bucket), f32),
            vmem((8, bucket), f32), vmem((bucket, 128), f32), vmem((128, bucket), f32),
            vmem((1, width), f32), vmem((1, width), f32),
            vmem((4, *small), f32), vmem((3, *small), f32), vmem((nz, *small), f32),
            dma(17), dma(4, 2, 4), dma(4, 2, 4), dma(4, 4), dma(4, 4), dma(2, 3, 4), dma(2, 3, 4),
            dma(AHEAD), dma(steps), dma(ring), dma(jobs * (nz + 1)), dma(nz), dma(nz + 1), dma(1), dma(1), dma(3),
            dma(3), dma(3), dma(nz), dma(nz), pltpu.SemaphoreType.REGULAR((2,)),
        ],
        compiler_params=pltpu.CompilerParams(
            collective_id=collective_id, has_side_effects=True, vmem_limit_bytes=VMEM_MB << 20
        ),
        name="layer",
    )(
        gain, gain_attn, length, den_row, attended, w_out, denom, tokens, w_gate, w_up, w_down, cot_all,
        normed, query, key, value, w_query, w_key, w_value,
    )
    return outs[:11]


def front_kernel(
    gain, length, tokens_h, cotangent_h, w_query_h, w_key_h, w_value_h,
    query, key, value, attended, denom_t, den_row, normed_h, cot_h,
    tokens, w_query, w_key, w_value, denom, normed, cot_own, load_sem, ag_s, ag_r,
):
    g = Group()
    own_rows = tokens.shape[0]
    loads = [
        pltpu.make_async_copy(src, dst, load_sem.at[2 + n])
        for n, (src, dst) in enumerate(
            [(tokens_h, tokens), (cotangent_h, cot_own), (w_value_h, w_value), (w_query_h, w_query), (w_key_h, w_key)]
        )
    ]
    for copy in loads:
        copy.start()
    bucket = normed.shape[0]
    feat_width, feat_pad = w_query.shape[0], query.shape[1]
    head_width = 128
    heads = value.shape[1] // head_width
    feat = feat_width // heads
    scale = 1.0 / math.sqrt(feat)
    own_first = pl.multiple_of(g.t * own_rows, own_rows)
    meet(g, 0)
    rows_out = Spread(g, own_rows, 64, None, normed, (ag_s, ag_r), 0)
    cots = Spread(g, own_rows, 64, cot_own, cot_h, (ag_s, ag_r), 1)

    def first_norm(j):
        for a in range(64 // STRIP):
            r = pl.ds(pl.multiple_of(j * 64 + a * STRIP, STRIP), STRIP)
            to = pl.ds(pl.multiple_of(own_first + j * 64 + a * STRIP, STRIP), STRIP)
            normal, _ = norm_parts(tokens[r].astype(f32))
            normed[to] = (normal * gain[...]).astype(bf16)
        rows_out.start(j)

    loads[0].wait()
    loop(rows_out.count, first_norm)
    for copy in loads[1:]:
        copy.wait()
    position = own_first + lax.broadcasted_iota(jnp.int32, (own_rows, 1), 0)
    real_rows = (position < length[...]).astype(f32)
    cot_own[...] = (cot_own[...].astype(f32) * real_rows).astype(bf16)
    own_cot = pltpu.make_async_copy(cot_own, cot_h.at[pl.ds(own_first, own_rows)], load_sem.at[0])
    own_cot.start()

    def project(y, c, half):
        r = pl.ds(pl.multiple_of((y * 2 + c) * own_rows + half * 128, 128), 128)
        value[r] = dot(normed[r], w_value[...]).astype(bf16)
        for out, weight in ((query, w_query), (key, w_key)):
            out[r] = jnp.zeros((128, feat_pad), bf16)
            out[r, :feat_width] = dot(normed[r], weight[...], NT).astype(bf16)

    def near(half):
        project(g.y, g.c, half)
        loop(2, lambda a: rows_out.sib_in(half * 2 + a))
        project(g.y, 1 - g.c, half)

    loop(2, near)

    def far(half):
        loop(2, lambda a: rows_out.relay(half * 2 + a))
        project(1 - g.y, g.c, half)
        loop(2, lambda a: rows_out.far_in(half * 2 + a))
        project(1 - g.y, 1 - g.c, half)

    loop(1, far)
    loop(2, lambda a: rows_out.relay(2 + a))
    loop(cots.count, cots.start)
    project(1 - g.y, g.c, 1)
    loop(2, lambda a: rows_out.far_in(2 + a))
    project(1 - g.y, 1 - g.c, 1)
    keep = pltpu.make_async_copy(normed, normed_h, load_sem.at[1])
    keep.start()
    denom[...] = jnp.zeros_like(denom)
    tile = 256

    def head(h):
        lanes = head_lanes(h, feat, feat_pad)
        cols = pl.ds(pl.multiple_of(h * head_width, head_width), head_width)
        for qb in range(bucket // tile):
            q0, nk = qb * tile, (qb + 1) * tile
            scores = dot(query[q0:nk] * lanes, key[:nk], NT) * scale
            spot = lax.broadcasted_iota(jnp.int32, (tile, nk), 1)
            below = spot <= q0 + lax.broadcasted_iota(jnp.int32, (tile, nk), 0)
            real = lax.broadcasted_iota(jnp.int32, (1, nk), 1) < length[...]
            taylor = (1.0 + scores + 0.5 * scores * scores) * (below.astype(f32) * real.astype(f32))
            den = jnp.sum(taylor, axis=1, keepdims=True)
            top = dot(taylor.astype(bf16), value[:nk, cols])
            attended[q0:nk, cols] = (top / den).astype(bf16)
            lane = lax.broadcasted_iota(jnp.int32, (tile, denom.shape[1]), 1)
            denom[q0:nk] = jnp.where(lane == h, den, denom[q0:nk])

    for h in range(heads):
        head(h)
        if h < cots.count:
            cots.relay(h)
    for h in range(heads, cots.count):
        cots.relay(h)
    place = lax.broadcasted_iota(jnp.int32, (bucket, 1), 0)
    weight = (place < length[...]).astype(f32) / (place.astype(f32) + 1.0)
    denom_t[...] = denom[...].T[: denom_t.shape[0]]
    den_row[...] = jnp.sum(denom[...] * weight, axis=0, keepdims=True)

    def arrive(j):
        cots.sib_in(j)
        cots.far_in(j)

    loop(cots.count, arrive)
    own_cot.wait()
    keep.wait()
    rows_out.drain()
    cots.drain()


def front_call(tokens, cotangent, gain, length, w_query, w_key, w_value, collective_id):
    own_rows, width = tokens.shape
    bucket = own_rows * lax.axis_size("tensor")
    values = w_value.shape[1]
    vm, hbm = pl.BlockSpec(memory_space=pltpu.VMEM), pl.BlockSpec(memory_space=pl.ANY)
    dma = lambda *shape: pltpu.SemaphoreType.DMA(shape)
    sds = jax.ShapeDtypeStruct
    return pl.pallas_call(
        front_kernel,
        out_shape=[
            sds((bucket, 128), bf16), sds((bucket, 128), bf16), sds((bucket, values), bf16),
            sds((bucket, values), bf16), sds((8, bucket), f32), sds((1, 128), f32),
            sds((bucket, width), bf16), sds((bucket, width), bf16),
        ],
        in_specs=[vm] * 2 + [hbm] * 5,
        out_specs=[vm] * 6 + [hbm] * 2,
        scratch_shapes=[
            pltpu.VMEM((own_rows, width), bf16), pltpu.VMEM(w_query.shape, bf16), pltpu.VMEM(w_key.shape, bf16),
            pltpu.VMEM(w_value.shape, bf16),
            pltpu.VMEM((bucket, 128), f32), pltpu.VMEM((bucket, width), bf16), pltpu.VMEM((own_rows, width), bf16), dma(7), dma(2, 3, 4), dma(2, 3, 4),
        ],
        compiler_params=pltpu.CompilerParams(
            collective_id=collective_id, has_side_effects=True, vmem_limit_bytes=48 << 20
        ),
        name="front",
    )(gain, length, tokens, cotangent, w_query, w_key, w_value)


def per_device(
    tokens,
    gain_attn,
    gain_mlp,
    w_query,
    w_key,
    w_value,
    w_out,
    w_gate,
    w_up,
    w_down,
    cotangent,
    lengths,
):
    groups = lax.axis_size("tensor")
    length = lax.dynamic_slice(lengths, (lax.axis_index("dp"),), (1,))[None]
    w_query_t, w_key_t, w_gate_t, w_up_t = w_query.T, w_key.T, w_gate.T, w_up.T
    query, key, value, attended, denom, den_row, normed_all, cot_all = front_call(
        tokens, cotangent, gain_attn[None], length, w_query_t, w_key_t, w_value, 1
    )
    small, output, _, _, down_total, gate_total, up_total, input_grad, out_total, value_total, qk_total = layer_call(
        attended, w_out, gain_mlp[None], gain_attn[None], length, denom, den_row, tokens, w_gate_t, w_up_t, w_down,
        cot_all, normed_all, query, key, value, w_query_t, w_key_t, w_value, 2,
    )
    quarter = w_query.shape[0] // 4
    gain_attn_total, gain_mlp_total = small[:4, :quarter].reshape(-1), small[4:, :quarter].reshape(-1)
    feat_width = w_query.shape[1]
    query_total, key_total = qk_total[:feat_width].T, qk_total[feat_width:].T
    gate_total, up_total = gate_total.T, up_total.T
    heads = feat_width // FEAT * groups
    den_mean = jnp.sum(small[0, quarter:]) / (heads * jnp.sum(lengths).astype(f32))
    return (
        output,
        input_grad,
        gain_attn_total,
        gain_mlp_total,
        query_total,
        key_total,
        value_total,
        out_total,
        gate_total,
        up_total,
        down_total,
        den_mean,
    )


def solution(mesh):
    return jax.shard_map(
        per_device,
        mesh=mesh,
        in_specs=(
            P(("dp", "tensor"), None),
            P(),
            P(),
            P(None, "tensor"),
            P(None, "tensor"),
            P(None, "tensor"),
            P("tensor", None),
            P(None, "tensor"),
            P(None, "tensor"),
            P("tensor", None),
            P(("dp", "tensor"), None),
            P(),
        ),
        out_specs=(
            P(("dp", "tensor"), None),
            P(("dp", "tensor"), None),
            P(),
            P(),
            P("dp", "tensor"),
            P("dp", "tensor"),
            P("dp", "tensor"),
            P("tensor", "dp"),
            P("dp", "tensor"),
            P("dp", "tensor"),
            P("tensor", "dp"),
            P(),
        ),
        check_vma=False,
    )
```
